32 devices in a mesh: batch: 4 (over y, x), seq: 8 (over z, core).
Axes of the slice: x: 2, y: 2, z: 4, core: 2. Of those that a mesh axis runs over, the one named last changes fastest.
Arguments:
- tokens: bfloat16 [8, 2048, 768], P('batch', 'seq'), may hold values from -6 to 6
- neighbours: bfloat16 [8, 32, 2, 128, 768], P('batch', 'seq'), may hold values from -6 to 6
- present: int32 [8, 32, 2], P('batch', 'seq'), may hold values 0 or 1
- qkv_weight: bfloat16 [768, 2304], replicated, may hold values from -0.21875 to 0.21875
- attn_weight: bfloat16 [768, 768], replicated, may hold values from -1.75 to 1.75
- query_weight: bfloat16 [768, 768], replicated, may hold values from -0.21875 to 0.21875
- memory_weight: bfloat16 [768, 1536], replicated, may hold values from -0.21875 to 0.21875
- cross_weight: bfloat16 [768, 768], replicated, may hold values from -1.75 to 1.75
- up_weight: bfloat16 [768, 3072], replicated, may hold values from -0.21875 to 0.21875
- down_weight: bfloat16 [3072, 768], replicated, may hold values from -0.109375 to 0.109375
- attn_gain: float32 [768], replicated, may hold values from 0.1 to 1.9
- attn_shift: float32 [768], replicated, may hold values from -1.2 to 1.2
- cross_gain: float32 [768], replicated, may hold values from 0.1 to 1.9
- cross_shift: float32 [768], replicated, may hold values from -1.2 to 1.2
- mlp_gain: float32 [768], replicated, may hold values from 0.1 to 1.9
- mlp_shift: float32 [768], replicated, may hold values from -1.2 to 1.2
- cotangent: bfloat16 [8, 2048, 768], P('batch', 'seq'), may hold values from -6 to 6
Outputs:
- output: bfloat16 [8, 2048, 768], P('batch', 'seq')
- grad_tokens: bfloat16 [8, 2048, 768], P('batch', 'seq')
- grad_neighbours: bfloat16 [8, 32, 2, 128, 768], P('batch', 'seq')
- grad_qkv: float32 [768, 2304], P('seq')
- grad_attn: float32 [768, 768], P('seq')
- grad_query: float32 [768, 768], P('seq')
- grad_memory: float32 [768, 1536], P('seq')
- grad_cross: float32 [768, 768], P('seq')
- grad_up: float32 [768, 3072], P('seq')
- grad_down: float32 [3072, 768], P('seq')
- grad_attn_gain: float32 [768], P('seq')
- grad_attn_shift: float32 [768], P('seq')
- grad_cross_gain: float32 [768], P('seq')
- grad_cross_shift: float32 [768], P('seq')
- grad_mlp_gain: float32 [768], P('seq')
- grad_mlp_shift: float32 [768], P('seq')
The draws below stay inside these ranges and needn't reach their ends.
Inputs may be any that keep to these rules, and one draw needn't show every extreme that they name: `present`: 1 marks a retrieved neighbour of the window, 0 one that is absent.
All inputs are finite; a program needn't handle non-finite values. No bound on the sum of `present` on one device may be relied on, other than what follows from the above.
Results may differ from the reference program's by a relative error of at most 0.028.
Values may be sent and summed in bfloat16 or wider, within the bound.
No kernel may reach another device: no remote copies, remote signals or barrier semaphores. Data moves between devices by JAX's collectives and lax.ppermute only.
A program may use at most 512 MiB of HBM per device.

```python
import math
import jax
import jax.numpy as jnp
from jax import lax

D = 768
HEADS = 12
HD = 64
FF = 3072
GROUP = 64
NEIGH = 2
RET = 128
SEQUENCES = 8
LEN = 2048
NCH = 32


def with_ends(array, rng, least, high):
    longest = array.shape.index(max(array.shape))
    spots = []
    for shift in (0, 1):
        where = [jax.random.randint(jax.random.fold_in(rng, axis), (), 0, length) for axis, length in enumerate(array.shape)]
        where[longest] = (where[longest] + shift) % array.shape[longest]
        spots.append(tuple(where))
    return array.at[spots[0]].set(least).at[spots[1]].set(high)


def level_of(stream_key, extent, pieces, smallest, top_value):
    loudness, own = 1.0, jax.random.fold_in(stream_key, 6)
    for axis_at, blocks in pieces:
        steps = jnp.exp(jax.random.uniform(jax.random.fold_in(own, axis_at), (blocks,), jnp.float32, smallest / len(pieces), top_value / len(pieces)))
        loudness = loudness * jnp.repeat(steps, extent[axis_at] // blocks).reshape([-1 if axis == axis_at else 1 for axis in range(len(extent))])
    return loudness


def noise(stream_key, shape, width, most, cuts=(), kind=jnp.bfloat16):
    factor_of = level_of(stream_key, shape, cuts, -0.22, 0.18) if cuts else 1.0
    drawn = jax.random.normal(stream_key, shape, jnp.float32) * width * factor_of
    return jnp.minimum(jnp.maximum(drawn, -most), most).astype(kind)


def setup_inputs(seed: int = 0) -> dict:
    arg_keys = jax.random.split(jax.random.key(seed), 18)
    tokens = noise(arg_keys[0], (SEQUENCES, LEN, D), 1.0, 6.0, ((0, 4), (1, 8)))
    neighbours = noise(arg_keys[1], (SEQUENCES, NCH, NEIGH, RET, D), 1.0, 6.0, ((0, 4), (1, 8)))
    present = with_ends((jax.random.randint(arg_keys[2], (SEQUENCES, NCH, NEIGH), 0, 10) < 7).astype(jnp.int32), jax.random.fold_in(arg_keys[2], 1), 0, 1)
    qkv_weight = noise(arg_keys[3], (D, 3 * D), D ** -0.5, 0.21875)
    attn_weight = noise(arg_keys[4], (D, D), (max(1, D // 64)) ** -0.5, 1.75)
    query_weight = noise(arg_keys[5], (D, D), D ** -0.5, 0.21875)
    memory_weight = noise(arg_keys[6], (D, 2 * D), D ** -0.5, 0.21875)
    cross_weight = noise(arg_keys[7], (D, D), (max(1, D // 64)) ** -0.5, 1.75)
    up_weight = noise(arg_keys[8], (D, FF), D ** -0.5, 0.21875)
    down_weight = noise(arg_keys[9], (FF, D), FF ** -0.5, 0.109375)
    attn_gain = jnp.clip(1.0 + 0.18 * jax.random.normal(arg_keys[10], (D,), jnp.float32), 0.1, 1.9)
    attn_shift = noise(arg_keys[11], (D,), 0.3, 1.2, (), jnp.float32)
    cross_gain = jnp.clip(1.0 + 0.18 * jax.random.normal(arg_keys[12], (D,), jnp.float32), 0.1, 1.9)
    cross_shift = noise(arg_keys[13], (D,), 0.3, 1.2, (), jnp.float32)
    mlp_gain = jnp.clip(1.0 + 0.18 * jax.random.normal(arg_keys[14], (D,), jnp.float32), 0.1, 1.9)
    mlp_shift = noise(arg_keys[15], (D,), 0.3, 1.2, (), jnp.float32)
    cotangent = noise(arg_keys[16], (SEQUENCES, LEN, D), 1.0, 6.0, ((0, 4), (1, 8)))
    return dict(tokens=tokens, neighbours=neighbours, present=present, qkv_weight=qkv_weight, attn_weight=attn_weight, query_weight=query_weight, memory_weight=memory_weight, cross_weight=cross_weight, up_weight=up_weight, down_weight=down_weight, attn_gain=attn_gain, attn_shift=attn_shift, cross_gain=cross_gain, cross_shift=cross_shift, mlp_gain=mlp_gain, mlp_shift=mlp_shift, cotangent=cotangent)


@jax.custom_vjp
def low(v):
    return lax.optimization_barrier(v.astype(jnp.bfloat16)).astype(jnp.float32)

@jax.custom_vjp
def low_back(v):
    return v

def low_keep(v):
    return (low(v), None)

def low_pass(kept, grad):
    return (grad,)

def back_keep(v):
    return (v, None)

def back_low(kept, grad):
    return (low(grad),)
low.defvjp(low_keep, low_pass)
low_back.defvjp(back_keep, back_low)
EPSILON = 1e-05
HIGHEST = lax.Precision.HIGHEST

def matmul_high(left, right):
    return jnp.dot(left, right, precision=HIGHEST, preferred_element_type=jnp.float32)

def norm_rows(values, gain_vec, shift_vec):
    row_mean = lax.optimization_barrier(jnp.mean(values, axis=-1, keepdims=True))
    centred = values - row_mean
    variance = lax.optimization_barrier(jnp.mean(centred * centred, axis=-1, keepdims=True))
    return centred * lax.rsqrt(variance + EPSILON) * gain_vec + shift_vec

def rotate(values, positions, direction):
    half_dim = HD // 2
    frequency = 10000.0 ** (-jnp.arange(half_dim, dtype=jnp.float32) * 2.0 / HD)
    angles = positions.astype(jnp.float32)[:, None] * frequency[None, :]
    cosine = jnp.cos(angles)[:, None, :]
    sine_part = direction * jnp.sin(angles)[:, None, :]
    first_half = values[..., :half_dim]
    second_half = values[..., half_dim:]
    return jnp.concatenate([first_half * cosine - second_half * sine_part, second_half * cosine + first_half * sine_part], axis=-1)

def self_attend(queries, keys_rot, values_own):
    length = queries.shape[0]
    block_len = math.gcd(length, 512)
    score_scale = 1.0 / math.sqrt(HD)
    key_positions = jnp.arange(length).astype(jnp.int32)

    def visit_block(block_item):
        query_block, block_start = block_item
        scores = low_back(jnp.einsum('qhd,khd->hqk', query_block, keys_rot, precision=HIGHEST) * score_scale)
        query_positions = block_start + jnp.arange(block_len).astype(jnp.int32)
        allowed = (key_positions[None, :] <= query_positions[:, None])[None, :, :]
        masked = jnp.where(allowed, scores, -1e+30)
        row_max = lax.optimization_barrier(jnp.max(masked, axis=-1, keepdims=True))
        weights_exp = jnp.where(allowed, jnp.exp(masked - row_max), 0.0)
        probability = weights_exp / lax.optimization_barrier(jnp.sum(weights_exp, axis=-1, keepdims=True))
        return jnp.einsum('hqk,khd->qhd', low(probability), values_own, precision=HIGHEST)
    blocks = queries.reshape(length // block_len, block_len, HEADS, HD)
    starts = (jnp.arange(length // block_len) * block_len).astype(jnp.int32)
    attended = lax.map(jax.checkpoint(visit_block), (blocks, starts))
    return attended.reshape(length, HEADS * HD)

def cross_attend(cross_query, cross_keys, cross_values, neigh_valid):
    score_scale = 1.0 / math.sqrt(HD)
    scores = low_back(jnp.einsum('cqhd,ckhd->chqk', cross_query, cross_keys, precision=HIGHEST) * score_scale)
    allowed = neigh_valid[:, None, None, :]
    masked = jnp.where(allowed, scores, -1e+30)
    row_max = lax.optimization_barrier(jnp.max(masked, axis=-1, keepdims=True))
    weights_exp = jnp.where(allowed, jnp.exp(masked - row_max), 0.0)
    row_total = lax.optimization_barrier(jnp.sum(weights_exp, axis=-1, keepdims=True))
    probability = weights_exp / jnp.where(row_total > 0.0, row_total, 1.0)
    return jnp.einsum('chqk,ckhd->cqhd', low(probability), cross_values, precision=HIGHEST)

def decoder_layer(params, seq_tokens, seq_neigh, neigh_valid):
    qkv_weight, attn_weight, query_weight, memory_weight, cross_weight, up_weight, down_weight, attn_gain, attn_shift, cross_gain, cross_shift, mlp_gain, mlp_shift = params
    length = seq_tokens.shape[0]
    positions = jnp.arange(length).astype(jnp.int32)
    normed_one = low(norm_rows(seq_tokens, attn_gain, attn_shift))
    projected = low_back(matmul_high(normed_one, qkv_weight)).reshape(length, 3, HEADS, HD)
    queries = low(rotate(projected[:, 0], positions, 1.0))
    keys_rot = low(rotate(projected[:, 1], positions, 1.0))
    values_own = low(projected[:, 2])
    attended = low_back(low(self_attend(queries, keys_rot, values_own)))
    after_attn = seq_tokens + low_back(matmul_high(attended, attn_weight))
    normed_two = low(norm_rows(after_attn, cross_gain, cross_shift))
    shifted = jnp.concatenate([jnp.zeros((1, D), jnp.float32), normed_two[:-1]], axis=0)
    cross_query = low(low_back(matmul_high(shifted, query_weight))).reshape(NCH, GROUP, HEADS, HD)
    memory = low(low_back(matmul_high(seq_neigh.reshape(NCH * NEIGH * RET, D), memory_weight)))
    memory = memory.reshape(NCH, NEIGH * RET, 2, HEADS, HD)
    windows = low_back(low(cross_attend(cross_query, memory[:, :, 0], memory[:, :, 1], neigh_valid).reshape(length, D)))
    cross_rows = jnp.concatenate([windows[1:], jnp.zeros((1, D), jnp.float32)], axis=0)
    after_cross = after_attn + low_back(matmul_high(cross_rows, cross_weight))
    normed_three = low(norm_rows(after_cross, mlp_gain, mlp_shift))
    up_value = low_back(matmul_high(normed_three, up_weight))
    activated = low(jax.nn.gelu(up_value, approximate=False))
    return after_cross + low_back(matmul_high(activated, down_weight))

def reference(tokens, neighbours, present, qkv_weight, attn_weight, query_weight, memory_weight, cross_weight, up_weight, down_weight, attn_gain, attn_shift, cross_gain, cross_shift, mlp_gain, mlp_shift, cotangent):
    params = tuple((initial.astype(jnp.float32) for initial in (qkv_weight, attn_weight, query_weight, memory_weight, cross_weight, up_weight, down_weight, attn_gain, attn_shift, cross_gain, cross_shift, mlp_gain, mlp_shift)))

    def per_sequence(totals, seq_item):
        seq_tokens, seq_neigh, seq_present, seq_cotangent = seq_item
        neigh_valid = jnp.repeat(seq_present > 0, RET, axis=1)

        def forward(weights, token_rows, neigh_rows):
            return decoder_layer(weights, token_rows, neigh_rows, neigh_valid)
        result, pullback = jax.vjp(forward, params, seq_tokens.astype(jnp.float32), seq_neigh.astype(jnp.float32))
        grad_params, grad_rows, grad_neigh = pullback(seq_cotangent.astype(jnp.float32))
        totals = jax.tree.map(lambda running, addend: running + addend, totals, grad_params)
        return (totals, (result.astype(jnp.bfloat16), grad_rows.astype(jnp.bfloat16), grad_neigh.astype(jnp.bfloat16)))
    start_totals = jax.tree.map(jnp.zeros_like, params)
    totals, stacked = lax.scan(per_sequence, start_totals, (tokens, neighbours, present, cotangent))
    return (stacked[0], stacked[1], stacked[2], totals[0], totals[1], totals[2], totals[3], totals[4], totals[5], totals[6], totals[7], totals[8], totals[9], totals[10], totals[11], totals[12])
```

```python
import math

import jax
import jax.numpy as jnp
import numpy as np
from jax import lax
from jax.experimental import pallas as pl
from jax.experimental.pallas import tpu as pltpu
from jax.sharding import Mesh
from jax.sharding import PartitionSpec as P

D = 768
HEADS = 12
HD = 64
FF = 3072
GROUP = 64
NEIGH = 2
RET = 128
PAIR = 128
BLK = 256
GROUPS = 4

EPSILON = 1e-05
NEGATIVE = -1e30
SCALE = 1.0 / math.sqrt(HD)
LOG2E = math.log2(math.e)
VMEM_LIMIT = 56 * 1024 * 1024

F32 = jnp.float32
BF16 = jnp.bfloat16


def params(limit=VMEM_LIMIT):
    return pltpu.CompilerParams(vmem_limit_bytes=limit)


def dot(left, right):
    return jnp.dot(left, right, preferred_element_type=F32)


def dot_nt(left, right):
    return lax.dot_general(left, right, (((1,), (1,)), ((), ())), preferred_element_type=F32)


def dot_tn(left, right):
    return lax.dot_general(left, right, (((0,), (0,)), ((), ())), preferred_element_type=F32)


def flip(value):
    return jnp.transpose(value.astype(F32))


def rope_tables(length):
    half = HD // 2
    frequency = np.float32(10000.0) ** (-np.arange(half, dtype=np.float32) * np.float32(2.0) / np.float32(HD))
    angles = np.arange(length, dtype=np.float32)[:, None] * frequency[None, :].astype(np.float32)
    cosine, sine = np.cos(angles).astype(np.float32), np.sin(angles).astype(np.float32)
    return (
        np.concatenate([cosine] * 4, axis=1),
        np.concatenate([-sine, sine] * 2, axis=1),
    )


def lanes(rows):
    return lax.broadcasted_iota(jnp.int32, (rows, PAIR), 1)


def turn(tile, cosine, sine):
    rows = tile.shape[0]
    first = (lanes(rows) % HD) < HD // 2
    swapped = jnp.where(first, pltpu.roll(tile, PAIR - HD // 2, 1), pltpu.roll(tile, HD // 2, 1))
    return tile * cosine + swapped * sine


def swap_heads(tile):
    return pltpu.roll(tile, HD, 1)


def norm_stats(values):
    mean = jnp.mean(values, axis=-1, keepdims=True)
    centred = values - mean
    inverse = lax.rsqrt(jnp.mean(centred * centred, axis=-1, keepdims=True) + EPSILON)
    return centred * inverse, inverse


def norm_back(normed, inverse, gain, grad):
    scaled = grad * gain
    return inverse * (
        scaled
        - jnp.mean(scaled, axis=-1, keepdims=True)
        - normed * jnp.mean(scaled * normed, axis=-1, keepdims=True)
    )


def const(shape):
    rank = len(shape)
    return pl.BlockSpec(shape, lambda *ids: (0,) * rank)


def qkv_body(place, tok, gain, shift, weight, cosine, sine, first, second):
    rows = tok.shape[1]
    half = rows // 2
    normed, _ = norm_stats(tok[0].astype(F32))
    row = (normed * gain[...] + shift[...]).astype(BF16)
    out = dot(row, weight[...])
    cos, sin = cosine[...], sine[...]
    low = lanes(rows) < HD
    queries = [turn(out[:, i * PAIR : (i + 1) * PAIR], cos, sin) for i in range(6)]
    keys = [turn(out[:, D + i * PAIR : D + (i + 1) * PAIR], cos, sin) for i in range(6)]
    values = [out[:, 2 * D + i * PAIR : 2 * D + (i + 1) * PAIR] for i in range(6)]
    for g in range(GROUPS):
        first[g, 0, 0:rows] = queries[g].astype(BF16)
        first[g, 0, rows : 2 * rows] = keys[g].astype(BF16)
        first[g, 0, 2 * rows : 3 * rows] = values[g].astype(BF16)
        tile = GROUPS + g // 2
        key, value, query = keys[tile], values[tile], queries[tile]
        if g % 2 == 0:
            both = jnp.where(low, key, swap_heads(value))
            packed = jnp.where(low[:half], query[:half], swap_heads(query[half:]))
        else:
            both = jnp.where(low, swap_heads(key), value)
            packed = jnp.where(low[:half], swap_heads(query[:half]), query[half:])
        second[g, 0, 0:rows] = both.astype(BF16)
        second[g, 0, rows : rows + half] = packed.astype(BF16)


def qkv_call(place, tokens, gain, shift, weight, cosine, sine):
    seqs, rows, _ = tokens.shape
    return pl.pallas_call(
        qkv_body,
        grid_spec=pltpu.PrefetchScalarGridSpec(
            num_scalar_prefetch=1,
            grid=(seqs,),
            in_specs=[
                pl.BlockSpec((1, rows, D), lambda s, place: (s, 0, 0)),
                const((1, D)),
                const((1, D)),
                const((D, 3 * D)),
                pl.BlockSpec((rows, PAIR), lambda s, place: (place[0], 0)),
                pl.BlockSpec((rows, PAIR), lambda s, place: (place[0], 0)),
            ],
            out_specs=[
                pl.BlockSpec((GROUPS, 1, 3 * rows, PAIR), lambda s, place: (0, s, 0, 0)),
                pl.BlockSpec((GROUPS, 1, 3 * rows // 2, PAIR), lambda s, place: (0, s, 0, 0)),
            ],
        ),
        out_shape=[
            jax.ShapeDtypeStruct((GROUPS, seqs, 3 * rows, PAIR), BF16),
            jax.ShapeDtypeStruct((GROUPS, seqs, 3 * rows // 2, PAIR), BF16),
        ],
        compiler_params=params(),
        name="qkv",
    )(place, tokens, gain, shift, weight, cosine, sine)


def unpack_half(packed, rows):
    peers = packed.shape[0]
    wide = packed.astype(F32).reshape(peers * rows // 2, PAIR)
    low = lanes(peers * rows // 2) < HD
    top = jnp.where(low, wide, 0.0).reshape(peers, rows // 2, PAIR)
    bottom = jnp.where(low, swap_heads(wide), 0.0).reshape(peers, rows // 2, PAIR)
    return jnp.concatenate([top, bottom], axis=1).reshape(peers * rows, PAIR).astype(BF16)


def pack_half(tile, rows):
    blocks = tile.shape[0] // rows
    cut = tile.reshape(blocks, rows, PAIR)
    top = cut[:, : rows // 2].reshape(blocks * rows // 2, PAIR)
    bottom = cut[:, rows // 2 :].reshape(blocks * rows // 2, PAIR)
    return (top + swap_heads(bottom)).reshape(blocks, rows // 2, PAIR)


def causal():
    key = lax.broadcasted_iota(jnp.int32, (BLK, BLK), 0)
    query = lax.broadcasted_iota(jnp.int32, (BLK, BLK), 1)
    return key <= query


def head_masks(tile_t):
    upper = lax.broadcasted_iota(jnp.int32, tile_t.shape, 0) < HD
    return jnp.where(upper, tile_t, 0.0).astype(BF16), jnp.where(upper, 0.0, tile_t).astype(BF16)


def softmax_sweep(i, heads, key_at, value_t_at):
    c = SCALE * LOG2E

    def visit(j, carry, masked):
        keys = key_at(j)
        values_t = value_t_at(j)
        out = []
        for (query_t, at), (top, total, acc) in zip(heads, carry):
            s = dot(keys, query_t) * c
            if masked:
                s = jnp.where(causal(), s, NEGATIVE)
            peak = jnp.maximum(top, jnp.max(s, axis=0, keepdims=True))
            p = jnp.exp2(s - peak)
            fade = jnp.exp2(top - peak)
            out.append(
                (
                    peak,
                    total * fade + jnp.sum(p, axis=0, keepdims=True),
                    acc * fade + dot(values_t[at : at + HD], p.astype(BF16)),
                )
            )
        return tuple(out)

    start = tuple(
        (
            jnp.full((1, BLK), NEGATIVE, F32),
            jnp.zeros((1, BLK), F32),
            jnp.zeros((HD, BLK), F32),
        )
        for _ in heads
    )
    carry = lax.fori_loop(0, i, lambda j, carry: visit(j, carry, False), start)
    carry = visit(i, carry, True)
    return [(acc / total, top + jnp.log2(total)) for top, total, acc in carry]


def pair_forward_body(rows, peers, recv, out, out_t, lse, keys, values_t):
    i = pl.program_id(0)
    blocks = peers * rows // BLK

    @pl.when(i == 0)
    def _():
        keys[...] = recv[:, rows : 2 * rows].reshape(blocks, BLK, PAIR)
        values = recv[:, 2 * rows : 3 * rows].reshape(blocks, BLK, PAIR)
        for b in range(blocks):
            values_t[b] = flip(values[b]).astype(BF16)

    if rows >= BLK:
        query = recv[i, 0:BLK]
    else:
        query = recv[pl.ds(i * (BLK // rows), BLK // rows), 0:rows].reshape(BLK, PAIR)
    low, high = head_masks(flip(query))
    heads = softmax_sweep(
        i, [(low, 0), (high, HD)], lambda j: keys[j], lambda j: values_t[j]
    )
    o_t = jnp.concatenate([heads[0][0], heads[1][0]], axis=0)
    out_t[...] = o_t
    lse[0, 0:1] = heads[0][1]
    lse[0, 1:2] = heads[1][1]
    out[...] = jnp.transpose(o_t).astype(BF16)


def pair_forward(recv):
    peers, rows = recv.shape[0], recv.shape[1] // 3
    length = peers * rows
    blocks = length // BLK
    return pl.pallas_call(
        lambda *refs: pair_forward_body(rows, peers, *refs),
        grid=(blocks,),
        in_specs=[const(recv.shape)],
        out_specs=[
            pl.BlockSpec((BLK, PAIR), lambda i: (i, 0)),
            pl.BlockSpec((PAIR, BLK), lambda i: (0, i)),
            pl.BlockSpec((1, 8, BLK), lambda i: (i, 0, 0)),
        ],
        out_shape=[
            jax.ShapeDtypeStruct((length, PAIR), BF16),
            jax.ShapeDtypeStruct((PAIR, length), F32),
            jax.ShapeDtypeStruct((blocks, 8, BLK), F32),
        ],
        scratch_shapes=[
            pltpu.VMEM((blocks, BLK, PAIR), BF16),
            pltpu.VMEM((blocks, PAIR, BLK), BF16),
        ],
        compiler_params=params(),
        name="attend_pair",
    )(recv)


def single_forward_body(rows, peers, recv, out, out_t, lse, keys, values_t, queries):
    i = pl.program_id(0)
    blocks = peers * rows // BLK

    @pl.when(i == 0)
    def _():
        both = recv[:, 0:rows].reshape(blocks, BLK, PAIR)
        keys[...] = both
        for b in range(blocks):
            values_t[b] = flip(both[b]).astype(BF16)
        queries[...] = unpack_half(recv[:, rows : rows + rows // 2], rows).reshape(blocks, BLK, PAIR)

    query_t = flip(queries[i]).astype(BF16)
    ((o_t, total),) = softmax_sweep(
        i, [(query_t, HD)], lambda j: keys[j], lambda j: values_t[j]
    )
    out_t[...] = o_t
    lse[0, 0:1] = total
    tile = jnp.transpose(jnp.concatenate([o_t, jnp.zeros_like(o_t)], axis=0))
    out[...] = pack_half(tile, rows).astype(BF16)


def single_forward(recv):
    peers, rows = recv.shape[0], recv.shape[1] * 2 // 3
    length = peers * rows
    blocks = length // BLK
    per = BLK // rows
    return pl.pallas_call(
        lambda *refs: single_forward_body(rows, peers, *refs),
        grid=(blocks,),
        in_specs=[const(recv.shape)],
        out_specs=[
            pl.BlockSpec((per, rows // 2, PAIR), lambda i: (i, 0, 0)),
            pl.BlockSpec((HD, BLK), lambda i: (0, i)),
            pl.BlockSpec((1, 8, BLK), lambda i: (i, 0, 0)),
        ],
        out_shape=[
            jax.ShapeDtypeStruct((peers, rows // 2, PAIR), BF16),
            jax.ShapeDtypeStruct((HD, length), F32),
            jax.ShapeDtypeStruct((blocks, 8, BLK), F32),
        ],
        scratch_shapes=[
            pltpu.VMEM((blocks, BLK, PAIR), BF16),
            pltpu.VMEM((blocks, PAIR, BLK), BF16),
            pltpu.VMEM((blocks, BLK, PAIR), BF16),
        ],
        compiler_params=params(),
        name="attend_single",
    )(recv)


def unturn_t(part_t, cosine_t, sine_t):
    first, second = part_t[: HD // 2], part_t[HD // 2 :]
    return jnp.concatenate(
        [first * cosine_t + second * sine_t, second * cosine_t - first * sine_t], axis=0
    )


def grads_sweep(i, heads, key_at, value_at, key_t_at, add):
    c = SCALE * LOG2E

    def visit(j, carry, masked):
        keys, values, keys_t = key_at(j), value_at(j), key_t_at(j)
        ps, dss, out = [], [], []
        for (query_t, grad_t, lse, delta, at), dq in zip(heads, carry):
            p = jnp.exp2(dot(keys, query_t) * c - lse)
            if masked:
                p = jnp.where(causal(), p, 0.0)
            ds = (p * (dot(values, grad_t) - delta)).astype(BF16)
            ps.append(p.astype(BF16))
            dss.append(ds)
            out.append(dq + dot(keys_t[at : at + HD], ds))
        add(j, ps, dss)
        return tuple(out)

    start = tuple(jnp.zeros((HD, BLK), F32) for _ in heads)
    carry = lax.fori_loop(0, i, lambda j, carry: visit(j, carry, False), start)
    return visit(i, carry, True)


def pair_backward_body(
    rows, peers, recv, grad, out_t, lse, cos_t, sin_t, cosine, sine, out, keys, values, keys_t, dk, dv
):
    i = pl.program_id(0)
    blocks = peers * rows // BLK
    per = BLK // rows

    @pl.when(i == 0)
    def _():
        keys[...] = recv[:, rows : 2 * rows].reshape(blocks, BLK, PAIR)
        values[...] = recv[:, 2 * rows : 3 * rows].reshape(blocks, BLK, PAIR)
        for b in range(blocks):
            keys_t[b] = flip(keys[b]).astype(BF16)
        dk[...] = jnp.zeros_like(dk)
        dv[...] = jnp.zeros_like(dv)

    query = recv[pl.ds(i * per, per), 0:rows].reshape(BLK, PAIR)
    do = grad[pl.ds(i * per, per), 0:rows].reshape(BLK, PAIR)
    q_low, q_high = head_masks(flip(query))
    do_t = flip(do)
    do_low, do_high = head_masks(do_t)
    product = do_t * out_t[...]
    low = lanes(BLK) < HD
    wide_q, wide_do = query.astype(F32), do.astype(F32)
    q_rows = jnp.concatenate(
        [jnp.where(low, wide_q, 0.0), jnp.where(low, 0.0, wide_q)], axis=0
    ).astype(BF16)
    do_rows = jnp.concatenate(
        [jnp.where(low, wide_do, 0.0), jnp.where(low, 0.0, wide_do)], axis=0
    ).astype(BF16)

    def add(j, ps, dss):
        dv[j] += dot(jnp.concatenate(ps, axis=1), do_rows)
        dk[j] += dot(jnp.concatenate(dss, axis=1), q_rows)

    heads = [
        (q_low, do_low, lse[0, 0:1], jnp.sum(product[:HD], axis=0, keepdims=True), 0),
        (q_high, do_high, lse[0, 1:2], jnp.sum(product[HD:], axis=0, keepdims=True), HD),
    ]
    dqs = grads_sweep(
        i, heads, lambda j: keys[j], lambda j: values[j], lambda j: keys_t[j], add
    )
    cos, sin = cos_t[...], sin_t[...]
    dq = jnp.concatenate([unturn_t(part * SCALE, cos, sin) for part in dqs], axis=0)
    out[pl.ds(i * per, per), 0:rows] = jnp.transpose(dq).reshape(per, rows, PAIR).astype(BF16)

    @pl.when(i == blocks - 1)
    def _():
        for b in range(blocks):
            at = pl.ds(b * BLK, BLK)
            back = turn(dk[b] * SCALE, cosine[at], -sine[at])
            out[b * per : (b + 1) * per, rows : 2 * rows] = back.reshape(per, rows, PAIR).astype(BF16)
            out[b * per : (b + 1) * per, 2 * rows : 3 * rows] = (
                dv[b].reshape(per, rows, PAIR).astype(BF16)
            )


def pair_backward(recv, grad, out_t, lse, cos_t, sin_t, cosine, sine):
    peers, rows = recv.shape[0], recv.shape[1] // 3
    length = peers * rows
    blocks = length // BLK
    return pl.pallas_call(
        lambda *refs: pair_backward_body(rows, peers, *refs),
        grid=(blocks,),
        in_specs=[
            const(recv.shape),
            const(grad.shape),
            pl.BlockSpec((PAIR, BLK), lambda i: (0, i)),
            pl.BlockSpec((1, 8, BLK), lambda i: (i, 0, 0)),
            pl.BlockSpec((HD // 2, BLK), lambda i: (0, i)),
            pl.BlockSpec((HD // 2, BLK), lambda i: (0, i)),
            const(cosine.shape),
            const(sine.shape),
        ],
        out_specs=const(recv.shape),
        out_shape=jax.ShapeDtypeStruct(recv.shape, BF16),
        scratch_shapes=[
            pltpu.VMEM((blocks, BLK, PAIR), BF16),
            pltpu.VMEM((blocks, BLK, PAIR), BF16),
            pltpu.VMEM((blocks, PAIR, BLK), BF16),
            pltpu.VMEM((blocks, BLK, PAIR), F32),
            pltpu.VMEM((blocks, BLK, PAIR), F32),
        ],
        compiler_params=params(),
        name="attend_pair_grads",
    )(recv, grad, out_t, lse, cos_t, sin_t, cosine, sine)


def single_backward_body(
    rows,
    peers,
    recv,
    grad,
    out_t,
    lse,
    cos_t,
    sin_t,
    cosine,
    sine,
    out,
    both,
    both_t,
    queries,
    grads,
    dboth,
):
    i = pl.program_id(0)
    blocks = peers * rows // BLK
    per = BLK // rows
    half = rows // 2

    @pl.when(i == 0)
    def _():
        both[...] = recv[:, 0:rows].reshape(blocks, BLK, PAIR)
        for b in range(blocks):
            both_t[b] = flip(both[b]).astype(BF16)
        queries[...] = unpack_half(recv[:, rows : rows + half], rows).reshape(blocks, BLK, PAIR)
        grads[...] = unpack_half(grad[...], rows).reshape(blocks, BLK, PAIR)
        dboth[...] = jnp.zeros_like(dboth)

    wide_q, wide_do = queries[i].astype(F32), grads[i].astype(F32)
    q_t = jnp.transpose(wide_q).astype(BF16)
    shifted = swap_heads(wide_do)
    do_t = jnp.transpose(shifted)
    delta = jnp.sum(do_t[HD:] * out_t[...], axis=0, keepdims=True)
    sides = jnp.concatenate([wide_q, shifted], axis=0).astype(BF16)

    def add(j, ps, dss):
        dboth[j] += dot(jnp.concatenate([dss[0], ps[0]], axis=1), sides)

    (dq,) = grads_sweep(
        i,
        [(q_t, do_t.astype(BF16), lse[0, 0:1], delta, 0)],
        lambda j: both[j],
        lambda j: both[j],
        lambda j: both_t[j],
        add,
    )
    dq = unturn_t(dq * SCALE, cos_t[...], sin_t[...])
    tile = jnp.transpose(jnp.concatenate([dq, jnp.zeros_like(dq)], axis=0))
    out[pl.ds(i * per, per), rows : rows + half] = pack_half(tile, rows).astype(BF16)

    @pl.when(i == blocks - 1)
    def _():
        low = lanes(BLK) < HD
        for b in range(blocks):
            at = pl.ds(b * BLK, BLK)
            part = dboth[b]
            back = turn(part * SCALE, cosine[at], -sine[at])
            out[b * per : (b + 1) * per, 0:rows] = (
                jnp.where(low, back, part).reshape(per, rows, PAIR).astype(BF16)
            )


def single_backward(recv, grad, out_t, lse, cos_t, sin_t, cosine, sine):
    peers, rows = recv.shape[0], recv.shape[1] * 2 // 3
    length = peers * rows
    blocks = length // BLK
    return pl.pallas_call(
        lambda *refs: single_backward_body(rows, peers, *refs),
        grid=(blocks,),
        in_specs=[
            const(recv.shape),
            const(grad.shape),
            pl.BlockSpec((HD, BLK), lambda i: (0, i)),
            pl.BlockSpec((1, 8, BLK), lambda i: (i, 0, 0)),
            pl.BlockSpec((HD // 2, BLK), lambda i: (0, i)),
            pl.BlockSpec((HD // 2, BLK), lambda i: (0, i)),
            const(cosine.shape),
            const(sine.shape),
        ],
        out_specs=const(recv.shape),
        out_shape=jax.ShapeDtypeStruct(recv.shape, BF16),
        scratch_shapes=[
            pltpu.VMEM((blocks, BLK, PAIR), BF16),
            pltpu.VMEM((blocks, PAIR, BLK), BF16),
            pltpu.VMEM((blocks, BLK, PAIR), BF16),
            pltpu.VMEM((blocks, BLK, PAIR), BF16),
            pltpu.VMEM((blocks, BLK, PAIR), F32),
        ],
        compiler_params=params(),
        name="attend_single_grads",
    )(recv, grad, out_t, lse, cos_t, sin_t, cosine, sine)


def from_behind(value, axis, by):
    peers = lax.axis_size(axis)
    pairs = [(i, i + by) for i in range(peers) if 0 <= i + by < peers]
    return lax.ppermute(value, axis, pairs)


def norm_rows(values, gain_vec, shift_vec):
    row_mean = jnp.mean(values, axis=-1, keepdims=True)
    centred = values - row_mean
    variance = jnp.mean(centred * centred, axis=-1, keepdims=True)
    return centred * lax.rsqrt(variance + EPSILON) * gain_vec + shift_vec


def gelu_exact(values):
    return jax.nn.gelu(values, approximate=False)


SEQ = ("hg", "sq")
BATCH = ("by", "bx")


def swap_all(value):
    return lax.all_to_all(value, SEQ, 0, 0, tiled=True)


def heads_in(pair, single, seqs, rows):
    first = pair.reshape(GROUPS, seqs, rows, PAIR).transpose(1, 2, 0, 3).reshape(seqs, rows, GROUPS * PAIR)
    second = (
        single.reshape(GROUPS, seqs, rows // 2, 2, HD)
        .transpose(1, 3, 2, 0, 4)
        .reshape(seqs, rows, GROUPS * HD)
    )
    return jnp.concatenate([first, second], axis=-1)


def heads_out(value, seqs, rows):
    first = value[..., : GROUPS * PAIR].reshape(seqs, rows, GROUPS, PAIR).transpose(2, 0, 1, 3)
    second = (
        value[..., GROUPS * PAIR :]
        .reshape(seqs, 2, rows // 2, GROUPS, HD)
        .transpose(3, 0, 2, 1, 4)
        .reshape(GROUPS, seqs, rows // 2, PAIR)
    )
    return (
        first.reshape(GROUPS * seqs, rows, PAIR),
        second.reshape(GROUPS * seqs, rows // 2, PAIR),
    )


def add_up(value):
    kept = value.shape[3:]
    flat = value.reshape((value.shape[0] * value.shape[1],) + value.shape[2:])
    own = lax.psum_scatter(flat, BATCH + ("sq",), scatter_dimension=0, tiled=True)
    own = own.reshape((value.shape[2],) + kept)
    parts = lax.all_to_all(own, "hg", 0, 0, tiled=True)
    total = jnp.sum(parts.astype(F32), axis=0).astype(BF16)
    return lax.all_gather(total, BATCH, axis=0)


def by_columns(value, batch, sq):
    rows, cols = value.shape
    cut = value.astype(BF16).reshape(GROUPS, sq, rows // GROUPS // sq, batch, cols // batch)
    return cut.transpose(3, 1, 0, 2, 4)


def shards(
    tokens,
    neighbours,
    present,
    qkv_weight,
    attn_weight,
    query_weight,
    memory_weight,
    cross_weight,
    up_weight,
    down_weight,
    attn_gain,
    attn_shift,
    cross_gain,
    cross_shift,
    mlp_gain,
    mlp_shift,
    cotangent,
):
    seq_count, tok_rows = tokens.shape[:2]
    all_rows = seq_count * tok_rows
    group_count = neighbours.shape[1]
    peers = lax.axis_size(SEQ)
    batch = lax.axis_size(BATCH)
    length = peers * tok_rows
    here = lax.axis_index(SEQ)
    place = here.astype(jnp.int32).reshape(1)
    cos_np, sin_np = rope_tables(length)
    cosine, sine = jnp.asarray(cos_np), jnp.asarray(sin_np)
    cos_t = jnp.asarray(np.ascontiguousarray(cos_np[:, : HD // 2].T))
    sin_t = jnp.asarray(np.ascontiguousarray(sin_np[:, HD // 2 : HD].T))
    token_vals = tokens.astype(F32).reshape(all_rows, D)
    normed_one = norm_rows(token_vals, attn_gain, attn_shift).astype(BF16)
    first, second = qkv_call(
        place, tokens, attn_gain.reshape(1, D), attn_shift.reshape(1, D), qkv_weight, cosine, sine
    )
    first = swap_all(first.reshape(peers, 3 * tok_rows, PAIR))
    second = swap_all(second.reshape(peers, 3 * tok_rows // 2, PAIR))
    o_pair, o_pair_t, lse_pair = pair_forward(first)
    o_pair = swap_all(o_pair.reshape(peers, tok_rows, PAIR))
    o_single, o_single_t, lse_single = single_forward(second)
    o_single = swap_all(o_single)
    attn_low = heads_in(o_pair, o_single, seq_count, tok_rows).reshape(all_rows, D)
    score_scale = SCALE
    after_attn = token_vals + dot(attn_low, attn_weight)
    normed_two = (
        norm_rows(after_attn, cross_gain, cross_shift).astype(BF16).reshape(seq_count, tok_rows, D)
    )
    before_rows = from_behind(normed_two[:, -1:, :], SEQ, 1)
    shifted = jnp.concatenate([before_rows, normed_two[:, :-1, :]], axis=1).reshape(all_rows, D)
    cross_query = (
        dot(shifted, query_weight).astype(BF16).reshape(seq_count, group_count, GROUP, HEADS, HD)
    )
    neigh_rows = neighbours.reshape(seq_count * group_count * NEIGH * RET, D)
    memory = (
        dot(neigh_rows, memory_weight)
        .astype(BF16)
        .reshape(seq_count, group_count, NEIGH * RET, 2, HEADS, HD)
    )
    cross_keys = memory[:, :, :, 0]
    cross_values = memory[:, :, :, 1]
    allowed = jnp.repeat(present > 0, RET, axis=2)[:, :, None, None, :]
    scores = (
        jnp.einsum("scqhd,sckhd->scqhk", cross_query, cross_keys, preferred_element_type=F32)
        * score_scale
    )
    masked = jnp.where(allowed, scores, NEGATIVE)
    row_peak = jnp.max(masked, axis=-1, keepdims=True)
    weights_exp = jnp.where(allowed, jnp.exp(masked - row_peak), 0.0)
    cross_total = jnp.sum(weights_exp, axis=-1, keepdims=True)
    cross_prob = weights_exp / jnp.where(cross_total > 0.0, cross_total, 1.0)
    cross_low = cross_prob.astype(BF16)
    windows = (
        jnp.einsum("scqhk,sckhd->scqhd", cross_low, cross_values, preferred_element_type=F32)
        .astype(BF16)
        .reshape(seq_count, tok_rows, D)
    )
    after_rows = from_behind(windows[:, :1, :], SEQ, -1)
    cross_rows = jnp.concatenate([windows[:, 1:, :], after_rows], axis=1).reshape(all_rows, D)
    after_cross = after_attn + dot(cross_rows, cross_weight)
    normed_three = norm_rows(after_cross, mlp_gain, mlp_shift).astype(BF16)
    up_value = dot(normed_three, up_weight)
    activated_full, gelu_pull = jax.vjp(gelu_exact, up_value)
    activated = activated_full.astype(BF16)
    output = (after_cross + dot(activated, down_weight)).astype(BF16).reshape(seq_count, tok_rows, D)
    grad_rows = cotangent.reshape(all_rows, D)
    grad_down = dot_tn(activated, grad_rows)
    grad_up_in = gelu_pull(dot_nt(grad_rows, down_weight))[0].astype(BF16)
    grad_up = dot_tn(normed_three, grad_up_in)
    up_part = by_columns(grad_up, batch, seq_count)
    down_part = (
        grad_down.astype(BF16)
        .reshape(GROUPS, seq_count, batch, FF // peers // batch, D)
        .transpose(2, 1, 0, 3, 4)
    )
    feed = add_up(jnp.concatenate([up_part.reshape(down_part.shape), down_part], axis=3))
    mlp_norm_pull = jax.vjp(norm_rows, after_cross, mlp_gain, mlp_shift)[1]
    grad_into_three, grad_mlp_gain, grad_mlp_shift = mlp_norm_pull(dot_nt(grad_up_in, up_weight))
    grad_cross_res = grad_rows.astype(F32) + grad_into_three
    grad_cross_low = grad_cross_res.astype(BF16)
    grad_cross = dot_tn(cross_rows, grad_cross_low)
    grad_cross_rows = (
        dot_nt(grad_cross_low, cross_weight).astype(BF16).reshape(seq_count, tok_rows, D)
    )
    from_before = from_behind(grad_cross_rows[:, -1:, :], SEQ, 1)
    grad_windows = jnp.concatenate([from_before, grad_cross_rows[:, :-1, :]], axis=1).reshape(
        seq_count, group_count, GROUP, HEADS, HD
    )
    grad_prob = jnp.einsum(
        "scqhd,sckhd->scqhk", grad_windows, cross_values, preferred_element_type=F32
    )
    grad_scores = (
        cross_prob * (grad_prob - jnp.sum(cross_prob * grad_prob, axis=-1, keepdims=True))
    ).astype(BF16)
    query_grad_low = (
        (
            jnp.einsum("scqhk,sckhd->scqhd", grad_scores, cross_keys, preferred_element_type=F32)
            * score_scale
        )
        .astype(BF16)
        .reshape(all_rows, D)
    )
    key_grad = (
        jnp.einsum("scqhk,scqhd->sckhd", grad_scores, cross_query, preferred_element_type=F32)
        * score_scale
    )
    value_grad = jnp.einsum(
        "scqhk,scqhd->sckhd", cross_low, grad_windows, preferred_element_type=F32
    )
    memory_grad_low = (
        jnp.stack([key_grad, value_grad], axis=3)
        .astype(BF16)
        .reshape(seq_count * group_count * NEIGH * RET, 2 * D)
    )
    grad_memory = dot_tn(neigh_rows, memory_grad_low)
    grad_neighbours = dot_nt(memory_grad_low, memory_weight).astype(BF16).reshape(neighbours.shape)
    grad_query = dot_tn(shifted, query_grad_low)
    grad_shifted = dot_nt(query_grad_low, query_weight).reshape(seq_count, tok_rows, D)
    after_grads = from_behind(grad_shifted[:, :1, :], SEQ, -1)
    grad_normed_two = jnp.concatenate([grad_shifted[:, 1:, :], after_grads], axis=1).reshape(
        all_rows, D
    )
    cross_norm_pull = jax.vjp(norm_rows, after_attn, cross_gain, cross_shift)[1]
    grad_into_two, grad_cross_gain, grad_cross_shift = cross_norm_pull(grad_normed_two)
    grad_attn_res = grad_cross_res + grad_into_two
    grad_attn_low = grad_attn_res.astype(BF16)
    grad_heads = dot_nt(grad_attn_low, attn_weight).astype(BF16).reshape(seq_count, tok_rows, D)
    do_pair, do_single = heads_out(grad_heads, seq_count, tok_rows)
    do_pair, do_single = swap_all(do_pair), swap_all(do_single)
    grad_attn = dot_tn(attn_low, grad_attn_low)
    others = add_up(
        by_columns(
            jnp.concatenate(
                [grad_attn, grad_query, grad_cross, grad_memory, jnp.zeros((D, PAIR * 2), F32)], axis=1
            ),
            batch,
            seq_count,
        )
    )
    d_pair = pair_backward(first, do_pair, o_pair_t, lse_pair, cos_t, sin_t, cosine, sine)
    d_pair = swap_all(d_pair)
    d_single = single_backward(second, do_single, o_single_t, lse_single, cos_t, sin_t, cosine, sine)
    d_single = swap_all(d_single)
    pair_parts = d_pair.reshape(peers, 3, tok_rows, PAIR)
    both = d_single[:, :tok_rows].reshape(GROUPS, seq_count, tok_rows, 2, HD)
    both = both.transpose(3, 1, 2, 0, 4).reshape(2, seq_count, tok_rows, GROUPS * HD)

    def pair_rows(k):
        return (
            pair_parts[:, k]
            .reshape(GROUPS, seq_count, tok_rows, PAIR)
            .transpose(1, 2, 0, 3)
            .reshape(seq_count, tok_rows, GROUPS * PAIR)
        )

    grad_proj = jnp.concatenate(
        [
            heads_in(pair_parts[:, 0], d_single[:, tok_rows:], seq_count, tok_rows),
            pair_rows(1),
            both[0],
            pair_rows(2),
            both[1],
        ],
        axis=-1,
    ).reshape(all_rows, 3 * D)
    grad_qkv = dot_tn(normed_one, grad_proj)
    attn_norm_pull = jax.vjp(norm_rows, token_vals, attn_gain, attn_shift)[1]
    grad_into_one, grad_attn_gain, grad_attn_shift = attn_norm_pull(dot_nt(grad_proj, qkv_weight))
    grad_tokens = (grad_attn_res + grad_into_one).astype(BF16).reshape(seq_count, tok_rows, D)
    vectors = jnp.stack(
        [
            grad_attn_gain,
            grad_attn_shift,
            grad_cross_gain,
            grad_cross_shift,
            grad_mlp_gain,
            grad_mlp_shift,
        ],
        axis=1,
    )
    last = add_up(
        by_columns(
            jnp.concatenate(
                [grad_qkv, jnp.pad(vectors, ((0, 0), (0, 2 * PAIR - vectors.shape[1])))], axis=1
            ),
            batch,
            seq_count,
        )
    )
    own = D // peers

    def columns(value):
        return value.transpose(1, 0, 2).reshape(own, -1).astype(F32)

    deep = FF // peers // batch
    feed = feed.reshape(batch, 2, deep * D)
    grad_up = columns(feed[:, 0].reshape(batch, own, FF // batch))
    grad_down = feed[:, 1].reshape(batch * deep, D).astype(F32)
    others = columns(others)
    last = columns(last)
    return (
        output,
        grad_tokens,
        grad_neighbours,
        last[:, : 3 * D],
        others[:, :D],
        others[:, D : 2 * D],
        others[:, 3 * D : 5 * D],
        others[:, 2 * D : 3 * D],
        grad_up,
        grad_down,
    ) + tuple(last[:, 3 * D + k] for k in range(6))


def solution(mesh):
    batch, seq = mesh.shape["batch"], mesh.shape["seq"]
    fine = Mesh(
        mesh.devices.reshape(batch // 2, 2, GROUPS, seq // GROUPS), ("by", "bx", "hg", "sq")
    )
    rows = P(BATCH, SEQ, None)
    windows = P(BATCH, SEQ, None, None, None)
    return jax.shard_map(
        shards,
        mesh=fine,
        in_specs=(rows, windows, rows) + (P(),) * 13 + (rows,),
        out_specs=(rows, rows, windows) + (P(SEQ, None),) * 7 + (P(SEQ),) * 6,
        check_vma=False,
    )
```

```python
import math

import jax
import jax.numpy as jnp
import numpy as np
from jax import lax
from jax.experimental import pallas as pl
from jax.experimental.pallas import tpu as pltpu
from jax.sharding import Mesh
from jax.sharding import PartitionSpec as P

D = 768
HEADS = 12
HD = 64
FF = 3072
GROUP = 64
NEIGH = 2
RET = 128
PAIR = 128
BLK = 512
GROUPS = 4

EPSILON = 1e-05
NEGATIVE = -1e30
SCALE = 1.0 / math.sqrt(HD)
LOG2E = math.log2(math.e)
VMEM_LIMIT = 56 * 1024 * 1024

F32 = jnp.float32
BF16 = jnp.bfloat16


def params(limit=VMEM_LIMIT):
    return pltpu.CompilerParams(vmem_limit_bytes=limit)


def dot(left, right):
    return jnp.dot(left, right, preferred_element_type=F32)


def dot_nt(left, right):
    return lax.dot_general(left, right, (((1,), (1,)), ((), ())), preferred_element_type=F32)


def dot_tn(left, right):
    return lax.dot_general(left, right, (((0,), (0,)), ((), ())), preferred_element_type=F32)


def flip(value):
    return jnp.transpose(value.astype(F32))


def rope_tables(length):
    half = HD // 2
    frequency = np.float32(10000.0) ** (-np.arange(half, dtype=np.float32) * np.float32(2.0) / np.float32(HD))
    angles = np.arange(length, dtype=np.float32)[:, None] * frequency[None, :].astype(np.float32)
    cosine, sine = np.cos(angles).astype(np.float32), np.sin(angles).astype(np.float32)
    return (
        np.concatenate([cosine] * 4, axis=1),
        np.concatenate([-sine, sine] * 2, axis=1),
    )


def lanes(rows):
    return lax.broadcasted_iota(jnp.int32, (rows, PAIR), 1)


def turn(tile, cosine, sine):
    rows = tile.shape[0]
    first = (lanes(rows) % HD) < HD // 2
    swapped = jnp.where(first, pltpu.roll(tile, PAIR - HD // 2, 1), pltpu.roll(tile, HD // 2, 1))
    return tile * cosine + swapped * sine


def swap_heads(tile):
    return pltpu.roll(tile, HD, 1)


def norm_stats(values):
    mean = jnp.mean(values, axis=-1, keepdims=True)
    centred = values - mean
    inverse = lax.rsqrt(jnp.mean(centred * centred, axis=-1, keepdims=True) + EPSILON)
    return centred * inverse, inverse


def norm_back(normed, inverse, gain, grad):
    scaled = grad * gain
    return inverse * (
        scaled
        - jnp.mean(scaled, axis=-1, keepdims=True)
        - normed * jnp.mean(scaled * normed, axis=-1, keepdims=True)
    )


VECTOR = pl.BlockSpec((D,), lambda *ids: (0,))


def const(shape):
    rank = len(shape)
    return pl.BlockSpec(shape, lambda *ids: (0,) * rank)


def chunk_body(which, place, *refs):
    halves = (len(refs) - 15) // 2
    near, far, refs = refs[:halves], refs[halves : 2 * halves], refs[2 * halves :]
    gain, shift = refs[:2]
    weights, (cosine, sine, normed, pair, single, tokens, columns) = refs[2:8], refs[8:]
    rows = tokens.shape[0] // halves
    first = use_first(which, place[0])
    for parts, wanted in ((near, first), (far, jnp.logical_not(first))):

        @pl.when(wanted)
        def _(parts=parts):
            for k, part in enumerate(parts):
                at = place[1] * (1 - 2 * k) + k if halves > 1 else 0
                tokens[pl.ds(at * rows, rows)] = part[...].reshape(rows, D)

    odd = lax.rem(place[0], 2) == 1
    for k, weight in enumerate(weights):
        columns[:, k * PAIR : (k + 1) * PAIR] = weight[...]
    n, _ = norm_stats(tokens[...].astype(F32))
    normed[...] = n.astype(BF16)
    out = dot((n * gain[...][None] + shift[...][None]).astype(BF16), columns[...])
    cos, sin = cosine[...], sine[...]
    q01, k01, v01, q2, k2, v2 = [out[:, k * PAIR : (k + 1) * PAIR] for k in range(6)]
    low = lanes(tokens.shape[0]) < HD
    q2, k2, v2 = [jnp.where(odd, swap_heads(t), t) for t in (q2, k2, v2)]
    pair[:, :PAIR] = (turn(q01, cos, sin) * (SCALE * LOG2E)).astype(BF16)
    pair[:, PAIR : 2 * PAIR] = turn(k01, cos, sin).astype(BF16)
    pair[:, 2 * PAIR :] = v01.astype(BF16)
    single[:, :PAIR] = jnp.where(low, turn(k2, cos, sin), swap_heads(v2)).astype(BF16)
    single[:, PAIR:] = jnp.where(low, turn(q2, cos, sin) * (SCALE * LOG2E), 0.0).astype(BF16)


def use_first(which, group):
    if which == 0:
        return group >= 0
    if which == 1:
        return group < GROUPS - 1
    if which == 2:
        return group < 2
    return group == 0


def chunk_of(which, group):
    if which == 0:
        return group
    if which == 1:
        return jnp.where(group < GROUPS - 1, group + 1, group - 1)
    if which == 2:
        return lax.rem(group + 2, GROUPS)
    return jnp.where(group == 0, GROUPS - 1, jnp.where(group == GROUPS - 1, 0, group - 1))


def head_columns(index):
    def column(first, shared):
        def at(i, place):
            return (0, first + (place[0] // 2 if shared else place[0]))

        return pl.BlockSpec((D, PAIR), at)

    return [column(6 * k, False) for k in range(3)] + [column(6 * k + 4, True) for k in range(3)]


def chunk_call(which, place, near, far, gain, shift, weight, cosine, sine):
    count = sum(part.size for part in near) // D
    whole = lambda part: pl.BlockSpec(part.shape, lambda i, place: (0,) * part.ndim)
    table = pl.BlockSpec((count, PAIR), lambda i, place: (place[2 + which], 0))
    return pl.pallas_call(
        lambda *refs: chunk_body(which, *refs),
        grid_spec=pltpu.PrefetchScalarGridSpec(
            num_scalar_prefetch=1,
            grid=(1,),
            in_specs=[whole(part) for part in (*near, *far)]
            + [VECTOR, VECTOR]
            + head_columns(0)
            + [table, table],
            out_specs=[const((count, D)), const((count, 3 * PAIR)), const((count, 2 * PAIR))],
            scratch_shapes=[pltpu.VMEM((count, D), BF16), pltpu.VMEM((D, 6 * PAIR), BF16)],
        ),
        out_shape=[
            jax.ShapeDtypeStruct((count, D), BF16),
            jax.ShapeDtypeStruct((count, 3 * PAIR), BF16),
            jax.ShapeDtypeStruct((count, 2 * PAIR), BF16),
        ],
        compiler_params=params(),
        name="qkv_chunk",
    )(place, *near, *far, gain, shift, *[weight] * 6, cosine, sine)


def unpack_half(packed, rows):
    peers = packed.shape[0]
    wide = packed.astype(F32).reshape(peers * rows // 2, PAIR)
    low = lanes(peers * rows // 2) < HD
    top = jnp.where(low, wide, 0.0).reshape(peers, rows // 2, PAIR)
    bottom = jnp.where(low, swap_heads(wide), 0.0).reshape(peers, rows // 2, PAIR)
    return jnp.concatenate([top, bottom], axis=1).reshape(peers * rows, PAIR).astype(BF16)


def pack_half(tile, rows):
    blocks = tile.shape[0] // rows
    cut = tile.reshape(blocks, rows, PAIR)
    top = cut[:, : rows // 2].reshape(blocks * rows // 2, PAIR)
    bottom = cut[:, rows // 2 :].reshape(blocks * rows // 2, PAIR)
    return (top + swap_heads(bottom)).reshape(blocks, rows // 2, PAIR)


def causal():
    key = lax.broadcasted_iota(jnp.int32, (BLK, BLK), 0)
    query = lax.broadcasted_iota(jnp.int32, (BLK, BLK), 1)
    return key <= query


def head_masks(tile_t):
    upper = lax.broadcasted_iota(jnp.int32, tile_t.shape, 0) < HD
    return jnp.where(upper, tile_t, 0.0).astype(BF16), jnp.where(upper, 0.0, tile_t).astype(BF16)


def softmax_sweep(i, heads, key_at, value_t_at):
    def visit(j, carry, masked):
        keys = key_at(j)
        values_t = value_t_at(j)
        out = []
        for (query_t, at), (top, total, acc) in zip(heads, carry):
            s = dot(keys, query_t)
            if masked:
                s = jnp.where(causal(), s, NEGATIVE)
            peak = jnp.maximum(top, jnp.max(s, axis=0, keepdims=True))
            p = jnp.exp2(s - peak)
            fade = jnp.exp2(top - peak)
            out.append(
                (
                    peak,
                    total * fade + jnp.sum(p, axis=0, keepdims=True),
                    acc * fade + dot(values_t[at : at + HD], p.astype(BF16)),
                )
            )
        return tuple(out)

    start = tuple(
        (
            jnp.full((1, BLK), NEGATIVE, F32),
            jnp.zeros((1, BLK), F32),
            jnp.zeros((HD, BLK), F32),
        )
        for _ in heads
    )
    carry = lax.fori_loop(0, i, lambda j, carry: visit(j, carry, False), start)
    carry = visit(i, carry, True)
    return [(acc / total, top + jnp.log2(total)) for top, total, acc in carry]


def pair_forward_body(place, *refs):
    chunks, (out, out_t, lse, whole, values_t) = refs[:GROUPS], refs[GROUPS:]
    i = pl.program_id(0)

    @pl.when(i == 0)
    def _():
        for which, chunk in enumerate(chunks):
            at = place[2 + which]
            whole[at] = chunk[...]
            values_t[at] = flip(chunk[:, 2 * PAIR :]).astype(BF16)

    low, high = head_masks(flip(whole[i, :, :PAIR]))
    heads = softmax_sweep(
        i,
        [(low, 0), (high, HD)],
        lambda j: whole[j, :, PAIR : 2 * PAIR],
        lambda j: values_t[j],
    )
    o_t = jnp.concatenate([heads[0][0], heads[1][0]], axis=0)
    out_t[...] = o_t
    lse[0, 0:1] = heads[0][1]
    lse[0, 1:2] = heads[1][1]
    out[...] = jnp.transpose(o_t).astype(BF16)


def pair_forward(place, chunks):
    return pl.pallas_call(
        pair_forward_body,
        grid_spec=pltpu.PrefetchScalarGridSpec(
            num_scalar_prefetch=1,
            grid=(GROUPS,),
            in_specs=[const((BLK, 3 * PAIR))] * GROUPS,
            out_specs=[
                pl.BlockSpec((BLK, PAIR), lambda i, place: (i, 0)),
                pl.BlockSpec((PAIR, BLK), lambda i, place: (0, i)),
                pl.BlockSpec((1, 8, BLK), lambda i, place: (i, 0, 0)),
                const((GROUPS, BLK, 3 * PAIR)),
            ],
            scratch_shapes=[pltpu.VMEM((GROUPS, PAIR, BLK), BF16)],
        ),
        out_shape=[
            jax.ShapeDtypeStruct((GROUPS * BLK, PAIR), BF16),
            jax.ShapeDtypeStruct((PAIR, GROUPS * BLK), F32),
            jax.ShapeDtypeStruct((GROUPS, 8, BLK), F32),
            jax.ShapeDtypeStruct((GROUPS, BLK, 3 * PAIR), BF16),
        ],
        compiler_params=params(),
        name="attend_pair",
    )(place, *chunks)


def single_forward_body(rows, place, *refs):
    chunks, (out, out_t, lse, whole, values_t) = refs[:GROUPS], refs[GROUPS:]
    i = pl.program_id(0)

    @pl.when(i == 0)
    def _():
        for which, chunk in enumerate(chunks):
            at = place[2 + which]
            whole[at] = chunk[...]
            values_t[at] = flip(chunk[:, :PAIR]).astype(BF16)

    query_t = flip(whole[i, :, PAIR:]).astype(BF16)
    ((o_t, total),) = softmax_sweep(
        i, [(query_t, HD)], lambda j: whole[j, :, :PAIR], lambda j: values_t[j]
    )
    out_t[...] = o_t
    lse[0, 0:1] = total
    tile = jnp.transpose(jnp.concatenate([o_t, jnp.zeros_like(o_t)], axis=0))
    out[...] = pack_half(tile, rows).astype(BF16)


def single_forward(place, chunks, rows):
    per = BLK // rows
    return pl.pallas_call(
        lambda *refs: single_forward_body(rows, *refs),
        grid_spec=pltpu.PrefetchScalarGridSpec(
            num_scalar_prefetch=1,
            grid=(GROUPS,),
            in_specs=[const((BLK, 2 * PAIR))] * GROUPS,
            out_specs=[
                pl.BlockSpec((per, rows // 2, PAIR), lambda i, place: (i, 0, 0)),
                pl.BlockSpec((HD, BLK), lambda i, place: (0, i)),
                pl.BlockSpec((1, 8, BLK), lambda i, place: (i, 0, 0)),
                const((GROUPS, BLK, 2 * PAIR)),
            ],
            scratch_shapes=[pltpu.VMEM((GROUPS, PAIR, BLK), BF16)],
        ),
        out_shape=[
            jax.ShapeDtypeStruct((GROUPS * per, rows // 2, PAIR), BF16),
            jax.ShapeDtypeStruct((HD, GROUPS * BLK), F32),
            jax.ShapeDtypeStruct((GROUPS, 8, BLK), F32),
            jax.ShapeDtypeStruct((GROUPS, BLK, 2 * PAIR), BF16),
        ],
        compiler_params=params(),
        name="attend_single",
    )(place, *chunks)


def unturn_t(part_t, cosine_t, sine_t):
    first, second = part_t[: HD // 2], part_t[HD // 2 :]
    return jnp.concatenate(
        [first * cosine_t + second * sine_t, second * cosine_t - first * sine_t], axis=0
    )


def grads_sweep(i, heads, key_at, value_at, key_t_at, add):
    def visit(j, carry, masked):
        keys, values, keys_t = key_at(j), value_at(j), key_t_at(j)
        ps, dss, out = [], [], []
        for (query_t, grad_t, lse, delta, at), dq in zip(heads, carry):
            p = jnp.exp2(dot(keys, query_t) - lse)
            if masked:
                p = jnp.where(causal(), p, 0.0)
            ds = (p * (dot(values, grad_t) - delta)).astype(BF16)
            ps.append(p.astype(BF16))
            dss.append(ds)
            out.append(dq + dot(keys_t[at : at + HD], ds))
        add(j, ps, dss)
        return tuple(out)

    start = tuple(jnp.zeros((HD, BLK), F32) for _ in heads)
    carry = lax.fori_loop(0, i, lambda j, carry: visit(j, carry, False), start)
    return visit(i, carry, True)


def pair_backward_body(
    rows, whole, grad, out_t, lse, cos_t, sin_t, cosine, sine, out, keys_t, dk, dv
):
    i = pl.program_id(0)
    blocks = whole.shape[0]
    per = BLK // rows

    @pl.when(i == 0)
    def _():
        for b in range(blocks):
            keys_t[b] = flip(whole[b, :, PAIR : 2 * PAIR]).astype(BF16)
        dk[...] = jnp.zeros_like(dk)
        dv[...] = jnp.zeros_like(dv)

    query = whole[i, :, :PAIR]
    do = grad[pl.ds(i * per, per), 0:rows].reshape(BLK, PAIR)
    q_low, q_high = head_masks(flip(query))
    do_t = flip(do)
    do_low, do_high = head_masks(do_t)
    product = do_t * out_t[...]
    low = lanes(BLK) < HD
    wide_q, wide_do = query.astype(F32), do.astype(F32)
    q_rows = jnp.concatenate(
        [jnp.where(low, wide_q, 0.0), jnp.where(low, 0.0, wide_q)], axis=0
    ).astype(BF16)
    do_rows = jnp.concatenate(
        [jnp.where(low, wide_do, 0.0), jnp.where(low, 0.0, wide_do)], axis=0
    ).astype(BF16)

    def add(j, ps, dss):
        dv[j] += dot(jnp.concatenate(ps, axis=1), do_rows)
        dk[j] += dot(jnp.concatenate(dss, axis=1), q_rows)

    heads = [
        (q_low, do_low, lse[0, 0:1], jnp.sum(product[:HD], axis=0, keepdims=True), 0),
        (q_high, do_high, lse[0, 1:2], jnp.sum(product[HD:], axis=0, keepdims=True), HD),
    ]
    dqs = grads_sweep(
        i,
        heads,
        lambda j: whole[j, :, PAIR : 2 * PAIR],
        lambda j: whole[j, :, 2 * PAIR :],
        lambda j: keys_t[j],
        add,
    )
    cos, sin = cos_t[...], sin_t[...]
    dq = jnp.concatenate([unturn_t(part * SCALE, cos, sin) for part in dqs], axis=0)
    out[pl.ds(i * per, per), 0:rows] = jnp.transpose(dq).reshape(per, rows, PAIR).astype(BF16)

    @pl.when(i == blocks - 1)
    def _():
        for b in range(blocks):
            at = pl.ds(b * BLK, BLK)
            back = turn(dk[b] * (1.0 / LOG2E), cosine[at], -sine[at])
            out[b * per : (b + 1) * per, rows : 2 * rows] = back.reshape(per, rows, PAIR).astype(BF16)
            out[b * per : (b + 1) * per, 2 * rows : 3 * rows] = (
                dv[b].reshape(per, rows, PAIR).astype(BF16)
            )


def pair_backward(whole, grad, out_t, lse, cos_t, sin_t, cosine, sine):
    peers, rows = grad.shape[0], grad.shape[1] * 2 // 3
    blocks = whole.shape[0]
    shape = (peers, 3 * rows, PAIR)
    return pl.pallas_call(
        lambda *refs: pair_backward_body(rows, *refs),
        grid=(blocks,),
        in_specs=[
            const(whole.shape),
            const(grad.shape),
            pl.BlockSpec((PAIR, BLK), lambda i: (0, i)),
            pl.BlockSpec((1, 8, BLK), lambda i: (i, 0, 0)),
            pl.BlockSpec((HD // 2, BLK), lambda i: (0, i)),
            pl.BlockSpec((HD // 2, BLK), lambda i: (0, i)),
            const(cosine.shape),
            const(sine.shape),
        ],
        out_specs=const(shape),
        out_shape=jax.ShapeDtypeStruct(shape, BF16),
        scratch_shapes=[
            pltpu.VMEM((blocks, PAIR, BLK), BF16),
            pltpu.VMEM((blocks, BLK, PAIR), F32),
            pltpu.VMEM((blocks, BLK, PAIR), F32),
        ],
        compiler_params=params(),
        name="attend_pair_grads",
    )(whole, grad, out_t, lse, cos_t, sin_t, cosine, sine)


def single_backward_body(
    rows, whole, grad, out_t, lse, cos_t, sin_t, cosine, sine, out, both_t, grads, dboth
):
    i = pl.program_id(0)
    blocks = whole.shape[0]
    per = BLK // rows
    half = rows // 2

    @pl.when(i == 0)
    def _():
        for b in range(blocks):
            both_t[b] = flip(whole[b, :, :PAIR]).astype(BF16)
        grads[...] = unpack_half(grad[:, rows:], rows).reshape(blocks, BLK, PAIR)
        dboth[...] = jnp.zeros_like(dboth)

    wide_q, wide_do = whole[i, :, PAIR:].astype(F32), grads[i].astype(F32)
    q_t = jnp.transpose(wide_q).astype(BF16)
    shifted = swap_heads(wide_do)
    do_t = jnp.transpose(shifted)
    delta = jnp.sum(do_t[HD:] * out_t[...], axis=0, keepdims=True)
    sides = jnp.concatenate([wide_q, shifted], axis=0).astype(BF16)

    def add(j, ps, dss):
        dboth[j] += dot(jnp.concatenate([dss[0], ps[0]], axis=1), sides)

    (dq,) = grads_sweep(
        i,
        [(q_t, do_t.astype(BF16), lse[0, 0:1], delta, 0)],
        lambda j: whole[j, :, :PAIR],
        lambda j: whole[j, :, :PAIR],
        lambda j: both_t[j],
        add,
    )
    dq = unturn_t(dq * SCALE, cos_t[...], sin_t[...])
    tile = jnp.transpose(jnp.concatenate([dq, jnp.zeros_like(dq)], axis=0))
    out[pl.ds(i * per, per), rows : rows + half] = pack_half(tile, rows).astype(BF16)

    @pl.when(i == blocks - 1)
    def _():
        low = lanes(BLK) < HD
        for b in range(blocks):
            at = pl.ds(b * BLK, BLK)
            part = dboth[b]
            back = turn(part * (1.0 / LOG2E), cosine[at], -sine[at])
            out[b * per : (b + 1) * per, 0:rows] = (
                jnp.where(low, back, part).reshape(per, rows, PAIR).astype(BF16)
            )


def single_backward(whole, grad, out_t, lse, cos_t, sin_t, cosine, sine):
    peers, rows = grad.shape[0], grad.shape[1] * 2 // 3
    blocks = whole.shape[0]
    shape = (peers, 3 * rows // 2, PAIR)
    return pl.pallas_call(
        lambda *refs: single_backward_body(rows, *refs),
        grid=(blocks,),
        in_specs=[
            const(whole.shape),
            const(grad.shape),
            pl.BlockSpec((HD, BLK), lambda i: (0, i)),
            pl.BlockSpec((1, 8, BLK), lambda i: (i, 0, 0)),
            pl.BlockSpec((HD // 2, BLK), lambda i: (0, i)),
            pl.BlockSpec((HD // 2, BLK), lambda i: (0, i)),
            const(cosine.shape),
            const(sine.shape),
        ],
        out_specs=const(shape),
        out_shape=jax.ShapeDtypeStruct(shape, BF16),
        scratch_shapes=[
            pltpu.VMEM((blocks, PAIR, BLK), BF16),
            pltpu.VMEM((blocks, BLK, PAIR), BF16),
            pltpu.VMEM((blocks, BLK, PAIR), F32),
        ],
        compiler_params=params(),
        name="attend_single_grads",
    )(whole, grad, out_t, lse, cos_t, sin_t, cosine, sine)


def third_tiles(parts):
    low = lanes(parts[0].shape[0]) < HD
    tiles = []
    for k in (0, 2):
        a, b = parts[k], parts[k + 1]
        top = jnp.where(low, a, swap_heads(b))
        bottom = jnp.where(low, swap_heads(a), b)
        tiles.append(jnp.concatenate([top, bottom], axis=0))
    return tiles


def third_parts(tiles):
    parts = []
    for tile in tiles:
        half = tile.shape[0] // 2
        top, bottom = tile[:half], tile[half:]
        low = lanes(half) < HD
        parts.append(jnp.where(low, top, swap_heads(bottom)))
        parts.append(jnp.where(low, swap_heads(top), bottom))
    return parts


def project_body(pair, single, tok, w_attn, gain, shift, w_query, o, r1, c, cq):
    tiles = [pair[g, 0].astype(F32) for g in range(GROUPS)]
    tiles += third_tiles([single[g, 0].astype(F32) for g in range(GROUPS)])
    heads = jnp.concatenate(tiles, axis=1).astype(BF16)
    o[0] = heads
    after = tok[0].astype(F32) + dot(heads, w_attn[...])
    r1[0] = after
    row = (norm_stats(after)[0] * gain[...][None] + shift[...][None]).astype(BF16)
    c[0] = row
    cq[0] = dot(row, w_query[...]).astype(BF16)


def project_call(pair, single, tokens, w_attn, gain, shift, w_query):
    seqs, rows, _ = tokens.shape
    block = pl.BlockSpec((1, rows, D), lambda s: (s, 0, 0))
    shape = lambda kind: jax.ShapeDtypeStruct((seqs, rows, D), kind)
    return pl.pallas_call(
        project_body,
        grid=(seqs,),
        in_specs=[
            pl.BlockSpec((GROUPS, 1, rows, PAIR), lambda s: (0, s, 0, 0)),
            pl.BlockSpec((GROUPS, 1, rows // 2, PAIR), lambda s: (0, s, 0, 0)),
            block,
            const((D, D)),
            VECTOR,
            VECTOR,
            const((D, D)),
        ],
        out_specs=[block] * 4,
        out_shape=[shape(BF16), shape(F32), shape(BF16), shape(BF16)],
        compiler_params=params(),
        name="project",
    )(
        pair.reshape(GROUPS, seqs, rows, PAIR),
        single.reshape(GROUPS, seqs, rows // 2, PAIR),
        tokens,
        w_attn,
        gain,
        shift,
        w_query,
    )


def memory_body(near, weight, out):
    out[...] = dot(near[...], weight[...]).astype(BF16)


def memory_call(near, weight):
    rows = near.shape[0]
    step = min(rows, 512)
    return pl.pallas_call(
        memory_body,
        grid=(rows // step,),
        in_specs=[pl.BlockSpec((step, D), lambda i: (i, 0)), const((D, 2 * D))],
        out_specs=pl.BlockSpec((step, 2 * D), lambda i: (i, 0)),
        out_shape=jax.ShapeDtypeStruct((rows, 2 * D), BF16),
        compiler_params=params(),
        name="memory",
    )(near, weight)


def move_later(values, before):
    first = lax.broadcasted_iota(jnp.int32, values.shape, 0) == 0
    return jnp.where(first, before.astype(F32), pltpu.roll(values.astype(F32), 1, 0))


def move_earlier(values, after):
    rows = values.shape[0]
    last = lax.broadcasted_iota(jnp.int32, values.shape, 0) == rows - 1
    return jnp.where(last, after.astype(F32), pltpu.roll(values.astype(F32), rows - 1, 0))


def head_rows(tile):
    low = lanes(GROUP) < HD
    return jnp.concatenate(
        [jnp.where(low, tile, 0.0), jnp.where(low, 0.0, tile)], axis=0
    ).astype(BF16)


def fold_rows(both):
    return jnp.where(lanes(GROUP) < HD, both[:GROUP], both[GROUP:])


def cross_scores(keys, query_rows, have):
    scores = dot_nt(keys, query_rows) * (SCALE * LOG2E)
    row = lax.broadcasted_iota(jnp.int32, scores.shape, 0)
    kept = jnp.where(row < RET, have[0], have[1]) > 0
    return jnp.where(kept, scores, NEGATIVE), kept


def row_heads(row):
    return jnp.where(diagonal(), row, 0.0).astype(BF16)


def diagonal():
    head = lax.broadcasted_iota(jnp.int32, (16, D), 1) // HD
    return head == lax.broadcasted_iota(jnp.int32, (16, D), 0)


def own_heads(wide):
    return jnp.sum(jnp.where(diagonal(), wide, 0.0), axis=0, keepdims=True)


def softmax_columns(scores, kept):
    peak = jnp.max(scores, axis=0, keepdims=True)
    weights = jnp.where(kept, jnp.exp2(scores - peak), 0.0)
    total = jnp.sum(weights, axis=0, keepdims=True)
    some = total > 0.0
    safe = jnp.where(some, total, 1.0)
    return weights / safe, jnp.where(some, peak + jnp.log2(safe), 0.0)


def cross_body(windows, present, present_next, cq, memory, memory_next, out, lse, shifted, win):
    s = pl.program_id(0)
    rows = cq.shape[1]
    zero = jnp.zeros((1, D), F32)
    wide = cq[0].astype(F32)
    shifted[...] = move_later(wide, zero).reshape(windows, GROUP, D)

    def window(w, _):
        have = [present[s, w, k] for k in range(NEIGH)]
        for p in range(HEADS // 2):
            at = pl.ds(p * PAIR, PAIR)
            keys = memory[0, w, :, p * PAIR : (p + 1) * PAIR]
            values = memory[0, w, :, D + p * PAIR : D + (p + 1) * PAIR]
            ca, logs = softmax_columns(*cross_scores(keys, head_rows(shifted[w, :, at]), have))
            win[w, :, at] = fold_rows(dot_tn(ca.astype(BF16), values))
            lse[0, w, p : p + 1] = logs
        return 0

    lax.fori_loop(0, windows, window, 0)
    have = [present_next[s, k] for k in range(NEIGH)]
    ca, _ = softmax_columns(
        *cross_scores(memory_next[0, :, :D], row_heads(wide[rows - 1 :]), have)
    )
    last = own_heads(dot_tn(ca.astype(BF16), memory_next[0, :, D:]))
    out[0] = move_earlier(win[...].reshape(rows, D), last).astype(BF16)


def cross_call(present, present_next, cq, memory, memory_next):
    seqs, windows = present.shape[:2]
    rows = cq.shape[1]
    keys = NEIGH * RET
    block = pl.BlockSpec((1, rows, D), lambda s: (s, 0, 0))
    return pl.pallas_call(
        lambda *refs: cross_body(windows, *refs),
        grid=(seqs,),
        in_specs=[
            pl.BlockSpec(memory_space=pltpu.SMEM),
            pl.BlockSpec(memory_space=pltpu.SMEM),
            block,
            pl.BlockSpec((1, windows, keys, 2 * D), lambda s: (s, 0, 0, 0)),
            pl.BlockSpec((1, keys, 2 * D), lambda s: (s, 0, 0)),
        ],
        out_specs=[block, pl.BlockSpec((1, windows, 8, PAIR), lambda s: (s, 0, 0, 0))],
        out_shape=[
            jax.ShapeDtypeStruct((seqs, rows, D), BF16),
            jax.ShapeDtypeStruct((seqs, windows, 8, PAIR), F32),
        ],
        scratch_shapes=[pltpu.VMEM((windows, GROUP, D), F32)] * 2,
        compiler_params=params(),
        name="cross",
    )(present, present_next, cq, memory, memory_next)


def gelu_parts(u):
    phi = 0.5 + 0.5 * lax.erf(u * math.sqrt(0.5))
    slope = phi + u * (jnp.exp2(u * u * (-0.5 * LOG2E)) * (1.0 / math.sqrt(2.0 * math.pi)))
    return u * phi, slope


def feed_body(
    steps,
    r1,
    cross_rows,
    cot,
    w_cross,
    gain,
    shift,
    w_up,
    w_down,
    output,
    d2,
    e2,
    dr,
    vectors,
    grads,
    normed,
    inverse,
    row,
    row_t,
    total,
    grad,
    up_stage,
    down_stage,
    sems,
):
    f = pl.program_id(0)
    seqs, rows = r1.shape[:2]
    batch, sq, groups, _, own, cols = grads.shape
    near = down_stage.shape[2]

    def copies(at):
        slot = lax.rem(at, 2)
        first = at * near
        return (
            pltpu.make_async_copy(up_stage.at[slot], grads.at[at, :, :, 0], sems.at[slot, 0]),
            pltpu.make_async_copy(
                down_stage.at[slot],
                grads.at[:, pl.ds(lax.rem(first, sq), near), first // sq, 1],
                sems.at[slot, 1],
            ),
        )

    @pl.when(f == 0)
    def _():
        for s in range(seqs):
            at = pl.ds(s * rows, rows)
            r2 = r1[s] + dot(cross_rows[s], w_cross[...])
            total[at] = r2
            n, inv = norm_stats(r2)
            normed[at] = n
            inverse[at] = inv
            a3 = (n * gain[...][None] + shift[...][None]).astype(BF16)
            row[at] = a3
            row_t[:, at] = flip(a3).astype(BF16)
        grad[...] = jnp.zeros_like(grad)

    up, down = w_up[...], w_down[...]
    given = cot[...]
    act, slope = gelu_parts(dot(row[...], up))
    act_low = act.astype(BF16)
    total[...] += dot(act_low, down)
    gu = (dot_nt(given, down) * slope).astype(BF16)
    grad[...] += dot_nt(gu, up)
    part = dot(row_t[...], gu).astype(BF16)
    part_down = dot(flip(act).astype(BF16), given).astype(BF16)

    @pl.when(f >= 2)
    def _():
        for copy in copies(f - 2):
            copy.wait()

    slot = lax.rem(f, 2)
    for g in range(groups):
        for q in range(sq):
            start = (g * sq + q) * own
            up_stage[slot, q, g] = part[start : start + own]
    deep = own * cols // D
    for q in range(near):
        for b in range(batch):
            start = (q * batch + b) * deep
            for x in range(D // cols):
                down_stage[slot, b, q, x * deep : (x + 1) * deep] = part_down[
                    start : start + deep, x * cols : (x + 1) * cols
                ]
    for copy in copies(f):
        copy.start()

    @pl.when(f == steps - 1)
    def _():
        output[...] = total[...].astype(BF16)
        n, back = normed[...], grad[...]
        vectors[0:1] = jnp.sum(n * back, axis=0, keepdims=True)
        vectors[1:2] = jnp.sum(back, axis=0, keepdims=True)
        summed = given.astype(F32) + norm_back(n, inverse[...], gain[...][None], back)
        d2[...] = summed
        low = summed.astype(BF16)
        e2[...] = low
        dr[...] = dot_nt(low, w_cross[...]).astype(BF16)
        for at in (steps - 2, steps - 1):
            for copy in copies(at):
                copy.wait()


def feed_call(r1, cross_rows, cot, w_cross, gain, shift, w_up, w_down, batch, peers):
    seqs, rows, _ = r1.shape
    count = seqs * rows
    sq = peers // GROUPS
    steps = batch
    cols = FF // steps
    own = D // peers
    near = peers // batch
    flat = jax.ShapeDtypeStruct((count, D), BF16)
    wide = jax.ShapeDtypeStruct((count, D), F32)
    return pl.pallas_call(
        lambda *refs: feed_body(steps, *refs),
        grid=(steps,),
        in_specs=[
            const((seqs, rows, D)),
            const((seqs, rows, D)),
            const((count, D)),
            const((D, D)),
            VECTOR,
            VECTOR,
            pl.BlockSpec((D, cols), lambda f: (0, f)),
            pl.BlockSpec((cols, D), lambda f: (f, 0)),
        ],
        out_specs=[const((count, D))] * 4
        + [const((8, D)), pl.BlockSpec(memory_space=pl.ANY)],
        out_shape=[
            flat,
            wide,
            flat,
            flat,
            jax.ShapeDtypeStruct((8, D), F32),
            jax.ShapeDtypeStruct((batch, sq, GROUPS, 2, own, cols), BF16),
        ],
        scratch_shapes=[
            pltpu.VMEM((count, D), F32),
            pltpu.VMEM((count, 1), F32),
            pltpu.VMEM((count, D), BF16),
            pltpu.VMEM((D, count), BF16),
            pltpu.VMEM((count, D), F32),
            pltpu.VMEM((count, D), F32),
            pltpu.VMEM((2, sq, GROUPS, own, cols), BF16),
            pltpu.VMEM((2, batch, near, own, cols), BF16),
            pltpu.SemaphoreType.DMA((2, 2)),
        ],
        compiler_params=params(),
        name="feed",
    )(r1, cross_rows, cot, w_cross, gain, shift, w_up, w_down)


def cross_back_body(
    windows, present, present_next, cq, dr, memory, memory_next, lse, dmem, dcq, shifted, dwin, dshifted
):
    s = pl.program_id(0)
    rows = cq.shape[1]
    zero = jnp.zeros((1, D), F32)
    wide, wide_dr = cq[0].astype(F32), dr[0].astype(F32)
    shifted[...] = move_later(wide, zero).reshape(windows, GROUP, D)
    dwin[...] = move_later(wide_dr, zero).reshape(windows, GROUP, D)

    def window(w, _):
        have = [present[s, w, k] for k in range(NEIGH)]
        for p in range(HEADS // 2):
            at = pl.ds(p * PAIR, PAIR)
            keys = memory[0, w, :, p * PAIR : (p + 1) * PAIR]
            values = memory[0, w, :, D + p * PAIR : D + (p + 1) * PAIR]
            query_rows = head_rows(shifted[w, :, at])
            grad_rows = head_rows(dwin[w, :, at])
            scores, kept = cross_scores(keys, query_rows, have)
            ca = jnp.where(kept, jnp.exp2(scores - lse[0, w, p : p + 1]), 0.0)
            dca = dot_nt(values, grad_rows)
            inner = jnp.sum(ca * dca, axis=0, keepdims=True)
            dcs = (ca * (dca - inner)).astype(BF16)
            dmem[0, w, :, at] = (dot(dcs, query_rows) * SCALE).astype(BF16)
            dmem[0, w, :, pl.ds(D + p * PAIR, PAIR)] = dot(ca.astype(BF16), grad_rows).astype(BF16)
            dshifted[w, :, at] = fold_rows(dot_tn(dcs, keys)) * SCALE
        return 0

    lax.fori_loop(0, windows, window, 0)
    have = [present_next[s, k] for k in range(NEIGH)]
    _, dcs, _ = row_grads(memory_next[0], wide[rows - 1 :], wide_dr[rows - 1 :], have)
    last = own_heads(dot_tn(dcs, memory_next[0, :, :D])) * SCALE
    dcq[0] = move_earlier(dshifted[...].reshape(rows, D), last).astype(BF16)


def row_grads(memory, row, grad, have):
    query_rows, grad_rows = row_heads(row), row_heads(grad)
    ca, _ = softmax_columns(*cross_scores(memory[:, :D], query_rows, have))
    dca = dot_nt(memory[:, D:], grad_rows)
    inner = jnp.sum(ca * dca, axis=0, keepdims=True)
    return ca.astype(BF16), (ca * (dca - inner)).astype(BF16), (query_rows, grad_rows)


def cross_back_call(present, present_next, cq, dr, memory, memory_next, lse):
    seqs, windows = present.shape[:2]
    rows = cq.shape[1]
    keys = NEIGH * RET
    block = pl.BlockSpec((1, rows, D), lambda s: (s, 0, 0))
    wide = pl.BlockSpec((1, windows, keys, 2 * D), lambda s: (s, 0, 0, 0))
    return pl.pallas_call(
        lambda *refs: cross_back_body(windows, *refs),
        grid=(seqs,),
        in_specs=[
            pl.BlockSpec(memory_space=pltpu.SMEM),
            pl.BlockSpec(memory_space=pltpu.SMEM),
            block,
            block,
            wide,
            pl.BlockSpec((1, keys, 2 * D), lambda s: (s, 0, 0)),
            pl.BlockSpec((1, windows, 8, PAIR), lambda s: (s, 0, 0, 0)),
        ],
        out_specs=[wide, block],
        out_shape=[
            jax.ShapeDtypeStruct((seqs, windows, keys, 2 * D), BF16),
            jax.ShapeDtypeStruct((seqs, rows, D), BF16),
        ],
        scratch_shapes=[pltpu.VMEM((windows, GROUP, D), F32)] * 3,
        compiler_params=params(),
        name="cross_grads",
    )(present, present_next, cq, dr, memory, memory_next, lse)


def project_back_body(dcq, r1, d2, w_query, gain, w_attn, do, d1, e1, vectors):
    s = pl.program_id(0)
    rows = r1.shape[1]
    back = dot_nt(dcq[0], w_query[...])
    normed, inverse = norm_stats(r1[0])

    @pl.when(s == 0)
    def _():
        vectors[...] = jnp.zeros_like(vectors)

    vectors[0:1] += jnp.sum(normed * back, axis=0, keepdims=True)
    vectors[1:2] += jnp.sum(back, axis=0, keepdims=True)
    summed = d2[0] + norm_back(normed, inverse, gain[...][None], back)
    d1[0] = summed
    low = summed.astype(BF16)
    e1[0] = low
    heads = dot_nt(low, w_attn[...])
    for g in range(GROUPS):
        do[g, 0, 0:rows] = heads[:, g * PAIR : (g + 1) * PAIR].astype(BF16)
    tiles = [heads[:, (GROUPS + k) * PAIR : (GROUPS + k + 1) * PAIR] for k in range(2)]
    for g, part in enumerate(third_parts(tiles)):
        do[g, 0, rows:] = part.astype(BF16)


def project_back_call(dcq, r1, d2, w_query, gain, w_attn):
    seqs, rows, _ = r1.shape
    block = pl.BlockSpec((1, rows, D), lambda s: (s, 0, 0))
    shape = lambda kind: jax.ShapeDtypeStruct((seqs, rows, D), kind)
    return pl.pallas_call(
        project_back_body,
        grid=(seqs,),
        in_specs=[
            block,
            block,
            block,
            const((D, D)),
            VECTOR,
            const((D, D)),
        ],
        out_specs=[
            pl.BlockSpec((GROUPS, 1, rows + rows // 2, PAIR), lambda s: (0, s, 0, 0)),
            block,
            block,
            const((8, D)),
        ],
        out_shape=[
            jax.ShapeDtypeStruct((GROUPS, seqs, rows + rows // 2, PAIR), BF16),
            shape(F32),
            shape(BF16),
            jax.ShapeDtypeStruct((8, D), F32),
        ],
        compiler_params=params(),
        name="project_grads",
    )(dcq, r1, d2, w_query, gain, w_attn)


def put_rows(place, outs, block, value):
    batch, groups, part, _ = outs[0].shape[:1] + outs[0].shape[-3:]
    sq = 2 if len(outs) == 2 else outs[0].shape[1]
    own = D // (sq * groups)
    value = value.astype(BF16)

    def store(q, slot):
        for g in range(groups):
            start, done = block * own, 0
            at = (g * sq + q) * own
            while done < own:
                b, x = divmod(start + done, part)
                count = min(part - x, own - done)
                slot(b, g, x, count, value[at + done : at + done + count])
                done += count

    for q in range(sq):
        if len(outs) == 1:

            def put(b, g, x, count, rows, q=q):
                outs[0][b, q, g, x : x + count] = rows

            store(q, put)
            continue
        for k, out in enumerate(outs):

            @pl.when(place[1] == q ^ k)
            def _(q=q, out=out):
                def put(b, g, x, count, rows):
                    out[b, g, x : x + count] = rows

                store(q, put)


def others_body(
    split,
    place,
    present,
    near,
    dmem,
    memory,
    before,
    w_memory,
    o,
    e1,
    c,
    dq,
    cross_rows,
    e2,
    vectors,
    dnear,
    *refs,
):
    outs, acc = refs[:-1], refs[-1]
    s = pl.program_id(0)
    keys = memory.shape[2]
    have = [present[s, 0, k] for k in range(NEIGH)]
    ca, dcs, (query_rows, grad_rows) = row_grads(
        memory[0, 0], before[0, 0:1].astype(F32), before[0, 1:2].astype(F32), have
    )
    edge = jnp.concatenate([dot(dcs, query_rows) * SCALE, dot(ca, grad_rows)], axis=1)
    first = (dmem[0, 0].astype(F32) + edge).astype(BF16)
    whole = dmem[0].reshape(-1, 2 * D)
    grads = jnp.concatenate([first, whole[keys:]], axis=0) if whole.shape[0] > keys else first
    dnear[...] = dot_nt(grads, w_memory[...]).astype(BF16)
    part = dot_tn(near[...], grads)

    @pl.when(s == 0)
    def _():
        acc[...] = part
        put_rows(place, outs, 0, dot_tn(o[...], e1[...]))
        put_rows(place, outs, 1, dot_tn(c[...], dq[...]))

    @pl.when(s > 0)
    def _():
        acc[...] += part

    @pl.when(s == pl.num_programs(0) - 1)
    def _():
        put_rows(place, outs, 2, dot_tn(cross_rows[...], e2[...]))
        put_rows(place, outs, 3, acc[:, :D])
        put_rows(place, outs, 4, acc[:, D:])
        batch, groups, size = outs[0].shape[0], outs[0].shape[-3], outs[0].shape[-2]
        sq = vectors.shape[0] // groups
        used = 5 * D // (sq * groups) - (batch - 1) * size
        for g in range(groups):
            if split:
                for k, out in enumerate(outs):
                    out[batch - 1, g, used:] = vectors[g * sq + (place[1] ^ k)]
            else:
                for q in range(sq):
                    outs[0][batch - 1, q, g, used:] = vectors[g * sq + q]


def others_call(
    split,
    place,
    present,
    near,
    dmem,
    memory,
    before,
    w_memory,
    o,
    e1,
    c,
    dq,
    cross_rows,
    e2,
    vectors,
    batch,
    peers,
):
    seqs, windows, keys, _ = dmem.shape
    count = o.shape[0]
    step = windows * keys
    own = D // peers
    size = (5 * own + vectors.shape[1]) // batch
    shapes = [(batch, peers // GROUPS, GROUPS, size, D)]
    if split:
        shapes = [(batch, GROUPS, size, D)] * 2
    smem = pl.BlockSpec(memory_space=pltpu.SMEM)
    return pl.pallas_call(
        lambda *refs: others_body(split, *refs),
        grid=(seqs,),
        in_specs=[
            smem,
            smem,
            pl.BlockSpec((step, D), lambda s: (s, 0)),
            pl.BlockSpec((1, windows, keys, 2 * D), lambda s: (s, 0, 0, 0)),
            pl.BlockSpec((1, 1, keys, 2 * D), lambda s: (s, 0, 0, 0)),
            pl.BlockSpec((1, 2, D), lambda s: (s, 0, 0)),
            const((D, 2 * D)),
        ]
        + [const((count, D))] * 6
        + [const(vectors.shape)],
        out_specs=[pl.BlockSpec((step, D), lambda s: (s, 0))] + [const(shape) for shape in shapes],
        out_shape=[jax.ShapeDtypeStruct(near.shape, BF16)]
        + [jax.ShapeDtypeStruct(shape, BF16) for shape in shapes],
        scratch_shapes=[pltpu.VMEM((D, 2 * D), F32)],
        compiler_params=params(),
        name="other_grads",
    )(place, present, near, dmem, memory, before, w_memory, o, e1, c, dq, cross_rows, e2, vectors)


def last_body(pair, single, tok, d1, gain, w_qkv, out):
    rows = tok.shape[1]
    half = rows // 2
    low = lanes(rows) < HD
    boths = [single[g, 0, 0:rows].astype(F32) for g in range(GROUPS)]
    queries = third_tiles([single[g, 0, rows : rows + half].astype(F32) for g in range(GROUPS)])
    keys = [jnp.where(low, boths[k], swap_heads(boths[k + 1])) for k in (0, 2)]
    values = [jnp.where(low, swap_heads(boths[k]), boths[k + 1]) for k in (0, 2)]
    parts = []
    for at, third in ((0, queries), (rows, keys), (2 * rows, values)):
        parts += [pair[g, 0, at : at + rows] for g in range(GROUPS)]
        parts += [tile.astype(BF16) for tile in third]
    back = dot_nt(jnp.concatenate(parts, axis=1), w_qkv[...])
    normed, inverse = norm_stats(tok[0].astype(F32))
    out[0] = (d1[0] + norm_back(normed, inverse, gain[...][None], back)).astype(BF16)


def last_call(pair, single, tokens, d1, gain, w_qkv):
    seqs, rows, _ = tokens.shape
    block = pl.BlockSpec((1, rows, D), lambda s: (s, 0, 0))
    return pl.pallas_call(
        last_body,
        grid=(seqs,),
        in_specs=[
            pl.BlockSpec((GROUPS, 1, 3 * rows, PAIR), lambda s: (0, s, 0, 0)),
            pl.BlockSpec((GROUPS, 1, 3 * rows // 2, PAIR), lambda s: (0, s, 0, 0)),
            block,
            block,
            VECTOR,
            const((D, 3 * D)),
        ],
        out_specs=block,
        out_shape=jax.ShapeDtypeStruct((seqs, rows, D), BF16),
        compiler_params=params(),
        name="token_grads",
    )(
        pair.reshape(GROUPS, seqs, 3 * rows, PAIR),
        single.reshape(GROUPS, seqs, 3 * rows // 2, PAIR),
        tokens,
        d1,
        gain,
        w_qkv,
    )


def heads_body(place, *refs):
    pieces, (pair, single, gain, shift) = refs[:GROUPS], refs[GROUPS : GROUPS + 4]
    weights, (out, acc, sums, held) = refs[GROUPS + 4 : GROUPS + 10], refs[GROUPS + 10 :]
    i = pl.program_id(0)
    per, rows = pair.shape[0], pair.shape[1] // 3
    for k, piece in enumerate(pieces):

        @pl.when(i == k)
        def _(piece=piece):
            held[...] = piece[...]

    third = unpack_half(single[:, rows : rows + rows // 2], rows)
    grads = jnp.concatenate(
        [pair[:, k * rows : (k + 1) * rows].reshape(per * rows, PAIR) for k in range(3)]
        + [single[:, 0:rows].reshape(per * rows, PAIR), third],
        axis=1,
    )
    part = dot_tn(held[...], grads)
    total = jnp.sum(grads.astype(F32), axis=0, keepdims=True)

    @pl.when(i == 0)
    def _():
        acc[...] = part
        sums[0:1] = total

    @pl.when(i > 0)
    def _():
        acc[...] += part
        sums[0:1] += total

    @pl.when(i == pl.num_programs(0) - 1)
    def _():
        low = lanes(D) < HD
        odd = lax.rem(place[0], 2) == 1
        wide = [weight[...].astype(F32) for weight in weights]
        q3, k3, v3 = [jnp.where(odd, swap_heads(t), t) for t in wide[3:]]
        columns = wide[:3] + [jnp.where(low, k3, swap_heads(v3)), jnp.where(low, q3, 0.0)]
        columns = jnp.concatenate(columns, axis=1)
        whole, over = acc[...], sums[0:1]
        d_gain = jnp.sum(whole * columns, axis=1, keepdims=True)
        d_shift = jnp.sum(over * columns, axis=1, keepdims=True)
        lane = lax.broadcasted_iota(jnp.int32, whole.shape, 1)
        value = whole * gain[...] + shift[...] * over
        at = 4 * PAIR + HD
        value = jnp.where(lane == at, d_gain, jnp.where(lane == at + 1, d_shift, value))
        high, low, sq, groups, own, _ = out.shape
        for g in range(groups):
            for q in range(sq):
                for b in range(high * low):
                    start = ((g * sq + q) * high * low + b) * own
                    out[b // low, b % low, q, g] = value[start : start + own].astype(BF16)


def heads_call(place, pieces, pair, single, gain, shift, weight, batch):
    peers, rows = pair.shape[0], pair.shape[1] // 3
    per = peers // GROUPS
    shape = (batch // 2, 2, per, GROUPS, D // peers // batch, 5 * PAIR)

    def chunk(i, place):
        return (place[2 + i], 0, 0)

    return pl.pallas_call(
        heads_body,
        grid_spec=pltpu.PrefetchScalarGridSpec(
            num_scalar_prefetch=1,
            grid=(GROUPS,),
            in_specs=[const((per * rows, D))] * GROUPS
            + [
                pl.BlockSpec((per, 3 * rows, PAIR), chunk),
                pl.BlockSpec((per, 3 * rows // 2, PAIR), chunk),
                const((D, 1)),
                const((D, 1)),
            ]
            + head_columns(0),
            out_specs=const(shape),
            scratch_shapes=[
                pltpu.VMEM((D, 5 * PAIR), F32),
                pltpu.VMEM((8, 5 * PAIR), F32),
                pltpu.VMEM((per * rows, D), BF16),
            ],
        ),
        out_shape=jax.ShapeDtypeStruct(shape, BF16),
        compiler_params=params(),
        name="qkv_grads",
    )(place, *pieces, pair, single, gain.reshape(D, 1), shift.reshape(D, 1), *[weight] * 6)


SEQ = ("hg", "sq")
BATCH = ("by", "bx")


def from_behind(value, by):
    peers = lax.axis_size(SEQ)
    pairs = [(i, i + by) for i in range(peers) if 0 <= i + by < peers]
    return lax.ppermute(value, SEQ, pairs)


def swap_all(value):
    return lax.all_to_all(value, SEQ, 0, 0, tiled=True)


def add_rows(value):
    flat = value.reshape((value.shape[0] * value.shape[1],) + value.shape[2:])
    own = lax.psum_scatter(flat, BATCH + ("sq",), scatter_dimension=0, tiled=True)
    return own.reshape(value.shape[2:])


def rotated(value, by):
    return lax.ppermute(value, "hg", [(i, (i + by) % GROUPS) for i in range(GROUPS)])


def add_groups(own):
    here = lax.axis_index("hg")
    total = lax.dynamic_index_in_dim(own, here, 0, keepdims=False).astype(F32)
    for k in range(1, GROUPS):
        part = lax.dynamic_index_in_dim(own, lax.rem(here + k, GROUPS), 0, keepdims=False)
        total += rotated(part, k).astype(F32)
    return total.astype(BF16)


def gather_groups(own):
    here = lax.axis_index("hg")
    pieces = [lax.dynamic_index_in_dim(own, here, 0, keepdims=False)]
    for k in range(1, GROUPS):
        part = lax.dynamic_index_in_dim(own, lax.rem(here + k, GROUPS), 0, keepdims=False)
        pieces.append(rotated(part, k))
    return in_order([pieces[(-j) % GROUPS] for j in range(GROUPS)], here, "shift")


def passed(value, by):
    pairs = [(i, i + by) for i in range(GROUPS) if 0 <= i + by < GROUPS]
    return lax.ppermute(value, "hg", pairs)


def in_order(pieces, here, how):
    count = len(pieces)
    out = []
    for j in range(count):
        value = pieces[j]
        for me in range(1, count):
            at = (j - me) % count if how == "shift" else j ^ me
            value = jnp.where(here == me, pieces[at], value)
        out.append(value)
    return out


def gather_batch(value):
    size = lax.axis_size(BATCH)
    pieces = [value] + [
        lax.ppermute(value, BATCH, [(i, i ^ k) for i in range(size)]) for k in range(1, size)
    ]
    return in_order(pieces, lax.axis_index(BATCH), "xor")


def halve(value, name, axis):
    if lax.axis_size(name) == 2:
        here = lax.axis_index(name)
        kept = lax.dynamic_index_in_dim(value, here, axis, keepdims=False)
        given = lax.dynamic_index_in_dim(value, 1 - here, axis, keepdims=False)
        got = lax.ppermute(given, name, [(0, 1), (1, 0)])
        return (kept.astype(F32) + got.astype(F32)).astype(BF16)
    parts = lax.all_to_all(value, name, axis, 0, tiled=False)
    return jnp.sum(parts.astype(F32), axis=0).astype(BF16)


def own_sequence(value):
    if lax.axis_size("sq") == 2:
        here = lax.axis_index("sq")
        kept = lax.dynamic_index_in_dim(value, here, 0, keepdims=False)
        given = lax.dynamic_index_in_dim(value, 1 - here, 0, keepdims=False)
        return [kept, lax.ppermute(given, "sq", [(0, 1), (1, 0)])]
    return [lax.all_to_all(value, "sq", 0, 0, tiled=True)]


def together(*values):
    return lax.optimization_barrier(values)


def shards(
    tokens,
    neighbours,
    present,
    qkv_weight,
    attn_weight,
    query_weight,
    memory_weight,
    cross_weight,
    up_weight,
    down_weight,
    attn_gain,
    attn_shift,
    cross_gain,
    cross_shift,
    mlp_gain,
    mlp_shift,
    cotangent,
):
    seqs, rows = tokens.shape[:2]
    count = seqs * rows
    peers = lax.axis_size(SEQ)
    batch = lax.axis_size(BATCH)
    easy = [lax.axis_size(name) for name in ("by", "bx", "sq")] == [2, 2, 2]
    group, core = lax.axis_index("hg"), lax.axis_index("sq")
    place = jnp.stack([group, core] + [chunk_of(which, group) for which in range(GROUPS)])
    place = place.astype(jnp.int32)
    cos_np, sin_np = rope_tables(peers * rows)
    cosine, sine = jnp.asarray(cos_np), jnp.asarray(sin_np)
    cos_t = jnp.asarray(np.ascontiguousarray(cos_np[:, : HD // 2].T))
    sin_t = jnp.asarray(np.ascontiguousarray(sin_np[:, HD // 2 : HD].T))

    windows = present.shape[1]
    keys = NEIGH * RET
    near = neighbours.reshape(-1, D)

    def chunk(which, first, second):
        return chunk_call(
            which, place, first, second, attn_gain, attn_shift, qkv_weight, cosine, sine
        )

    own = own_sequence(tokens)
    behind, ahead = [passed(part, 1) for part in own], [passed(part, -1) for part in own]
    chunks = [chunk(0, own, own)]
    chunks[0], behind[0], ahead[0] = together(chunks[0], behind[0], ahead[0])
    behind_two = [passed(part, 1) for part in behind]
    ahead_two = [passed(part, -1) for part in ahead]
    memory = memory_call(near, memory_weight)
    memory, behind_two[0], ahead_two[0] = together(memory, behind_two[0], ahead_two[0])
    chunks.append(chunk(1, ahead, behind))
    chunks[1], behind_two[-1], ahead_two[-1] = together(chunks[1], behind_two[-1], ahead_two[-1])
    behind_three = [passed(part, 1) for part in behind_two]
    ahead_three = [passed(part, -1) for part in ahead_two]
    chunks.append(chunk(2, ahead_two, behind_two))
    chunks[2], behind_three, ahead_three = together(chunks[2], behind_three, ahead_three)
    last = [jnp.where(group == GROUPS - 1, x, y) for x, y in zip(behind_three, behind)]
    chunks.append(chunk(3, ahead_three, last))
    memory = memory.reshape(seqs, windows, keys, 2 * D)
    near_next, chunks[3] = together(neighbours[:, 0].reshape(seqs * keys, D), chunks[3])
    near_next = from_behind(near_next, -1)
    present_next = from_behind(present[:, 0], -1)
    pieces = [chunk[0] for chunk in chunks]
    o_pair, o_pair_t, lse_pair, pairs = pair_forward(place, [chunk[1] for chunk in chunks])
    singles, o_pair, near_next = together([chunk[2] for chunk in chunks], o_pair, near_next)
    memory_next = memory_call(near_next, memory_weight).reshape(seqs, keys, 2 * D)
    o_pair = swap_all(o_pair.reshape(peers, rows, PAIR))
    o_single, o_single_t, lse_single, singles = single_forward(place, singles, rows)
    o_single, o_pair = together(o_single, o_pair)
    o_single = swap_all(o_single)
    o_single, memory_next = together(o_single, memory_next)
    o, r1, c, cq = project_call(
        o_pair, o_single, tokens, attn_weight, cross_gain, cross_shift, query_weight
    )
    cross_rows, lse = cross_call(present, present_next, cq, memory, memory_next)
    output, d2, e2, dr, mlp_vectors, feed = feed_call(
        r1,
        cross_rows,
        cotangent.reshape(count, D),
        cross_weight,
        mlp_gain,
        mlp_shift,
        up_weight,
        down_weight,
        batch,
        peers,
    )
    feed = add_rows(feed)
    dr = dr.reshape(seqs, rows, D)
    before = jnp.concatenate([cq[:, -1:], dr[:, -1:]], axis=1)
    dmem, dq = cross_back_call(present, present_next, cq, dr, memory, memory_next, lse)
    dq, before = together(dq, before)
    before = from_behind(before, 1)
    do, d1, e1, cross_vectors = project_back_call(
        dq, r1, d2.reshape(seqs, rows, D), query_weight, cross_gain, attn_weight
    )
    do, before = together(do, before)
    do = swap_all(do.reshape(peers, 3 * rows // 2, PAIR))
    own = D // peers
    vectors = jnp.concatenate([mlp_vectors[:2], cross_vectors[:2]], axis=0).astype(BF16)
    vectors = vectors.reshape(4, peers, own).transpose(1, 0, 2).reshape(peers, 1, 4 * own)
    vectors = jnp.pad(vectors, ((0, 0), (0, own // 3 - 1), (0, D - 4 * own)))
    dnear, *others = others_call(
        easy,
        place,
        present,
        near,
        dmem,
        memory,
        before,
        memory_weight,
        o.reshape(count, D),
        e1.reshape(count, D),
        c.reshape(count, D),
        dq.reshape(count, D),
        cross_rows.reshape(count, D),
        e2,
        vectors,
        batch,
        peers,
    )
    do, others = together(do, others)
    if easy:
        kept, given = others
        got = lax.ppermute(given, "sq", [(0, 1), (1, 0)])
    else:
        others = add_rows(others[0])
    d_single = single_backward(singles, do, o_single_t, lse_single, cos_t, sin_t, cosine, sine)
    do, d_single, feed = together(do, d_single, feed)
    d_single_all = swap_all(d_single)
    feed = lax.psum_scatter(feed, "hg", scatter_dimension=0, tiled=False)
    d_pair = pair_backward(pairs, do, o_pair_t, lse_pair, cos_t, sin_t, cosine, sine)
    d_pair_all, d_single_all = together(d_pair, d_single_all)
    d_pair_all = swap_all(d_pair_all)
    if easy:
        d_pair, kept, got = together(d_pair, kept, got)
        others = (kept.astype(F32) + got.astype(F32)).astype(BF16)
        others = others.reshape((2, 2) + others.shape[1:])
        cut = GROUPS // 2
        others = [halve(others[:, :, :cut], "bx", 1), halve(others[:, :, cut:], "by", 0)]
    g_qkv = heads_call(place, pieces, d_pair, d_single, attn_gain, attn_shift, qkv_weight, batch)
    g_qkv, others, feed = together(g_qkv, others, feed)
    if easy:
        others = [halve(others[0], "by", 0), halve(others[1], "bx", 0)]
        others = jnp.concatenate(others, axis=0)
    g_qkv = halve(halve(halve(g_qkv, "sq", 2), "bx", 1), "by", 0)
    feed = gather_batch(feed)
    g_qkv, others, feed = together(g_qkv, others, feed)
    others = add_groups(others)
    g_qkv = jnp.stack(gather_groups(g_qkv))
    g_qkv, others, d_pair_all = together(g_qkv, others, d_pair_all)
    others = gather_batch(others)
    g_qkv = jnp.stack(gather_batch(g_qkv))
    grad_tokens = last_call(d_pair_all, d_single_all, tokens, d1, attn_gain, qkv_weight)

    others = jnp.concatenate(others, axis=0).astype(F32)
    kinds = [others[k * own : (k + 1) * own] for k in range(5)]
    others = others[5 * own, : 4 * own].reshape(4, own)
    g_up = jnp.concatenate([part[0] for part in feed], axis=1).astype(F32)
    deep = FF // peers // batch
    g_down = jnp.stack([part[1] for part in feed]).reshape(batch, D * batch // FF, deep, FF // batch)
    g_down = g_down.transpose(0, 2, 1, 3).reshape(FF // peers, D).astype(F32)
    g_qkv = g_qkv.transpose(0, 2, 1, 3).reshape(own, GROUPS, 5 * PAIR).astype(F32)

    def mine(start, width):
        return g_qkv[:, :, start : start + width].reshape(own, GROUPS * width)

    third = 3 * PAIR
    grad_qkv = jnp.concatenate(
        [
            mine(0, PAIR),
            mine(4 * PAIR, HD),
            mine(PAIR, PAIR),
            mine(third, HD),
            mine(2 * PAIR, PAIR),
            mine(third + HD, HD),
        ],
        axis=1,
    )
    vectors = jnp.sum(g_qkv[:, :, 4 * PAIR + HD : 4 * PAIR + HD + 2], axis=1)
    return (
        output.reshape(seqs, rows, D),
        grad_tokens,
        dnear.reshape(neighbours.shape),
        grad_qkv,
        kinds[0],
        kinds[1],
        jnp.concatenate(kinds[3:], axis=1),
        kinds[2],
        g_up,
        g_down,
        vectors[:, 0],
        vectors[:, 1],
        others[2],
        others[3],
        others[0],
        others[1],
    )


def solution(mesh):
    batch, seq = mesh.shape["batch"], mesh.shape["seq"]
    fine = Mesh(
        mesh.devices.reshape(batch // 2, 2, GROUPS, seq // GROUPS), ("by", "bx", "hg", "sq")
    )
    rows = P(BATCH, SEQ, None)
    windows = P(BATCH, SEQ, None, None, None)
    return jax.shard_map(
        shards,
        mesh=fine,
        in_specs=(rows, windows, rows) + (P(),) * 13 + (rows,),
        out_specs=(rows, rows, windows) + (P(SEQ, None),) * 7 + (P(SEQ),) * 6,
        check_vma=False,
    )
```

```python
import math

import jax
import jax.numpy as jnp
import numpy as np
from jax import lax
from jax.experimental import pallas as pl
from jax.experimental.pallas import tpu as pltpu
from jax.sharding import Mesh
from jax.sharding import PartitionSpec as P

D = 768
HEADS = 12
HD = 64
FF = 3072
GROUP = 64
NEIGH = 2
RET = 128
PAIR = 128
BLK = 512
GROUPS = 4

EPSILON = 1e-05
NEGATIVE = -1e30
SCALE = 1.0 / math.sqrt(HD)
LOG2E = math.log2(math.e)
VMEM_LIMIT = 56 * 1024 * 1024

F32 = jnp.float32
BF16 = jnp.bfloat16


def params(limit=VMEM_LIMIT):
    return pltpu.CompilerParams(vmem_limit_bytes=limit)


def dot(left, right):
    return jnp.dot(left, right, preferred_element_type=F32)


def dot_nt(left, right):
    return lax.dot_general(left, right, (((1,), (1,)), ((), ())), preferred_element_type=F32)


def dot_tn(left, right):
    return lax.dot_general(left, right, (((0,), (0,)), ((), ())), preferred_element_type=F32)


def flip(value):
    return jnp.transpose(value.astype(F32))


def rope_tables(length):
    half = HD // 2
    frequency = np.float32(10000.0) ** (-np.arange(half, dtype=np.float32) * np.float32(2.0) / np.float32(HD))
    angles = np.arange(length, dtype=np.float32)[:, None] * frequency[None, :].astype(np.float32)
    cosine, sine = np.cos(angles).astype(np.float32), np.sin(angles).astype(np.float32)
    return (
        np.concatenate([cosine] * 4, axis=1),
        np.concatenate([-sine, sine] * 2, axis=1),
    )


def lanes(rows):
    return lax.broadcasted_iota(jnp.int32, (rows, PAIR), 1)


def turn(tile, cosine, sine):
    rows = tile.shape[0]
    first = (lanes(rows) % HD) < HD // 2
    swapped = jnp.where(first, pltpu.roll(tile, PAIR - HD // 2, 1), pltpu.roll(tile, HD // 2, 1))
    return tile * cosine + swapped * sine


def swap_heads(tile):
    return pltpu.roll(tile, HD, 1)


def norm_stats(values):
    mean = jnp.mean(values, axis=-1, keepdims=True)
    centred = values - mean
    inverse = lax.rsqrt(jnp.mean(centred * centred, axis=-1, keepdims=True) + EPSILON)
    return centred * inverse, inverse


def norm_back(normed, inverse, gain, grad):
    scaled = grad * gain
    return inverse * (
        scaled
        - jnp.mean(scaled, axis=-1, keepdims=True)
        - normed * jnp.mean(scaled * normed, axis=-1, keepdims=True)
    )


VECTOR = pl.BlockSpec((D,), lambda *ids: (0,))


def const(shape):
    rank = len(shape)
    return pl.BlockSpec(shape, lambda *ids: (0,) * rank)


def chunk_body(which, place, *refs):
    halves = (len(refs) - 15) // 2
    near, far, refs = refs[:halves], refs[halves : 2 * halves], refs[2 * halves :]
    gain, shift = refs[:2]
    weights, (cosine, sine, normed, pair, single, tokens, columns) = refs[2:8], refs[8:]
    rows = tokens.shape[0] // halves
    first = use_first(which, place[0])
    for parts, wanted in ((near, first), (far, jnp.logical_not(first))):

        @pl.when(wanted)
        def _(parts=parts):
            for k, part in enumerate(parts):
                at = place[1] * (1 - 2 * k) + k if halves > 1 else 0
                tokens[pl.ds(at * rows, rows)] = part[...].reshape(rows, D)

    odd = lax.rem(place[0], 2) == 1
    for k, weight in enumerate(weights):
        columns[:, k * PAIR : (k + 1) * PAIR] = weight[...]
    n, _ = norm_stats(tokens[...].astype(F32))
    normed[...] = n.astype(BF16)
    out = dot((n * gain[...][None] + shift[...][None]).astype(BF16), columns[...])
    cos, sin = cosine[...], sine[...]
    q01, k01, v01, q2, k2, v2 = [out[:, k * PAIR : (k + 1) * PAIR] for k in range(6)]
    low = lanes(tokens.shape[0]) < HD
    q2, k2, v2 = [jnp.where(odd, swap_heads(t), t) for t in (q2, k2, v2)]
    pair[:, :PAIR] = (turn(q01, cos, sin) * (SCALE * LOG2E)).astype(BF16)
    pair[:, PAIR : 2 * PAIR] = turn(k01, cos, sin).astype(BF16)
    pair[:, 2 * PAIR :] = v01.astype(BF16)
    single[:, :PAIR] = jnp.where(low, turn(k2, cos, sin), swap_heads(v2)).astype(BF16)
    single[:, PAIR:] = jnp.where(low, turn(q2, cos, sin) * (SCALE * LOG2E), 0.0).astype(BF16)


def use_first(which, group):
    if which == 0:
        return group >= 0
    if which == 1:
        return group < GROUPS - 1
    if which == 2:
        return group < 2
    return group == 0


def chunk_of(which, group):
    if which == 0:
        return group
    if which == 1:
        return jnp.where(group < GROUPS - 1, group + 1, group - 1)
    if which == 2:
        return lax.rem(group + 2, GROUPS)
    return jnp.where(group == 0, GROUPS - 1, jnp.where(group == GROUPS - 1, 0, group - 1))


def head_columns(index):
    def column(first, shared):
        def at(i, place):
            return (0, first + (place[0] // 2 if shared else place[0]))

        return pl.BlockSpec((D, PAIR), at)

    return [column(6 * k, False) for k in range(3)] + [column(6 * k + 4, True) for k in range(3)]


def chunk_call(which, place, near, far, gain, shift, weight, cosine, sine):
    count = sum(part.size for part in near) // D
    whole = lambda part: pl.BlockSpec(part.shape, lambda i, place: (0,) * part.ndim)
    table = pl.BlockSpec((count, PAIR), lambda i, place: (place[2 + which], 0))
    return pl.pallas_call(
        lambda *refs: chunk_body(which, *refs),
        grid_spec=pltpu.PrefetchScalarGridSpec(
            num_scalar_prefetch=1,
            grid=(1,),
            in_specs=[whole(part) for part in (*near, *far)]
            + [VECTOR, VECTOR]
            + head_columns(0)
            + [table, table],
            out_specs=[const((count, D)), const((count, 3 * PAIR)), const((count, 2 * PAIR))],
            scratch_shapes=[pltpu.VMEM((count, D), BF16), pltpu.VMEM((D, 6 * PAIR), BF16)],
        ),
        out_shape=[
            jax.ShapeDtypeStruct((count, D), BF16),
            jax.ShapeDtypeStruct((count, 3 * PAIR), BF16),
            jax.ShapeDtypeStruct((count, 2 * PAIR), BF16),
        ],
        compiler_params=params(),
        name="qkv_chunk",
    )(place, *near, *far, gain, shift, *[weight] * 6, cosine, sine)


def unpack_half(packed, rows):
    peers = packed.shape[0]
    wide = packed.astype(F32).reshape(peers * rows // 2, PAIR)
    low = lanes(peers * rows // 2) < HD
    top = jnp.where(low, wide, 0.0).reshape(peers, rows // 2, PAIR)
    bottom = jnp.where(low, swap_heads(wide), 0.0).reshape(peers, rows // 2, PAIR)
    return jnp.concatenate([top, bottom], axis=1).reshape(peers * rows, PAIR).astype(BF16)


def pack_half(tile, rows):
    blocks = tile.shape[0] // rows
    cut = tile.reshape(blocks, rows, PAIR)
    top = cut[:, : rows // 2].reshape(blocks * rows // 2, PAIR)
    bottom = cut[:, rows // 2 :].reshape(blocks * rows // 2, PAIR)
    return (top + swap_heads(bottom)).reshape(blocks, rows // 2, PAIR)


def causal():
    key = lax.broadcasted_iota(jnp.int32, (BLK, BLK), 0)
    query = lax.broadcasted_iota(jnp.int32, (BLK, BLK), 1)
    return key <= query


def head_masks(tile_t):
    upper = lax.broadcasted_iota(jnp.int32, tile_t.shape, 0) < HD
    return jnp.where(upper, tile_t, 0.0).astype(BF16), jnp.where(upper, 0.0, tile_t).astype(BF16)


def softmax_sweep(i, heads, key_at, value_t_at):
    def visit(j, carry, masked):
        keys = key_at(j)
        values_t = value_t_at(j)
        out = []
        for (query_t, at), (top, total, acc) in zip(heads, carry):
            s = dot(keys, query_t)
            if masked:
                s = jnp.where(causal(), s, NEGATIVE)
            peak = jnp.maximum(top, jnp.max(s, axis=0, keepdims=True))
            p = jnp.exp2(s - peak)
            fade = jnp.exp2(top - peak)
            out.append(
                (
                    peak,
                    total * fade + jnp.sum(p, axis=0, keepdims=True),
                    acc * fade + dot(values_t[at : at + HD], p.astype(BF16)),
                )
            )
        return tuple(out)

    start = tuple(
        (
            jnp.full((1, BLK), NEGATIVE, F32),
            jnp.zeros((1, BLK), F32),
            jnp.zeros((HD, BLK), F32),
        )
        for _ in heads
    )
    carry = lax.fori_loop(0, i, lambda j, carry: visit(j, carry, False), start)
    carry = visit(i, carry, True)
    return [(acc / total, top + jnp.log2(total)) for top, total, acc in carry]


def pair_forward_body(place, *refs):
    chunks, (out, out_t, lse, whole, values_t) = refs[:GROUPS], refs[GROUPS:]
    i = pl.program_id(0)

    @pl.when(i == 0)
    def _():
        for which, chunk in enumerate(chunks):
            at = place[2 + which]
            whole[at] = chunk[...]
            values_t[at] = flip(chunk[:, 2 * PAIR :]).astype(BF16)

    low, high = head_masks(flip(whole[i, :, :PAIR]))
    heads = softmax_sweep(
        i,
        [(low, 0), (high, HD)],
        lambda j: whole[j, :, PAIR : 2 * PAIR],
        lambda j: values_t[j],
    )
    o_t = jnp.concatenate([heads[0][0], heads[1][0]], axis=0)
    out_t[...] = o_t
    lse[0, 0:1] = heads[0][1]
    lse[0, 1:2] = heads[1][1]
    out[...] = jnp.transpose(o_t).astype(BF16)


def pair_forward(place, chunks):
    return pl.pallas_call(
        pair_forward_body,
        grid_spec=pltpu.PrefetchScalarGridSpec(
            num_scalar_prefetch=1,
            grid=(GROUPS,),
            in_specs=[const((BLK, 3 * PAIR))] * GROUPS,
            out_specs=[
                pl.BlockSpec((BLK, PAIR), lambda i, place: (i, 0)),
                pl.BlockSpec((PAIR, BLK), lambda i, place: (0, i)),
                pl.BlockSpec((1, 8, BLK), lambda i, place: (i, 0, 0)),
                const((GROUPS, BLK, 3 * PAIR)),
            ],
            scratch_shapes=[pltpu.VMEM((GROUPS, PAIR, BLK), BF16)],
        ),
        out_shape=[
            jax.ShapeDtypeStruct((GROUPS * BLK, PAIR), BF16),
            jax.ShapeDtypeStruct((PAIR, GROUPS * BLK), F32),
            jax.ShapeDtypeStruct((GROUPS, 8, BLK), F32),
            jax.ShapeDtypeStruct((GROUPS, BLK, 3 * PAIR), BF16),
        ],
        compiler_params=params(),
        name="attend_pair",
    )(place, *chunks)


def single_forward_body(rows, place, *refs):
    chunks, (out, out_t, lse, whole, values_t) = refs[:GROUPS], refs[GROUPS:]
    i = pl.program_id(0)

    @pl.when(i == 0)
    def _():
        for which, chunk in enumerate(chunks):
            at = place[2 + which]
            whole[at] = chunk[...]
            values_t[at] = flip(chunk[:, :PAIR]).astype(BF16)

    query_t = flip(whole[i, :, PAIR:]).astype(BF16)
    ((o_t, total),) = softmax_sweep(
        i, [(query_t, HD)], lambda j: whole[j, :, :PAIR], lambda j: values_t[j]
    )
    out_t[...] = o_t
    lse[0, 0:1] = total
    tile = jnp.transpose(jnp.concatenate([o_t, jnp.zeros_like(o_t)], axis=0))
    out[...] = pack_half(tile, rows).astype(BF16)


def single_forward(place, chunks, rows):
    per = BLK // rows
    return pl.pallas_call(
        lambda *refs: single_forward_body(rows, *refs),
        grid_spec=pltpu.PrefetchScalarGridSpec(
            num_scalar_prefetch=1,
            grid=(GROUPS,),
            in_specs=[const((BLK, 2 * PAIR))] * GROUPS,
            out_specs=[
                pl.BlockSpec((per, rows // 2, PAIR), lambda i, place: (i, 0, 0)),
                pl.BlockSpec((HD, BLK), lambda i, place: (0, i)),
                pl.BlockSpec((1, 8, BLK), lambda i, place: (i, 0, 0)),
                const((GROUPS, BLK, 2 * PAIR)),
            ],
            scratch_shapes=[pltpu.VMEM((GROUPS, PAIR, BLK), BF16)],
        ),
        out_shape=[
            jax.ShapeDtypeStruct((GROUPS * per, rows // 2, PAIR), BF16),
            jax.ShapeDtypeStruct((HD, GROUPS * BLK), F32),
            jax.ShapeDtypeStruct((GROUPS, 8, BLK), F32),
            jax.ShapeDtypeStruct((GROUPS, BLK, 2 * PAIR), BF16),
        ],
        compiler_params=params(),
        name="attend_single",
    )(place, *chunks)


def unturn_t(part_t, cosine_t, sine_t):
    first, second = part_t[: HD // 2], part_t[HD // 2 :]
    return jnp.concatenate(
        [first * cosine_t + second * sine_t, second * cosine_t - first * sine_t], axis=0
    )


def grads_sweep(i, heads, key_at, value_at, key_t_at, add):
    def visit(j, carry, masked):
        keys, values, keys_t = key_at(j), value_at(j), key_t_at(j)
        ps, dss, out = [], [], []
        for (query_t, grad_t, lse, delta, at), dq in zip(heads, carry):
            p = jnp.exp2(dot(keys, query_t) - lse)
            if masked:
                p = jnp.where(causal(), p, 0.0)
            ds = (p * (dot(values, grad_t) - delta)).astype(BF16)
            ps.append(p.astype(BF16))
            dss.append(ds)
            out.append(dq + dot(keys_t[at : at + HD], ds))
        add(j, ps, dss)
        return tuple(out)

    start = tuple(jnp.zeros((HD, BLK), F32) for _ in heads)
    carry = lax.fori_loop(0, i, lambda j, carry: visit(j, carry, False), start)
    return visit(i, carry, True)


def pair_backward_body(
    rows, whole, grad, out_t, lse, cos_t, sin_t, cosine, sine, out, keys_t, dk, dv
):
    i = pl.program_id(0)
    blocks = whole.shape[0]
    per = BLK // rows

    @pl.when(i == 0)
    def _():
        for b in range(blocks):
            keys_t[b] = flip(whole[b, :, PAIR : 2 * PAIR]).astype(BF16)
        dk[...] = jnp.zeros_like(dk)
        dv[...] = jnp.zeros_like(dv)

    query = whole[i, :, :PAIR]
    do = grad[pl.ds(i * per, per), 0:rows].reshape(BLK, PAIR)
    q_low, q_high = head_masks(flip(query))
    do_t = flip(do)
    do_low, do_high = head_masks(do_t)
    product = do_t * out_t[...]
    low = lanes(BLK) < HD
    wide_q, wide_do = query.astype(F32), do.astype(F32)
    q_rows = jnp.concatenate(
        [jnp.where(low, wide_q, 0.0), jnp.where(low, 0.0, wide_q)], axis=0
    ).astype(BF16)
    do_rows = jnp.concatenate(
        [jnp.where(low, wide_do, 0.0), jnp.where(low, 0.0, wide_do)], axis=0
    ).astype(BF16)

    def add(j, ps, dss):
        dv[j] += dot(jnp.concatenate(ps, axis=1), do_rows)
        dk[j] += dot(jnp.concatenate(dss, axis=1), q_rows)

    heads = [
        (q_low, do_low, lse[0, 0:1], jnp.sum(product[:HD], axis=0, keepdims=True), 0),
        (q_high, do_high, lse[0, 1:2], jnp.sum(product[HD:], axis=0, keepdims=True), HD),
    ]
    dqs = grads_sweep(
        i,
        heads,
        lambda j: whole[j, :, PAIR : 2 * PAIR],
        lambda j: whole[j, :, 2 * PAIR :],
        lambda j: keys_t[j],
        add,
    )
    cos, sin = cos_t[...], sin_t[...]
    dq = jnp.concatenate([unturn_t(part * SCALE, cos, sin) for part in dqs], axis=0)
    out[pl.ds(i * per, per), 0:rows] = jnp.transpose(dq).reshape(per, rows, PAIR).astype(BF16)

    @pl.when(i == blocks - 1)
    def _():
        for b in range(blocks):
            at = pl.ds(b * BLK, BLK)
            back = turn(dk[b] * (1.0 / LOG2E), cosine[at], -sine[at])
            out[b * per : (b + 1) * per, rows : 2 * rows] = back.reshape(per, rows, PAIR).astype(BF16)
            out[b * per : (b + 1) * per, 2 * rows : 3 * rows] = (
                dv[b].reshape(per, rows, PAIR).astype(BF16)
            )


def pair_backward(whole, grad, out_t, lse, cos_t, sin_t, cosine, sine):
    peers, rows = grad.shape[0], grad.shape[1] * 2 // 3
    blocks = whole.shape[0]
    shape = (peers, 3 * rows, PAIR)
    return pl.pallas_call(
        lambda *refs: pair_backward_body(rows, *refs),
        grid=(blocks,),
        in_specs=[
            const(whole.shape),
            const(grad.shape),
            pl.BlockSpec((PAIR, BLK), lambda i: (0, i)),
            pl.BlockSpec((1, 8, BLK), lambda i: (i, 0, 0)),
            pl.BlockSpec((HD // 2, BLK), lambda i: (0, i)),
            pl.BlockSpec((HD // 2, BLK), lambda i: (0, i)),
            const(cosine.shape),
            const(sine.shape),
        ],
        out_specs=const(shape),
        out_shape=jax.ShapeDtypeStruct(shape, BF16),
        scratch_shapes=[
            pltpu.VMEM((blocks, PAIR, BLK), BF16),
            pltpu.VMEM((blocks, BLK, PAIR), F32),
            pltpu.VMEM((blocks, BLK, PAIR), F32),
        ],
        compiler_params=params(),
        name="attend_pair_grads",
    )(whole, grad, out_t, lse, cos_t, sin_t, cosine, sine)


def single_backward_body(
    rows, whole, grad, out_t, lse, cos_t, sin_t, cosine, sine, out, both_t, grads, dboth
):
    i = pl.program_id(0)
    blocks = whole.shape[0]
    per = BLK // rows
    half = rows // 2

    @pl.when(i == 0)
    def _():
        for b in range(blocks):
            both_t[b] = flip(whole[b, :, :PAIR]).astype(BF16)
        grads[...] = unpack_half(grad[:, rows:], rows).reshape(blocks, BLK, PAIR)
        dboth[...] = jnp.zeros_like(dboth)

    wide_q, wide_do = whole[i, :, PAIR:].astype(F32), grads[i].astype(F32)
    q_t = jnp.transpose(wide_q).astype(BF16)
    shifted = swap_heads(wide_do)
    do_t = jnp.transpose(shifted)
    delta = jnp.sum(do_t[HD:] * out_t[...], axis=0, keepdims=True)
    sides = jnp.concatenate([wide_q, shifted], axis=0).astype(BF16)

    def add(j, ps, dss):
        dboth[j] += dot(jnp.concatenate([dss[0], ps[0]], axis=1), sides)

    (dq,) = grads_sweep(
        i,
        [(q_t, do_t.astype(BF16), lse[0, 0:1], delta, 0)],
        lambda j: whole[j, :, :PAIR],
        lambda j: whole[j, :, :PAIR],
        lambda j: both_t[j],
        add,
    )
    dq = unturn_t(dq * SCALE, cos_t[...], sin_t[...])
    tile = jnp.transpose(jnp.concatenate([dq, jnp.zeros_like(dq)], axis=0))
    out[pl.ds(i * per, per), rows : rows + half] = pack_half(tile, rows).astype(BF16)

    @pl.when(i == blocks - 1)
    def _():
        low = lanes(BLK) < HD
        for b in range(blocks):
            at = pl.ds(b * BLK, BLK)
            part = dboth[b]
            back = turn(part * (1.0 / LOG2E), cosine[at], -sine[at])
            out[b * per : (b + 1) * per, 0:rows] = (
                jnp.where(low, back, part).reshape(per, rows, PAIR).astype(BF16)
            )


def single_backward(whole, grad, out_t, lse, cos_t, sin_t, cosine, sine):
    peers, rows = grad.shape[0], grad.shape[1] * 2 // 3
    blocks = whole.shape[0]
    shape = (peers, 3 * rows // 2, PAIR)
    return pl.pallas_call(
        lambda *refs: single_backward_body(rows, *refs),
        grid=(blocks,),
        in_specs=[
            const(whole.shape),
            const(grad.shape),
            pl.BlockSpec((HD, BLK), lambda i: (0, i)),
            pl.BlockSpec((1, 8, BLK), lambda i: (i, 0, 0)),
            pl.BlockSpec((HD // 2, BLK), lambda i: (0, i)),
            pl.BlockSpec((HD // 2, BLK), lambda i: (0, i)),
            const(cosine.shape),
            const(sine.shape),
        ],
        out_specs=const(shape),
        out_shape=jax.ShapeDtypeStruct(shape, BF16),
        scratch_shapes=[
            pltpu.VMEM((blocks, PAIR, BLK), BF16),
            pltpu.VMEM((blocks, BLK, PAIR), BF16),
            pltpu.VMEM((blocks, BLK, PAIR), F32),
        ],
        compiler_params=params(),
        name="attend_single_grads",
    )(whole, grad, out_t, lse, cos_t, sin_t, cosine, sine)


def third_tiles(parts):
    low = lanes(parts[0].shape[0]) < HD
    tiles = []
    for k in (0, 2):
        a, b = parts[k], parts[k + 1]
        top = jnp.where(low, a, swap_heads(b))
        bottom = jnp.where(low, swap_heads(a), b)
        tiles.append(jnp.concatenate([top, bottom], axis=0))
    return tiles


def third_parts(tiles):
    parts = []
    for tile in tiles:
        half = tile.shape[0] // 2
        top, bottom = tile[:half], tile[half:]
        low = lanes(half) < HD
        parts.append(jnp.where(low, top, swap_heads(bottom)))
        parts.append(jnp.where(low, swap_heads(top), bottom))
    return parts


def project_body(pair, single, tok, w_attn, gain, shift, w_query, o, r1, c, cq):
    tiles = [pair[g, 0].astype(F32) for g in range(GROUPS)]
    tiles += third_tiles([single[g, 0].astype(F32) for g in range(GROUPS)])
    heads = jnp.concatenate(tiles, axis=1).astype(BF16)
    o[0] = heads
    after = tok[0].astype(F32) + dot(heads, w_attn[...])
    r1[0] = after
    row = (norm_stats(after)[0] * gain[...][None] + shift[...][None]).astype(BF16)
    c[0] = row
    cq[0] = dot(row, w_query[...]).astype(BF16)


def project_call(pair, single, tokens, w_attn, gain, shift, w_query):
    seqs, rows, _ = tokens.shape
    block = pl.BlockSpec((1, rows, D), lambda s: (s, 0, 0))
    shape = lambda kind: jax.ShapeDtypeStruct((seqs, rows, D), kind)
    return pl.pallas_call(
        project_body,
        grid=(seqs,),
        in_specs=[
            pl.BlockSpec((GROUPS, 1, rows, PAIR), lambda s: (0, s, 0, 0)),
            pl.BlockSpec((GROUPS, 1, rows // 2, PAIR), lambda s: (0, s, 0, 0)),
            block,
            const((D, D)),
            VECTOR,
            VECTOR,
            const((D, D)),
        ],
        out_specs=[block] * 4,
        out_shape=[shape(BF16), shape(F32), shape(BF16), shape(BF16)],
        compiler_params=params(),
        name="project",
    )(
        pair.reshape(GROUPS, seqs, rows, PAIR),
        single.reshape(GROUPS, seqs, rows // 2, PAIR),
        tokens,
        w_attn,
        gain,
        shift,
        w_query,
    )


def memory_body(near, weight, out):
    out[...] = dot(near[...], weight[...]).astype(BF16)


def memory_call(near, weight):
    rows = near.shape[0]
    step = min(rows, 512)
    return pl.pallas_call(
        memory_body,
        grid=(rows // step,),
        in_specs=[pl.BlockSpec((step, D), lambda i: (i, 0)), const((D, 2 * D))],
        out_specs=pl.BlockSpec((step, 2 * D), lambda i: (i, 0)),
        out_shape=jax.ShapeDtypeStruct((rows, 2 * D), BF16),
        compiler_params=params(),
        name="memory",
    )(near, weight)


def move_later(values, before):
    first = lax.broadcasted_iota(jnp.int32, values.shape, 0) == 0
    return jnp.where(first, before.astype(F32), pltpu.roll(values.astype(F32), 1, 0))


def move_earlier(values, after):
    rows = values.shape[0]
    last = lax.broadcasted_iota(jnp.int32, values.shape, 0) == rows - 1
    return jnp.where(last, after.astype(F32), pltpu.roll(values.astype(F32), rows - 1, 0))


def head_rows(tile):
    low = lanes(GROUP) < HD
    return jnp.concatenate(
        [jnp.where(low, tile, 0.0), jnp.where(low, 0.0, tile)], axis=0
    ).astype(BF16)


def fold_rows(both):
    return jnp.where(lanes(GROUP) < HD, both[:GROUP], both[GROUP:])


def cross_scores(keys, query_rows, have):
    scores = dot_nt(keys, query_rows) * (SCALE * LOG2E)
    row = lax.broadcasted_iota(jnp.int32, scores.shape, 0)
    kept = jnp.where(row < RET, have[0], have[1]) > 0
    return jnp.where(kept, scores, NEGATIVE), kept


def row_heads(row):
    return jnp.where(diagonal(), row, 0.0).astype(BF16)


def diagonal():
    head = lax.broadcasted_iota(jnp.int32, (16, D), 1) // HD
    return head == lax.broadcasted_iota(jnp.int32, (16, D), 0)


def own_heads(wide):
    return jnp.sum(jnp.where(diagonal(), wide, 0.0), axis=0, keepdims=True)


def softmax_columns(scores, kept):
    peak = jnp.max(scores, axis=0, keepdims=True)
    weights = jnp.where(kept, jnp.exp2(scores - peak), 0.0)
    total = jnp.sum(weights, axis=0, keepdims=True)
    some = total > 0.0
    safe = jnp.where(some, total, 1.0)
    return weights / safe, jnp.where(some, peak + jnp.log2(safe), 0.0)


def cross_body(windows, present, present_next, cq, memory, memory_next, out, lse, shifted, win):
    s = pl.program_id(0)
    rows = cq.shape[1]
    zero = jnp.zeros((1, D), F32)
    wide = cq[0].astype(F32)
    shifted[...] = move_later(wide, zero).reshape(windows, GROUP, D)

    def window(w, _):
        have = [present[s, w, k] for k in range(NEIGH)]
        for p in range(HEADS // 2):
            at = pl.ds(p * PAIR, PAIR)
            keys = memory[0, w, :, p * PAIR : (p + 1) * PAIR]
            values = memory[0, w, :, D + p * PAIR : D + (p + 1) * PAIR]
            ca, logs = softmax_columns(*cross_scores(keys, head_rows(shifted[w, :, at]), have))
            win[w, :, at] = fold_rows(dot_tn(ca.astype(BF16), values))
            lse[0, w, p : p + 1] = logs
        return 0

    lax.fori_loop(0, windows, window, 0)
    have = [present_next[s, k] for k in range(NEIGH)]
    ca, _ = softmax_columns(
        *cross_scores(memory_next[0, :, :D], row_heads(wide[rows - 1 :]), have)
    )
    last = own_heads(dot_tn(ca.astype(BF16), memory_next[0, :, D:]))
    out[0] = move_earlier(win[...].reshape(rows, D), last).astype(BF16)


def cross_call(present, present_next, cq, memory, memory_next):
    seqs, windows = present.shape[:2]
    rows = cq.shape[1]
    keys = NEIGH * RET
    block = pl.BlockSpec((1, rows, D), lambda s: (s, 0, 0))
    return pl.pallas_call(
        lambda *refs: cross_body(windows, *refs),
        grid=(seqs,),
        in_specs=[
            pl.BlockSpec(memory_space=pltpu.SMEM),
            pl.BlockSpec(memory_space=pltpu.SMEM),
            block,
            pl.BlockSpec((1, windows, keys, 2 * D), lambda s: (s, 0, 0, 0)),
            pl.BlockSpec((1, keys, 2 * D), lambda s: (s, 0, 0)),
        ],
        out_specs=[block, pl.BlockSpec((1, windows, 8, PAIR), lambda s: (s, 0, 0, 0))],
        out_shape=[
            jax.ShapeDtypeStruct((seqs, rows, D), BF16),
            jax.ShapeDtypeStruct((seqs, windows, 8, PAIR), F32),
        ],
        scratch_shapes=[pltpu.VMEM((windows, GROUP, D), F32)] * 2,
        compiler_params=params(),
        name="cross",
    )(present, present_next, cq, memory, memory_next)


def gelu_parts(u):
    phi = 0.5 + 0.5 * lax.erf(u * math.sqrt(0.5))
    slope = phi + u * (jnp.exp2(u * u * (-0.5 * LOG2E)) * (1.0 / math.sqrt(2.0 * math.pi)))
    return u * phi, slope


def feed_body(
    steps,
    r1,
    cross_rows,
    cot,
    w_cross,
    gain,
    shift,
    w_up,
    w_down,
    output,
    d2,
    e2,
    dr,
    vectors,
    grads,
    normed,
    inverse,
    row,
    row_t,
    total,
    grad,
    up_stage,
    down_stage,
    sems,
):
    f = pl.program_id(0)
    seqs, rows = r1.shape[:2]
    batch, sq, groups, _, own, cols = grads.shape
    near = down_stage.shape[2]

    def copies(at):
        slot = lax.rem(at, 2)
        first = at * near
        return (
            pltpu.make_async_copy(up_stage.at[slot], grads.at[at, :, :, 0], sems.at[slot, 0]),
            pltpu.make_async_copy(
                down_stage.at[slot],
                grads.at[:, pl.ds(lax.rem(first, sq), near), first // sq, 1],
                sems.at[slot, 1],
            ),
        )

    @pl.when(f == 0)
    def _():
        for s in range(seqs):
            at = pl.ds(s * rows, rows)
            r2 = r1[s] + dot(cross_rows[s], w_cross[...])
            total[at] = r2
            n, inv = norm_stats(r2)
            normed[at] = n
            inverse[at] = inv
            a3 = (n * gain[...][None] + shift[...][None]).astype(BF16)
            row[at] = a3
            row_t[:, at] = flip(a3).astype(BF16)
        grad[...] = jnp.zeros_like(grad)

    up, down = w_up[...], w_down[...]
    given = cot[...]
    act, slope = gelu_parts(dot(row[...], up))
    act_low = act.astype(BF16)
    total[...] += dot(act_low, down)
    gu = (dot_nt(given, down) * slope).astype(BF16)
    grad[...] += dot_nt(gu, up)
    part = dot(row_t[...], gu).astype(BF16)
    part_down = dot(flip(act).astype(BF16), given).astype(BF16)

    @pl.when(f >= 2)
    def _():
        for copy in copies(f - 2):
            copy.wait()

    slot = lax.rem(f, 2)
    for g in range(groups):
        for q in range(sq):
            start = (g * sq + q) * own
            up_stage[slot, q, g] = part[start : start + own]
    deep = own * cols // D
    for q in range(near):
        for b in range(batch):
            start = (q * batch + b) * deep
            for x in range(D // cols):
                down_stage[slot, b, q, x * deep : (x + 1) * deep] = part_down[
                    start : start + deep, x * cols : (x + 1) * cols
                ]
    for copy in copies(f):
        copy.start()

    @pl.when(f == steps - 1)
    def _():
        output[...] = total[...].astype(BF16)
        n, back = normed[...], grad[...]
        vectors[0:1] = jnp.sum(n * back, axis=0, keepdims=True)
        vectors[1:2] = jnp.sum(back, axis=0, keepdims=True)
        summed = given.astype(F32) + norm_back(n, inverse[...], gain[...][None], back)
        d2[...] = summed
        low = summed.astype(BF16)
        e2[...] = low
        dr[...] = dot_nt(low, w_cross[...]).astype(BF16)
        for at in (steps - 2, steps - 1):
            for copy in copies(at):
                copy.wait()


def feed_call(r1, cross_rows, cot, w_cross, gain, shift, w_up, w_down, batch, peers):
    seqs, rows, _ = r1.shape
    count = seqs * rows
    sq = peers // GROUPS
    steps = batch
    cols = FF // steps
    own = D // peers
    near = peers // batch
    flat = jax.ShapeDtypeStruct((count, D), BF16)
    wide = jax.ShapeDtypeStruct((count, D), F32)
    return pl.pallas_call(
        lambda *refs: feed_body(steps, *refs),
        grid=(steps,),
        in_specs=[
            const((seqs, rows, D)),
            const((seqs, rows, D)),
            const((count, D)),
            const((D, D)),
            VECTOR,
            VECTOR,
            pl.BlockSpec((D, cols), lambda f: (0, f)),
            pl.BlockSpec((cols, D), lambda f: (f, 0)),
        ],
        out_specs=[const((count, D))] * 4
        + [const((8, D)), pl.BlockSpec(memory_space=pl.ANY)],
        out_shape=[
            flat,
            wide,
            flat,
            flat,
            jax.ShapeDtypeStruct((8, D), F32),
            jax.ShapeDtypeStruct((batch, sq, GROUPS, 2, own, cols), BF16),
        ],
        scratch_shapes=[
            pltpu.VMEM((count, D), F32),
            pltpu.VMEM((count, 1), F32),
            pltpu.VMEM((count, D), BF16),
            pltpu.VMEM((D, count), BF16),
            pltpu.VMEM((count, D), F32),
            pltpu.VMEM((count, D), F32),
            pltpu.VMEM((2, sq, GROUPS, own, cols), BF16),
            pltpu.VMEM((2, batch, near, own, cols), BF16),
            pltpu.SemaphoreType.DMA((2, 2)),
        ],
        compiler_params=params(),
        name="feed",
    )(r1, cross_rows, cot, w_cross, gain, shift, w_up, w_down)


def cross_back_body(
    windows, present, present_next, cq, dr, memory, memory_next, lse, dmem, dcq, shifted, dwin, dshifted
):
    s = pl.program_id(0)
    rows = cq.shape[1]
    zero = jnp.zeros((1, D), F32)
    wide, wide_dr = cq[0].astype(F32), dr[0].astype(F32)
    shifted[...] = move_later(wide, zero).reshape(windows, GROUP, D)
    dwin[...] = move_later(wide_dr, zero).reshape(windows, GROUP, D)

    def window(w, _):
        have = [present[s, w, k] for k in range(NEIGH)]
        for p in range(HEADS // 2):
            at = pl.ds(p * PAIR, PAIR)
            keys = memory[0, w, :, p * PAIR : (p + 1) * PAIR]
            values = memory[0, w, :, D + p * PAIR : D + (p + 1) * PAIR]
            query_rows = head_rows(shifted[w, :, at])
            grad_rows = head_rows(dwin[w, :, at])
            scores, kept = cross_scores(keys, query_rows, have)
            ca = jnp.where(kept, jnp.exp2(scores - lse[0, w, p : p + 1]), 0.0)
            dca = dot_nt(values, grad_rows)
            inner = jnp.sum(ca * dca, axis=0, keepdims=True)
            dcs = (ca * (dca - inner)).astype(BF16)
            dmem[0, w, :, at] = (dot(dcs, query_rows) * SCALE).astype(BF16)
            dmem[0, w, :, pl.ds(D + p * PAIR, PAIR)] = dot(ca.astype(BF16), grad_rows).astype(BF16)
            dshifted[w, :, at] = fold_rows(dot_tn(dcs, keys)) * SCALE
        return 0

    lax.fori_loop(0, windows, window, 0)
    have = [present_next[s, k] for k in range(NEIGH)]
    _, dcs, _ = row_grads(memory_next[0], wide[rows - 1 :], wide_dr[rows - 1 :], have)
    last = own_heads(dot_tn(dcs, memory_next[0, :, :D])) * SCALE
    dcq[0] = move_earlier(dshifted[...].reshape(rows, D), last).astype(BF16)


def row_grads(memory, row, grad, have):
    query_rows, grad_rows = row_heads(row), row_heads(grad)
    ca, _ = softmax_columns(*cross_scores(memory[:, :D], query_rows, have))
    dca = dot_nt(memory[:, D:], grad_rows)
    inner = jnp.sum(ca * dca, axis=0, keepdims=True)
    return ca.astype(BF16), (ca * (dca - inner)).astype(BF16), (query_rows, grad_rows)


def cross_back_call(present, present_next, cq, dr, memory, memory_next, lse):
    seqs, windows = present.shape[:2]
    rows = cq.shape[1]
    keys = NEIGH * RET
    block = pl.BlockSpec((1, rows, D), lambda s: (s, 0, 0))
    wide = pl.BlockSpec((1, windows, keys, 2 * D), lambda s: (s, 0, 0, 0))
    return pl.pallas_call(
        lambda *refs: cross_back_body(windows, *refs),
        grid=(seqs,),
        in_specs=[
            pl.BlockSpec(memory_space=pltpu.SMEM),
            pl.BlockSpec(memory_space=pltpu.SMEM),
            block,
            block,
            wide,
            pl.BlockSpec((1, keys, 2 * D), lambda s: (s, 0, 0)),
            pl.BlockSpec((1, windows, 8, PAIR), lambda s: (s, 0, 0, 0)),
        ],
        out_specs=[wide, block],
        out_shape=[
            jax.ShapeDtypeStruct((seqs, windows, keys, 2 * D), BF16),
            jax.ShapeDtypeStruct((seqs, rows, D), BF16),
        ],
        scratch_shapes=[pltpu.VMEM((windows, GROUP, D), F32)] * 3,
        compiler_params=params(),
        name="cross_grads",
    )(present, present_next, cq, dr, memory, memory_next, lse)


def project_back_body(dcq, r1, d2, w_query, gain, w_attn, do, d1, e1, vectors):
    s = pl.program_id(0)
    rows = r1.shape[1]
    back = dot_nt(dcq[0], w_query[...])
    normed, inverse = norm_stats(r1[0])

    @pl.when(s == 0)
    def _():
        vectors[...] = jnp.zeros_like(vectors)

    vectors[0:1] += jnp.sum(normed * back, axis=0, keepdims=True)
    vectors[1:2] += jnp.sum(back, axis=0, keepdims=True)
    summed = d2[0] + norm_back(normed, inverse, gain[...][None], back)
    d1[0] = summed
    low = summed.astype(BF16)
    e1[0] = low
    heads = dot_nt(low, w_attn[...])
    for g in range(GROUPS):
        do[g, 0, 0:rows] = heads[:, g * PAIR : (g + 1) * PAIR].astype(BF16)
    tiles = [heads[:, (GROUPS + k) * PAIR : (GROUPS + k + 1) * PAIR] for k in range(2)]
    for g, part in enumerate(third_parts(tiles)):
        do[g, 0, rows:] = part.astype(BF16)


def project_back_call(dcq, r1, d2, w_query, gain, w_attn):
    seqs, rows, _ = r1.shape
    block = pl.BlockSpec((1, rows, D), lambda s: (s, 0, 0))
    shape = lambda kind: jax.ShapeDtypeStruct((seqs, rows, D), kind)
    return pl.pallas_call(
        project_back_body,
        grid=(seqs,),
        in_specs=[
            block,
            block,
            block,
            const((D, D)),
            VECTOR,
            const((D, D)),
        ],
        out_specs=[
            pl.BlockSpec((GROUPS, 1, rows + rows // 2, PAIR), lambda s: (0, s, 0, 0)),
            block,
            block,
            const((8, D)),
        ],
        out_shape=[
            jax.ShapeDtypeStruct((GROUPS, seqs, rows + rows // 2, PAIR), BF16),
            shape(F32),
            shape(BF16),
            jax.ShapeDtypeStruct((8, D), F32),
        ],
        compiler_params=params(),
        name="project_grads",
    )(dcq, r1, d2, w_query, gain, w_attn)


def put_rows(place, outs, block, value):
    batch, groups, part, _ = outs[0].shape[:1] + outs[0].shape[-3:]
    sq = 2 if len(outs) == 2 else outs[0].shape[1]
    own = D // (sq * groups)
    value = value.astype(BF16)

    def store(q, slot):
        for g in range(groups):
            start, done = block * own, 0
            at = (g * sq + q) * own
            while done < own:
                b, x = divmod(start + done, part)
                count = min(part - x, own - done)
                slot(b, g, x, count, value[at + done : at + done + count])
                done += count

    for q in range(sq):
        if len(outs) == 1:

            def put(b, g, x, count, rows, q=q):
                outs[0][b, q, g, x : x + count] = rows

            store(q, put)
            continue
        for k, out in enumerate(outs):

            @pl.when(place[1] == q ^ k)
            def _(q=q, out=out):
                def put(b, g, x, count, rows):
                    out[b, g, x : x + count] = rows

                store(q, put)


def others_body(
    split,
    per_sequence,
    place,
    present,
    near,
    dmem,
    memory,
    before,
    w_memory,
    o,
    e1,
    vectors,
    c_far,
    dq_far,
    cross_far,
    e2_far,
    dnear,
    *refs,
):
    outs, (acc, grads, c, dq, cross_rows, e2, sems) = refs[:-7], refs[-7:]
    i = pl.program_id(0)
    copies = [
        pltpu.make_async_copy(source, target, sems.at[k])
        for k, (source, target) in enumerate(
            ((c_far, c), (dq_far, dq), (cross_far, cross_rows), (e2_far, e2))
        )
    ]

    @pl.when(i == 0)
    def _():
        for copy in copies:
            copy.start()
        acc[...] = jnp.zeros_like(acc)

    grads[...] = dmem[...].reshape(grads.shape)

    @pl.when(lax.rem(i, per_sequence) == 0)
    def _():
        keys = memory.shape[2]
        edge = edge_grads(
            memory[0, 0],
            before[0, 0:1].astype(F32),
            before[0, 1:2].astype(F32),
            [present[i // per_sequence, 0, k] for k in range(NEIGH)],
        )
        grads[0:keys] = (dmem[0, 0].astype(F32) + edge).astype(BF16)

    dnear[...] = dot_nt(grads[...], w_memory[...]).astype(BF16)
    acc[...] += dot_tn(near[...], grads[...])

    @pl.when(i == 0)
    def _():
        put_rows(place, outs, 0, dot_tn(o[...], e1[...]))

    @pl.when(i == pl.num_programs(0) - 1)
    def _():
        for copy in copies:
            copy.wait()
        put_rows(place, outs, 1, dot_tn(c[...], dq[...]))
        put_rows(place, outs, 2, dot_tn(cross_rows[...], e2[...]))
        put_rows(place, outs, 3, acc[:, :D])
        put_rows(place, outs, 4, acc[:, D:])
        batch, groups, size = outs[0].shape[0], outs[0].shape[-3], outs[0].shape[-2]
        sq = vectors.shape[0] // groups
        used = 5 * D // (sq * groups) - (batch - 1) * size
        for g in range(groups):
            if split:
                for k, out in enumerate(outs):
                    out[batch - 1, g, used:] = vectors[g * sq + (place[1] ^ k)]
            else:
                for q in range(sq):
                    outs[0][batch - 1, q, g, used:] = vectors[g * sq + q]


def edge_grads(memory, row, grad, have):
    ca, dcs, (query_rows, grad_rows) = row_grads(memory, row, grad, have)
    return jnp.concatenate([dot(dcs, query_rows) * SCALE, dot(ca, grad_rows)], axis=1)


def others_call(
    split,
    place,
    present,
    near,
    dmem,
    memory,
    before,
    w_memory,
    o,
    e1,
    c,
    dq,
    cross_rows,
    e2,
    vectors,
    batch,
    peers,
):
    seqs, windows, keys, _ = dmem.shape
    count = o.shape[0]
    size = min(2, windows)
    steps = windows // size
    own = D // peers
    part = (5 * own + vectors.shape[1]) // batch
    shapes = [(batch, peers // GROUPS, GROUPS, part, D)]
    if split:
        shapes = [(batch, GROUPS, part, D)] * 2
    smem = pl.BlockSpec(memory_space=pltpu.SMEM)
    far = pl.BlockSpec(memory_space=pl.ANY)
    block = pl.BlockSpec((size * keys, D), lambda i: (i, 0))
    return pl.pallas_call(
        lambda *refs: others_body(split, steps, *refs),
        grid=(seqs * steps,),
        in_specs=[
            smem,
            smem,
            block,
            pl.BlockSpec((1, size, keys, 2 * D), lambda i: (i // steps, lax.rem(i, steps), 0, 0)),
            pl.BlockSpec((1, 1, keys, 2 * D), lambda i: (i // steps, 0, 0, 0)),
            pl.BlockSpec((1, 2, D), lambda i: (i // steps, 0, 0)),
            const((D, 2 * D)),
            const((count, D)),
            const((count, D)),
            const(vectors.shape),
            far,
            far,
            far,
            far,
        ],
        out_specs=[block] + [const(shape) for shape in shapes],
        out_shape=[jax.ShapeDtypeStruct(near.shape, BF16)]
        + [jax.ShapeDtypeStruct(shape, BF16) for shape in shapes],
        scratch_shapes=[
            pltpu.VMEM((D, 2 * D), F32),
            pltpu.VMEM((size * keys, 2 * D), BF16),
        ]
        + [pltpu.VMEM((count, D), BF16)] * 4
        + [pltpu.SemaphoreType.DMA((4,))],
        compiler_params=params(),
        name="other_grads",
    )(
        place,
        present,
        near,
        dmem,
        memory,
        before,
        w_memory,
        o,
        e1,
        vectors,
        c,
        dq,
        cross_rows,
        e2,
    )


def last_body(pair, single, tok, d1, gain, w_qkv, out):
    rows = tok.shape[1]
    half = rows // 2
    low = lanes(rows) < HD
    boths = [single[g, 0, 0:rows].astype(F32) for g in range(GROUPS)]
    queries = third_tiles([single[g, 0, rows : rows + half].astype(F32) for g in range(GROUPS)])
    keys = [jnp.where(low, boths[k], swap_heads(boths[k + 1])) for k in (0, 2)]
    values = [jnp.where(low, swap_heads(boths[k]), boths[k + 1]) for k in (0, 2)]
    parts = []
    for at, third in ((0, queries), (rows, keys), (2 * rows, values)):
        parts += [pair[g, 0, at : at + rows] for g in range(GROUPS)]
        parts += [tile.astype(BF16) for tile in third]
    back = dot_nt(jnp.concatenate(parts, axis=1), w_qkv[...])
    normed, inverse = norm_stats(tok[0].astype(F32))
    out[0] = (d1[0] + norm_back(normed, inverse, gain[...][None], back)).astype(BF16)


def last_call(pair, single, tokens, d1, gain, w_qkv):
    seqs, rows, _ = tokens.shape
    block = pl.BlockSpec((1, rows, D), lambda s: (s, 0, 0))
    return pl.pallas_call(
        last_body,
        grid=(seqs,),
        in_specs=[
            pl.BlockSpec((GROUPS, 1, 3 * rows, PAIR), lambda s: (0, s, 0, 0)),
            pl.BlockSpec((GROUPS, 1, 3 * rows // 2, PAIR), lambda s: (0, s, 0, 0)),
            block,
            block,
            VECTOR,
            const((D, 3 * D)),
        ],
        out_specs=block,
        out_shape=jax.ShapeDtypeStruct((seqs, rows, D), BF16),
        compiler_params=params(),
        name="token_grads",
    )(
        pair.reshape(GROUPS, seqs, 3 * rows, PAIR),
        single.reshape(GROUPS, seqs, 3 * rows // 2, PAIR),
        tokens,
        d1,
        gain,
        w_qkv,
    )


def heads_body(place, *refs):
    pieces, (pair, single, gain, shift) = refs[:GROUPS], refs[GROUPS : GROUPS + 4]
    weights, (out, acc, sums, held) = refs[GROUPS + 4 : GROUPS + 10], refs[GROUPS + 10 :]
    i = pl.program_id(0)
    per, rows = pair.shape[0], pair.shape[1] // 3
    for k, piece in enumerate(pieces):

        @pl.when(i == k)
        def _(piece=piece):
            held[...] = piece[...]

    third = unpack_half(single[:, rows : rows + rows // 2], rows)
    grads = jnp.concatenate(
        [pair[:, k * rows : (k + 1) * rows].reshape(per * rows, PAIR) for k in range(3)]
        + [single[:, 0:rows].reshape(per * rows, PAIR), third],
        axis=1,
    )
    part = dot_tn(held[...], grads)
    total = jnp.sum(grads.astype(F32), axis=0, keepdims=True)

    @pl.when(i == 0)
    def _():
        acc[...] = part
        sums[0:1] = total

    @pl.when(i > 0)
    def _():
        acc[...] += part
        sums[0:1] += total

    @pl.when(i == pl.num_programs(0) - 1)
    def _():
        low = lanes(D) < HD
        odd = lax.rem(place[0], 2) == 1
        wide = [weight[...].astype(F32) for weight in weights]
        q3, k3, v3 = [jnp.where(odd, swap_heads(t), t) for t in wide[3:]]
        columns = wide[:3] + [jnp.where(low, k3, swap_heads(v3)), jnp.where(low, q3, 0.0)]
        columns = jnp.concatenate(columns, axis=1)
        whole, over = acc[...], sums[0:1]
        d_gain = jnp.sum(whole * columns, axis=1, keepdims=True)
        d_shift = jnp.sum(over * columns, axis=1, keepdims=True)
        lane = lax.broadcasted_iota(jnp.int32, whole.shape, 1)
        flipped = jnp.transpose(
            jnp.concatenate([gain[...][None], shift[...][None], jnp.zeros((6, D), F32)], axis=0)
        )
        value = whole * flipped[:, 0:1] + flipped[:, 1:2] * over
        at = 4 * PAIR + HD
        value = jnp.where(lane == at, d_gain, jnp.where(lane == at + 1, d_shift, value))
        high, low, sq, groups, own, _ = out.shape
        for g in range(groups):
            for q in range(sq):
                for b in range(high * low):
                    start = ((g * sq + q) * high * low + b) * own
                    out[b // low, b % low, q, g] = value[start : start + own].astype(BF16)


def heads_call(place, pieces, pair, single, gain, shift, weight, batch):
    peers, rows = pair.shape[0], pair.shape[1] // 3
    per = peers // GROUPS
    shape = (batch // 2, 2, per, GROUPS, D // peers // batch, 5 * PAIR)

    def chunk(i, place):
        return (place[2 + i], 0, 0)

    return pl.pallas_call(
        heads_body,
        grid_spec=pltpu.PrefetchScalarGridSpec(
            num_scalar_prefetch=1,
            grid=(GROUPS,),
            in_specs=[const((per * rows, D))] * GROUPS
            + [
                pl.BlockSpec((per, 3 * rows, PAIR), chunk),
                pl.BlockSpec((per, 3 * rows // 2, PAIR), chunk),
                VECTOR,
                VECTOR,
            ]
            + head_columns(0),
            out_specs=const(shape),
            scratch_shapes=[
                pltpu.VMEM((D, 5 * PAIR), F32),
                pltpu.VMEM((8, 5 * PAIR), F32),
                pltpu.VMEM((per * rows, D), BF16),
            ],
        ),
        out_shape=jax.ShapeDtypeStruct(shape, BF16),
        compiler_params=params(),
        name="qkv_grads",
    )(place, *pieces, pair, single, gain, shift, *[weight] * 6)


SEQ = ("hg", "sq")
BATCH = ("by", "bx")


def from_behind(value, by):
    peers = lax.axis_size(SEQ)
    pairs = [(i, i + by) for i in range(peers) if 0 <= i + by < peers]
    return lax.ppermute(value, SEQ, pairs)


def swap_all(value):
    return lax.all_to_all(value, SEQ, 0, 0, tiled=True)


def add_rows(value):
    flat = value.reshape((value.shape[0] * value.shape[1],) + value.shape[2:])
    own = lax.psum_scatter(flat, BATCH + ("sq",), scatter_dimension=0, tiled=True)
    return own.reshape(value.shape[2:])


def rotated(value, by):
    return lax.ppermute(value, "hg", [(i, (i + by) % GROUPS) for i in range(GROUPS)])


def add_groups(own):
    here = lax.axis_index("hg")
    total = lax.dynamic_index_in_dim(own, here, 0, keepdims=False).astype(F32)
    for k in range(1, GROUPS):
        part = lax.dynamic_index_in_dim(own, lax.rem(here + k, GROUPS), 0, keepdims=False)
        total += rotated(part, k).astype(F32)
    return total.astype(BF16)


def gather_groups(own):
    here = lax.axis_index("hg")
    pieces = [lax.dynamic_index_in_dim(own, here, 0, keepdims=False)]
    for k in range(1, GROUPS):
        part = lax.dynamic_index_in_dim(own, lax.rem(here + k, GROUPS), 0, keepdims=False)
        pieces.append(rotated(part, k))
    return in_order([pieces[(-j) % GROUPS] for j in range(GROUPS)], here, "shift")


def passed(value, by):
    pairs = [(i, i + by) for i in range(GROUPS) if 0 <= i + by < GROUPS]
    return lax.ppermute(value, "hg", pairs)


def in_order(pieces, here, how):
    count = len(pieces)
    out = []
    for j in range(count):
        value = pieces[j]
        for me in range(1, count):
            at = (j - me) % count if how == "shift" else j ^ me
            value = jnp.where(here == me, pieces[at], value)
        out.append(value)
    return out


def gather_batch(value):
    size = lax.axis_size(BATCH)
    pieces = [value] + [
        lax.ppermute(value, BATCH, [(i, i ^ k) for i in range(size)]) for k in range(1, size)
    ]
    return in_order(pieces, lax.axis_index(BATCH), "xor")


def halve(value, name, axis):
    if lax.axis_size(name) == 2:
        here = lax.axis_index(name)
        kept = lax.dynamic_index_in_dim(value, here, axis, keepdims=False)
        given = lax.dynamic_index_in_dim(value, 1 - here, axis, keepdims=False)
        got = lax.ppermute(given, name, [(0, 1), (1, 0)])
        return (kept.astype(F32) + got.astype(F32)).astype(BF16)
    parts = lax.all_to_all(value, name, axis, 0, tiled=False)
    return jnp.sum(parts.astype(F32), axis=0).astype(BF16)


def own_sequence(value):
    if lax.axis_size("sq") == 2:
        here = lax.axis_index("sq")
        kept = lax.dynamic_index_in_dim(value, here, 0, keepdims=False)
        given = lax.dynamic_index_in_dim(value, 1 - here, 0, keepdims=False)
        return [kept, lax.ppermute(given, "sq", [(0, 1), (1, 0)])]
    return [lax.all_to_all(value, "sq", 0, 0, tiled=True)]


def together(*values):
    return lax.optimization_barrier(values)


def shards(
    tokens,
    neighbours,
    present,
    qkv_weight,
    attn_weight,
    query_weight,
    memory_weight,
    cross_weight,
    up_weight,
    down_weight,
    attn_gain,
    attn_shift,
    cross_gain,
    cross_shift,
    mlp_gain,
    mlp_shift,
    cotangent,
):
    seqs, rows = tokens.shape[:2]
    count = seqs * rows
    peers = lax.axis_size(SEQ)
    batch = lax.axis_size(BATCH)
    easy = [lax.axis_size(name) for name in ("by", "bx", "sq")] == [2, 2, 2]
    group, core = lax.axis_index("hg"), lax.axis_index("sq")
    place = jnp.stack([group, core] + [chunk_of(which, group) for which in range(GROUPS)])
    place = place.astype(jnp.int32)
    cos_np, sin_np = rope_tables(peers * rows)
    cosine, sine = jnp.asarray(cos_np), jnp.asarray(sin_np)
    cos_t = jnp.asarray(np.ascontiguousarray(cos_np[:, : HD // 2].T))
    sin_t = jnp.asarray(np.ascontiguousarray(sin_np[:, HD // 2 : HD].T))

    windows = present.shape[1]
    keys = NEIGH * RET
    near = neighbours.reshape(-1, D)

    def chunk(which, first, second):
        return chunk_call(
            which, place, first, second, attn_gain, attn_shift, qkv_weight, cosine, sine
        )

    own = own_sequence(tokens)
    behind, ahead = [passed(part, 1) for part in own], [passed(part, -1) for part in own]
    chunks = [chunk(0, own, own)]
    chunks[0], behind[0], ahead[0] = together(chunks[0], behind[0], ahead[0])
    behind_two = [passed(part, 1) for part in behind]
    ahead_two = [passed(part, -1) for part in ahead]
    memory = memory_call(near, memory_weight)
    memory, behind_two[0], ahead_two[0] = together(memory, behind_two[0], ahead_two[0])
    chunks.append(chunk(1, ahead, behind))
    chunks[1], behind_two[-1], ahead_two[-1] = together(chunks[1], behind_two[-1], ahead_two[-1])
    behind_three = [passed(part, 1) for part in behind_two]
    ahead_three = [passed(part, -1) for part in ahead_two]
    chunks.append(chunk(2, ahead_two, behind_two))
    chunks[2], behind_three, ahead_three = together(chunks[2], behind_three, ahead_three)
    last = [jnp.where(group == GROUPS - 1, x, y) for x, y in zip(behind_three, behind)]
    chunks.append(chunk(3, ahead_three, last))
    memory = memory.reshape(seqs, windows, keys, 2 * D)
    near_next, chunks[3] = together(neighbours[:, 0].reshape(seqs * keys, D), chunks[3])
    near_next = from_behind(near_next, -1)
    present_next = from_behind(present[:, 0], -1)
    pieces = [chunk[0] for chunk in chunks]
    o_pair, o_pair_t, lse_pair, pairs = pair_forward(place, [chunk[1] for chunk in chunks])
    singles, o_pair, near_next = together([chunk[2] for chunk in chunks], o_pair, near_next)
    memory_next = memory_call(near_next, memory_weight).reshape(seqs, keys, 2 * D)
    o_pair = swap_all(o_pair.reshape(peers, rows, PAIR))
    o_single, o_single_t, lse_single, singles = single_forward(place, singles, rows)
    o_single, o_pair = together(o_single, o_pair)
    o_single = swap_all(o_single)
    o_single, memory_next = together(o_single, memory_next)
    o, r1, c, cq = project_call(
        o_pair, o_single, tokens, attn_weight, cross_gain, cross_shift, query_weight
    )
    cross_rows, lse = cross_call(present, present_next, cq, memory, memory_next)
    output, d2, e2, dr, mlp_vectors, feed = feed_call(
        r1,
        cross_rows,
        cotangent.reshape(count, D),
        cross_weight,
        mlp_gain,
        mlp_shift,
        up_weight,
        down_weight,
        batch,
        peers,
    )
    dr = dr.reshape(seqs, rows, D)
    before = from_behind(jnp.concatenate([cq[:, -1:], dr[:, -1:]], axis=1), 1)
    feed, before = together(feed, before)
    feed = add_rows(feed)
    dmem, dq = cross_back_call(present, present_next, cq, dr, memory, memory_next, lse)
    do, d1, e1, cross_vectors = project_back_call(
        dq, r1, d2.reshape(seqs, rows, D), query_weight, cross_gain, attn_weight
    )
    do = swap_all(do.reshape(peers, 3 * rows // 2, PAIR))
    own = D // peers
    vectors = jnp.concatenate([mlp_vectors[:2], cross_vectors[:2]], axis=0).astype(BF16)
    vectors = vectors.reshape(4, peers, own).transpose(1, 0, 2).reshape(peers, 1, 4 * own)
    vectors = jnp.pad(vectors, ((0, 0), (0, own // 3 - 1), (0, D - 4 * own)))
    dnear, *others = others_call(
        easy,
        place,
        present,
        near,
        dmem,
        memory,
        before,
        memory_weight,
        o.reshape(count, D),
        e1.reshape(count, D),
        c.reshape(count, D),
        dq.reshape(count, D),
        cross_rows.reshape(count, D),
        e2,
        vectors,
        batch,
        peers,
    )
    do, others = together(do, others)
    if easy:
        kept, given = others
        got = lax.ppermute(given, "sq", [(0, 1), (1, 0)])
    else:
        others = add_rows(others[0])
    d_single = single_backward(singles, do, o_single_t, lse_single, cos_t, sin_t, cosine, sine)
    do, d_single, feed = together(do, d_single, feed)
    d_single_all = swap_all(d_single)
    feed = lax.psum_scatter(feed, "hg", scatter_dimension=0, tiled=False)
    d_pair = pair_backward(pairs, do, o_pair_t, lse_pair, cos_t, sin_t, cosine, sine)
    d_pair_all, d_single_all = together(d_pair, d_single_all)
    d_pair_all = swap_all(d_pair_all)
    if easy:
        d_pair, kept, got = together(d_pair, kept, got)
        others = (kept.astype(F32) + got.astype(F32)).astype(BF16)
        others = others.reshape((2, 2) + others.shape[1:])
        cut = GROUPS // 2
        others = [halve(others[:, :, :cut], "bx", 1), halve(others[:, :, cut:], "by", 0)]
    g_qkv = heads_call(place, pieces, d_pair, d_single, attn_gain, attn_shift, qkv_weight, batch)
    g_qkv, others, feed = together(g_qkv, others, feed)
    g_qkv = add_rows(g_qkv.reshape((batch,) + g_qkv.shape[2:]))
    feed = gather_batch(feed)
    if easy:
        others = [halve(others[0], "by", 0), halve(others[1], "bx", 0)]
        others = jnp.concatenate(others, axis=0)
    others = add_groups(others)
    grad_tokens = last_call(d_pair_all, d_single_all, tokens, d1, attn_gain, qkv_weight)
    g_qkv, others, grad_tokens, feed = together(g_qkv, others, grad_tokens, feed)
    g_qkv = jnp.stack(gather_groups(g_qkv))
    others = gather_batch(others)
    g_qkv = jnp.stack(gather_batch(g_qkv))

    others = jnp.concatenate(others, axis=0).astype(F32)
    kinds = [others[k * own : (k + 1) * own] for k in range(5)]
    others = others[5 * own, : 4 * own].reshape(4, own)
    g_up = jnp.concatenate([part[0] for part in feed], axis=1).astype(F32)
    deep = FF // peers // batch
    g_down = jnp.stack([part[1] for part in feed]).reshape(batch, D * batch // FF, deep, FF // batch)
    g_down = g_down.transpose(0, 2, 1, 3).reshape(FF // peers, D).astype(F32)
    g_qkv = g_qkv.transpose(0, 2, 1, 3).reshape(own, GROUPS, 5 * PAIR).astype(F32)

    def mine(start, width):
        return g_qkv[:, :, start : start + width].reshape(own, GROUPS * width)

    third = 3 * PAIR
    grad_qkv = jnp.concatenate(
        [
            mine(0, PAIR),
            mine(4 * PAIR, HD),
            mine(PAIR, PAIR),
            mine(third, HD),
            mine(2 * PAIR, PAIR),
            mine(third + HD, HD),
        ],
        axis=1,
    )
    vectors = jnp.sum(g_qkv[:, :, 4 * PAIR + HD : 4 * PAIR + HD + 2], axis=1)
    return (
        output.reshape(seqs, rows, D),
        grad_tokens,
        dnear.reshape(neighbours.shape),
        grad_qkv,
        kinds[0],
        kinds[1],
        jnp.concatenate(kinds[3:], axis=1),
        kinds[2],
        g_up,
        g_down,
        vectors[:, 0],
        vectors[:, 1],
        others[2],
        others[3],
        others[0],
        others[1],
    )


def solution(mesh):
    batch, seq = mesh.shape["batch"], mesh.shape["seq"]
    fine = Mesh(
        mesh.devices.reshape(batch // 2, 2, GROUPS, seq // GROUPS), ("by", "bx", "hg", "sq")
    )
    rows = P(BATCH, SEQ, None)
    windows = P(BATCH, SEQ, None, None, None)
    return jax.shard_map(
        shards,
        mesh=fine,
        in_specs=(rows, windows, rows) + (P(),) * 13 + (rows,),
        out_specs=(rows, rows, windows) + (P(SEQ, None),) * 7 + (P(SEQ),) * 6,
        check_vma=False,
    )
```

```python
import math

import jax
import jax.numpy as jnp
import numpy as np
from jax import lax
from jax.experimental import pallas as pl
from jax.experimental.pallas import tpu as pltpu
from jax.sharding import Mesh
from jax.sharding import PartitionSpec as P

D = 768
HEADS = 12
HD = 64
FF = 3072
GROUP = 64
NEIGH = 2
RET = 128
PAIR = 128
BLK = 512
GROUPS = 4

EPSILON = 1e-05
NEGATIVE = -1e30
SCALE = 1.0 / math.sqrt(HD)
LOG2E = math.log2(math.e)
VMEM_LIMIT = 56 * 1024 * 1024

F32 = jnp.float32
BF16 = jnp.bfloat16


def params(limit=VMEM_LIMIT):
    return pltpu.CompilerParams(vmem_limit_bytes=limit)


def dot(left, right):
    return jnp.dot(left, right, preferred_element_type=F32)


def dot_nt(left, right):
    return lax.dot_general(left, right, (((1,), (1,)), ((), ())), preferred_element_type=F32)


def dot_tn(left, right):
    return lax.dot_general(left, right, (((0,), (0,)), ((), ())), preferred_element_type=F32)


def flip(value):
    return jnp.transpose(value.astype(F32))


def rope_tables(length):
    half = HD // 2
    frequency = np.float32(10000.0) ** (-np.arange(half, dtype=np.float32) * np.float32(2.0) / np.float32(HD))
    angles = np.arange(length, dtype=np.float32)[:, None] * frequency[None, :].astype(np.float32)
    cosine, sine = np.cos(angles).astype(np.float32), np.sin(angles).astype(np.float32)
    return (
        np.concatenate([cosine] * 4, axis=1),
        np.concatenate([-sine, sine] * 2, axis=1),
    )


def lanes(rows):
    return lax.broadcasted_iota(jnp.int32, (rows, PAIR), 1)


def turn(tile, cosine, sine):
    rows = tile.shape[0]
    first = (lanes(rows) % HD) < HD // 2
    swapped = jnp.where(first, pltpu.roll(tile, PAIR - HD // 2, 1), pltpu.roll(tile, HD // 2, 1))
    return tile * cosine + swapped * sine


def swap_heads(tile):
    return pltpu.roll(tile, HD, 1)


def norm_stats(values):
    mean = jnp.mean(values, axis=-1, keepdims=True)
    centred = values - mean
    inverse = lax.rsqrt(jnp.mean(centred * centred, axis=-1, keepdims=True) + EPSILON)
    return centred * inverse, inverse


def norm_back(normed, inverse, gain, grad):
    scaled = grad * gain
    return inverse * (
        scaled
        - jnp.mean(scaled, axis=-1, keepdims=True)
        - normed * jnp.mean(scaled * normed, axis=-1, keepdims=True)
    )


VECTOR = pl.BlockSpec((D,), lambda *ids: (0,))


def const(shape):
    rank = len(shape)
    return pl.BlockSpec(shape, lambda *ids: (0,) * rank)


def chunk_body(which, place, *refs):
    halves = (len(refs) - 15) // 2
    near, far, refs = refs[:halves], refs[halves : 2 * halves], refs[2 * halves :]
    gain, shift = refs[:2]
    weights, (cosine, sine, normed, pair, single, tokens, columns) = refs[2:8], refs[8:]
    rows = tokens.shape[0] // halves
    first = use_first(which, place[0])
    for parts, wanted in ((near, first), (far, jnp.logical_not(first))):

        @pl.when(wanted)
        def _(parts=parts):
            for k, part in enumerate(parts):
                at = place[1] * (1 - 2 * k) + k if halves > 1 else 0
                tokens[pl.ds(at * rows, rows)] = part[...].reshape(rows, D)

    odd = lax.rem(place[0], 2) == 1
    for k, weight in enumerate(weights):
        columns[:, k * PAIR : (k + 1) * PAIR] = weight[...]
    n, _ = norm_stats(tokens[...].astype(F32))
    normed[...] = n.astype(BF16)
    out = dot((n * gain[...][None] + shift[...][None]).astype(BF16), columns[...])
    cos, sin = cosine[...], sine[...]
    q01, k01, v01, q2, k2, v2 = [out[:, k * PAIR : (k + 1) * PAIR] for k in range(6)]
    low = lanes(tokens.shape[0]) < HD
    q2, k2, v2 = [jnp.where(odd, swap_heads(t), t) for t in (q2, k2, v2)]
    pair[:, :PAIR] = (turn(q01, cos, sin) * (SCALE * LOG2E)).astype(BF16)
    pair[:, PAIR : 2 * PAIR] = turn(k01, cos, sin).astype(BF16)
    pair[:, 2 * PAIR :] = v01.astype(BF16)
    single[:, :PAIR] = jnp.where(low, turn(k2, cos, sin), swap_heads(v2)).astype(BF16)
    single[:, PAIR:] = jnp.where(low, turn(q2, cos, sin) * (SCALE * LOG2E), 0.0).astype(BF16)


def use_first(which, group):
    if which == 0:
        return group >= 0
    if which == 1:
        return group < GROUPS - 1
    if which == 2:
        return group < 2
    return group == 0


def chunk_of(which, group):
    if which == 0:
        return group
    if which == 1:
        return jnp.where(group < GROUPS - 1, group + 1, group - 1)
    if which == 2:
        return lax.rem(group + 2, GROUPS)
    return jnp.where(group == 0, GROUPS - 1, jnp.where(group == GROUPS - 1, 0, group - 1))


def head_columns(index):
    def column(first, shared):
        def at(i, place):
            return (0, first + (place[0] // 2 if shared else place[0]))

        return pl.BlockSpec((D, PAIR), at)

    return [column(6 * k, False) for k in range(3)] + [column(6 * k + 4, True) for k in range(3)]


def chunk_call(which, place, near, far, gain, shift, weight, cosine, sine):
    count = sum(part.size for part in near) // D
    whole = lambda part: pl.BlockSpec(part.shape, lambda i, place: (0,) * part.ndim)
    table = pl.BlockSpec((count, PAIR), lambda i, place: (place[2 + which], 0))
    return pl.pallas_call(
        lambda *refs: chunk_body(which, *refs),
        grid_spec=pltpu.PrefetchScalarGridSpec(
            num_scalar_prefetch=1,
            grid=(1,),
            in_specs=[whole(part) for part in (*near, *far)]
            + [VECTOR, VECTOR]
            + head_columns(0)
            + [table, table],
            out_specs=[const((count, D)), const((count, 3 * PAIR)), const((count, 2 * PAIR))],
            scratch_shapes=[pltpu.VMEM((count, D), BF16), pltpu.VMEM((D, 6 * PAIR), BF16)],
        ),
        out_shape=[
            jax.ShapeDtypeStruct((count, D), BF16),
            jax.ShapeDtypeStruct((count, 3 * PAIR), BF16),
            jax.ShapeDtypeStruct((count, 2 * PAIR), BF16),
        ],
        compiler_params=params(),
        name="qkv_chunk",
    )(place, *near, *far, gain, shift, *[weight] * 6, cosine, sine)


def unpack_half(packed, rows):
    peers = packed.shape[0]
    wide = packed.astype(F32).reshape(peers * rows // 2, PAIR)
    low = lanes(peers * rows // 2) < HD
    top = jnp.where(low, wide, 0.0).reshape(peers, rows // 2, PAIR)
    bottom = jnp.where(low, swap_heads(wide), 0.0).reshape(peers, rows // 2, PAIR)
    return jnp.concatenate([top, bottom], axis=1).reshape(peers * rows, PAIR).astype(BF16)


def pack_half(tile, rows):
    blocks = tile.shape[0] // rows
    cut = tile.reshape(blocks, rows, PAIR)
    top = cut[:, : rows // 2].reshape(blocks * rows // 2, PAIR)
    bottom = cut[:, rows // 2 :].reshape(blocks * rows // 2, PAIR)
    return (top + swap_heads(bottom)).reshape(blocks, rows // 2, PAIR)


def causal():
    key = lax.broadcasted_iota(jnp.int32, (BLK, BLK), 0)
    query = lax.broadcasted_iota(jnp.int32, (BLK, BLK), 1)
    return key <= query


def head_masks(tile_t):
    upper = lax.broadcasted_iota(jnp.int32, tile_t.shape, 0) < HD
    return jnp.where(upper, tile_t, 0.0).astype(BF16), jnp.where(upper, 0.0, tile_t).astype(BF16)


def softmax_sweep(i, heads, key_at, value_t_at):
    def visit(j, carry, masked):
        keys = key_at(j)
        values_t = value_t_at(j)
        out = []
        for (query_t, at), (top, total, acc) in zip(heads, carry):
            s = dot(keys, query_t)
            if masked:
                s = jnp.where(causal(), s, NEGATIVE)
            peak = jnp.maximum(top, jnp.max(s, axis=0, keepdims=True))
            p = jnp.exp2(s - peak)
            fade = jnp.exp2(top - peak)
            out.append(
                (
                    peak,
                    total * fade + jnp.sum(p, axis=0, keepdims=True),
                    acc * fade + dot(values_t[at : at + HD], p.astype(BF16)),
                )
            )
        return tuple(out)

    start = tuple(
        (
            jnp.full((1, BLK), NEGATIVE, F32),
            jnp.zeros((1, BLK), F32),
            jnp.zeros((HD, BLK), F32),
        )
        for _ in heads
    )
    carry = lax.fori_loop(0, i, lambda j, carry: visit(j, carry, False), start)
    carry = visit(i, carry, True)
    return [(acc / total, top + jnp.log2(total)) for top, total, acc in carry]


def pair_forward_body(place, *refs):
    chunks, (out, out_t, lse, whole, values_t) = refs[:GROUPS], refs[GROUPS:]
    i = pl.program_id(0)

    @pl.when(i == 0)
    def _():
        for which, chunk in enumerate(chunks):
            at = place[2 + which]
            whole[at] = chunk[...]
            values_t[at] = flip(chunk[:, 2 * PAIR :]).astype(BF16)

    low, high = head_masks(flip(whole[i, :, :PAIR]))
    heads = softmax_sweep(
        i,
        [(low, 0), (high, HD)],
        lambda j: whole[j, :, PAIR : 2 * PAIR],
        lambda j: values_t[j],
    )
    o_t = jnp.concatenate([heads[0][0], heads[1][0]], axis=0)
    out_t[...] = o_t
    lse[0, 0:1] = heads[0][1]
    lse[0, 1:2] = heads[1][1]
    out[...] = jnp.transpose(o_t).astype(BF16)


def pair_forward(place, chunks):
    return pl.pallas_call(
        pair_forward_body,
        grid_spec=pltpu.PrefetchScalarGridSpec(
            num_scalar_prefetch=1,
            grid=(GROUPS,),
            in_specs=[const((BLK, 3 * PAIR))] * GROUPS,
            out_specs=[
                pl.BlockSpec((BLK, PAIR), lambda i, place: (i, 0)),
                pl.BlockSpec((PAIR, BLK), lambda i, place: (0, i)),
                pl.BlockSpec((1, 8, BLK), lambda i, place: (i, 0, 0)),
                const((GROUPS, BLK, 3 * PAIR)),
            ],
            scratch_shapes=[pltpu.VMEM((GROUPS, PAIR, BLK), BF16)],
        ),
        out_shape=[
            jax.ShapeDtypeStruct((GROUPS * BLK, PAIR), BF16),
            jax.ShapeDtypeStruct((PAIR, GROUPS * BLK), F32),
            jax.ShapeDtypeStruct((GROUPS, 8, BLK), F32),
            jax.ShapeDtypeStruct((GROUPS, BLK, 3 * PAIR), BF16),
        ],
        compiler_params=params(),
        name="attend_pair",
    )(place, *chunks)


def single_forward_body(rows, place, *refs):
    chunks, (out, out_t, lse, whole, values_t) = refs[:GROUPS], refs[GROUPS:]
    i = pl.program_id(0)

    @pl.when(i == 0)
    def _():
        for which, chunk in enumerate(chunks):
            at = place[2 + which]
            whole[at] = chunk[...]
            values_t[at] = flip(chunk[:, :PAIR]).astype(BF16)

    query_t = flip(whole[i, :, PAIR:]).astype(BF16)
    ((o_t, total),) = softmax_sweep(
        i, [(query_t, HD)], lambda j: whole[j, :, :PAIR], lambda j: values_t[j]
    )
    out_t[...] = o_t
    lse[0, 0:1] = total
    tile = jnp.transpose(jnp.concatenate([o_t, jnp.zeros_like(o_t)], axis=0))
    out[...] = pack_half(tile, rows).astype(BF16)


def single_forward(place, chunks, rows):
    per = BLK // rows
    return pl.pallas_call(
        lambda *refs: single_forward_body(rows, *refs),
        grid_spec=pltpu.PrefetchScalarGridSpec(
            num_scalar_prefetch=1,
            grid=(GROUPS,),
            in_specs=[const((BLK, 2 * PAIR))] * GROUPS,
            out_specs=[
                pl.BlockSpec((per, rows // 2, PAIR), lambda i, place: (i, 0, 0)),
                pl.BlockSpec((HD, BLK), lambda i, place: (0, i)),
                pl.BlockSpec((1, 8, BLK), lambda i, place: (i, 0, 0)),
                const((GROUPS, BLK, 2 * PAIR)),
            ],
            scratch_shapes=[pltpu.VMEM((GROUPS, PAIR, BLK), BF16)],
        ),
        out_shape=[
            jax.ShapeDtypeStruct((GROUPS * per, rows // 2, PAIR), BF16),
            jax.ShapeDtypeStruct((HD, GROUPS * BLK), F32),
            jax.ShapeDtypeStruct((GROUPS, 8, BLK), F32),
            jax.ShapeDtypeStruct((GROUPS, BLK, 2 * PAIR), BF16),
        ],
        compiler_params=params(),
        name="attend_single",
    )(place, *chunks)


def unturn_t(part_t, cosine_t, sine_t):
    first, second = part_t[: HD // 2], part_t[HD // 2 :]
    return jnp.concatenate(
        [first * cosine_t + second * sine_t, second * cosine_t - first * sine_t], axis=0
    )


def grads_sweep(i, heads, key_at, value_at, key_t_at, add):
    def visit(j, carry, masked):
        keys, values, keys_t = key_at(j), value_at(j), key_t_at(j)
        ps, dss, out = [], [], []
        for (query_t, grad_t, lse, delta, at), dq in zip(heads, carry):
            p = jnp.exp2(dot(keys, query_t) - lse)
            if masked:
                p = jnp.where(causal(), p, 0.0)
            ds = (p * (dot(values, grad_t) - delta)).astype(BF16)
            ps.append(p.astype(BF16))
            dss.append(ds)
            out.append(dq + dot(keys_t[at : at + HD], ds))
        add(j, ps, dss)
        return tuple(out)

    start = tuple(jnp.zeros((HD, BLK), F32) for _ in heads)
    carry = lax.fori_loop(0, i, lambda j, carry: visit(j, carry, False), start)
    return visit(i, carry, True)


def pair_backward_body(
    rows, whole, grad, out_t, lse, cos_t, sin_t, cosine, sine, out, keys_t, dk, dv
):
    i = pl.program_id(0)
    blocks = whole.shape[0]
    per = BLK // rows

    @pl.when(i == 0)
    def _():
        for b in range(blocks):
            keys_t[b] = flip(whole[b, :, PAIR : 2 * PAIR]).astype(BF16)
        dk[...] = jnp.zeros_like(dk)
        dv[...] = jnp.zeros_like(dv)

    query = whole[i, :, :PAIR]
    do = grad[pl.ds(i * per, per), 0:rows].reshape(BLK, PAIR)
    q_low, q_high = head_masks(flip(query))
    do_t = flip(do)
    do_low, do_high = head_masks(do_t)
    product = do_t * out_t[...]
    low = lanes(BLK) < HD
    wide_q, wide_do = query.astype(F32), do.astype(F32)
    q_rows = jnp.concatenate(
        [jnp.where(low, wide_q, 0.0), jnp.where(low, 0.0, wide_q)], axis=0
    ).astype(BF16)
    do_rows = jnp.concatenate(
        [jnp.where(low, wide_do, 0.0), jnp.where(low, 0.0, wide_do)], axis=0
    ).astype(BF16)

    def add(j, ps, dss):
        dv[j] += dot(jnp.concatenate(ps, axis=1), do_rows)
        dk[j] += dot(jnp.concatenate(dss, axis=1), q_rows)

    heads = [
        (q_low, do_low, lse[0, 0:1], jnp.sum(product[:HD], axis=0, keepdims=True), 0),
        (q_high, do_high, lse[0, 1:2], jnp.sum(product[HD:], axis=0, keepdims=True), HD),
    ]
    dqs = grads_sweep(
        i,
        heads,
        lambda j: whole[j, :, PAIR : 2 * PAIR],
        lambda j: whole[j, :, 2 * PAIR :],
        lambda j: keys_t[j],
        add,
    )
    cos, sin = cos_t[...], sin_t[...]
    dq = jnp.concatenate([unturn_t(part * SCALE, cos, sin) for part in dqs], axis=0)
    out[pl.ds(i * per, per), 0:rows] = jnp.transpose(dq).reshape(per, rows, PAIR).astype(BF16)

    @pl.when(i == blocks - 1)
    def _():
        for b in range(blocks):
            at = pl.ds(b * BLK, BLK)
            back = turn(dk[b] * (1.0 / LOG2E), cosine[at], -sine[at])
            out[b * per : (b + 1) * per, rows : 2 * rows] = back.reshape(per, rows, PAIR).astype(BF16)
            out[b * per : (b + 1) * per, 2 * rows : 3 * rows] = (
                dv[b].reshape(per, rows, PAIR).astype(BF16)
            )


def pair_backward(whole, grad, out_t, lse, cos_t, sin_t, cosine, sine):
    peers, rows = grad.shape[0], grad.shape[1] * 2 // 3
    blocks = whole.shape[0]
    shape = (peers, 3 * rows, PAIR)
    return pl.pallas_call(
        lambda *refs: pair_backward_body(rows, *refs),
        grid=(blocks,),
        in_specs=[
            const(whole.shape),
            const(grad.shape),
            pl.BlockSpec((PAIR, BLK), lambda i: (0, i)),
            pl.BlockSpec((1, 8, BLK), lambda i: (i, 0, 0)),
            pl.BlockSpec((HD // 2, BLK), lambda i: (0, i)),
            pl.BlockSpec((HD // 2, BLK), lambda i: (0, i)),
            const(cosine.shape),
            const(sine.shape),
        ],
        out_specs=const(shape),
        out_shape=jax.ShapeDtypeStruct(shape, BF16),
        scratch_shapes=[
            pltpu.VMEM((blocks, PAIR, BLK), BF16),
            pltpu.VMEM((blocks, BLK, PAIR), F32),
            pltpu.VMEM((blocks, BLK, PAIR), F32),
        ],
        compiler_params=params(),
        name="attend_pair_grads",
    )(whole, grad, out_t, lse, cos_t, sin_t, cosine, sine)


def single_backward_body(
    rows, whole, grad, out_t, lse, cos_t, sin_t, cosine, sine, out, both_t, grads, dboth
):
    i = pl.program_id(0)
    blocks = whole.shape[0]
    per = BLK // rows
    half = rows // 2

    @pl.when(i == 0)
    def _():
        for b in range(blocks):
            both_t[b] = flip(whole[b, :, :PAIR]).astype(BF16)
        grads[...] = unpack_half(grad[:, rows:], rows).reshape(blocks, BLK, PAIR)
        dboth[...] = jnp.zeros_like(dboth)

    wide_q, wide_do = whole[i, :, PAIR:].astype(F32), grads[i].astype(F32)
    q_t = jnp.transpose(wide_q).astype(BF16)
    shifted = swap_heads(wide_do)
    do_t = jnp.transpose(shifted)
    delta = jnp.sum(do_t[HD:] * out_t[...], axis=0, keepdims=True)
    sides = jnp.concatenate([wide_q, shifted], axis=0).astype(BF16)

    def add(j, ps, dss):
        dboth[j] += dot(jnp.concatenate([dss[0], ps[0]], axis=1), sides)

    (dq,) = grads_sweep(
        i,
        [(q_t, do_t.astype(BF16), lse[0, 0:1], delta, 0)],
        lambda j: whole[j, :, :PAIR],
        lambda j: whole[j, :, :PAIR],
        lambda j: both_t[j],
        add,
    )
    dq = unturn_t(dq * SCALE, cos_t[...], sin_t[...])
    tile = jnp.transpose(jnp.concatenate([dq, jnp.zeros_like(dq)], axis=0))
    out[pl.ds(i * per, per), rows : rows + half] = pack_half(tile, rows).astype(BF16)

    @pl.when(i == blocks - 1)
    def _():
        low = lanes(BLK) < HD
        for b in range(blocks):
            at = pl.ds(b * BLK, BLK)
            part = dboth[b]
            back = turn(part * (1.0 / LOG2E), cosine[at], -sine[at])
            out[b * per : (b + 1) * per, 0:rows] = (
                jnp.where(low, back, part).reshape(per, rows, PAIR).astype(BF16)
            )


def single_backward(whole, grad, out_t, lse, cos_t, sin_t, cosine, sine):
    peers, rows = grad.shape[0], grad.shape[1] * 2 // 3
    blocks = whole.shape[0]
    shape = (peers, 3 * rows // 2, PAIR)
    return pl.pallas_call(
        lambda *refs: single_backward_body(rows, *refs),
        grid=(blocks,),
        in_specs=[
            const(whole.shape),
            const(grad.shape),
            pl.BlockSpec((HD, BLK), lambda i: (0, i)),
            pl.BlockSpec((1, 8, BLK), lambda i: (i, 0, 0)),
            pl.BlockSpec((HD // 2, BLK), lambda i: (0, i)),
            pl.BlockSpec((HD // 2, BLK), lambda i: (0, i)),
            const(cosine.shape),
            const(sine.shape),
        ],
        out_specs=const(shape),
        out_shape=jax.ShapeDtypeStruct(shape, BF16),
        scratch_shapes=[
            pltpu.VMEM((blocks, PAIR, BLK), BF16),
            pltpu.VMEM((blocks, BLK, PAIR), BF16),
            pltpu.VMEM((blocks, BLK, PAIR), F32),
        ],
        compiler_params=params(),
        name="attend_single_grads",
    )(whole, grad, out_t, lse, cos_t, sin_t, cosine, sine)


def third_tiles(parts):
    low = lanes(parts[0].shape[0]) < HD
    tiles = []
    for k in (0, 2):
        a, b = parts[k], parts[k + 1]
        top = jnp.where(low, a, swap_heads(b))
        bottom = jnp.where(low, swap_heads(a), b)
        tiles.append(jnp.concatenate([top, bottom], axis=0))
    return tiles


def third_parts(tiles):
    parts = []
    for tile in tiles:
        half = tile.shape[0] // 2
        top, bottom = tile[:half], tile[half:]
        low = lanes(half) < HD
        parts.append(jnp.where(low, top, swap_heads(bottom)))
        parts.append(jnp.where(low, swap_heads(top), bottom))
    return parts


def project_body(pair, single, tok, w_attn, gain, shift, w_query, o, r1, c, cq):
    tiles = [pair[g, 0].astype(F32) for g in range(GROUPS)]
    tiles += third_tiles([single[g, 0].astype(F32) for g in range(GROUPS)])
    heads = jnp.concatenate(tiles, axis=1).astype(BF16)
    o[0] = heads
    after = tok[0].astype(F32) + dot(heads, w_attn[...])
    r1[0] = after
    row = (norm_stats(after)[0] * gain[...][None] + shift[...][None]).astype(BF16)
    c[0] = row
    cq[0] = dot(row, w_query[...]).astype(BF16)


def project_call(pair, single, tokens, w_attn, gain, shift, w_query):
    seqs, rows, _ = tokens.shape
    block = pl.BlockSpec((1, rows, D), lambda s: (s, 0, 0))
    shape = lambda kind: jax.ShapeDtypeStruct((seqs, rows, D), kind)
    return pl.pallas_call(
        project_body,
        grid=(seqs,),
        in_specs=[
            pl.BlockSpec((GROUPS, 1, rows, PAIR), lambda s: (0, s, 0, 0)),
            pl.BlockSpec((GROUPS, 1, rows // 2, PAIR), lambda s: (0, s, 0, 0)),
            block,
            const((D, D)),
            VECTOR,
            VECTOR,
            const((D, D)),
        ],
        out_specs=[block] * 4,
        out_shape=[shape(BF16), shape(F32), shape(BF16), shape(BF16)],
        compiler_params=params(),
        name="project",
    )(
        pair.reshape(GROUPS, seqs, rows, PAIR),
        single.reshape(GROUPS, seqs, rows // 2, PAIR),
        tokens,
        w_attn,
        gain,
        shift,
        w_query,
    )


def memory_body(near, weight, out):
    out[...] = dot(near[...], weight[...]).astype(BF16)


def memory_call(near, weight):
    rows = near.shape[0]
    step = min(rows, 512)
    return pl.pallas_call(
        memory_body,
        grid=(rows // step,),
        in_specs=[pl.BlockSpec((step, D), lambda i: (i, 0)), const((D, 2 * D))],
        out_specs=pl.BlockSpec((step, 2 * D), lambda i: (i, 0)),
        out_shape=jax.ShapeDtypeStruct((rows, 2 * D), BF16),
        compiler_params=params(),
        name="memory",
    )(near, weight)


def move_later(values, before):
    first = lax.broadcasted_iota(jnp.int32, values.shape, 0) == 0
    return jnp.where(first, before.astype(F32), pltpu.roll(values.astype(F32), 1, 0))


def move_earlier(values, after):
    rows = values.shape[0]
    last = lax.broadcasted_iota(jnp.int32, values.shape, 0) == rows - 1
    return jnp.where(last, after.astype(F32), pltpu.roll(values.astype(F32), rows - 1, 0))


def head_rows(tile):
    low = lanes(GROUP) < HD
    return jnp.concatenate(
        [jnp.where(low, tile, 0.0), jnp.where(low, 0.0, tile)], axis=0
    ).astype(BF16)


def fold_rows(both):
    return jnp.where(lanes(GROUP) < HD, both[:GROUP], both[GROUP:])


def cross_scores(keys, query_rows, have):
    scores = dot_nt(keys, query_rows) * (SCALE * LOG2E)
    row = lax.broadcasted_iota(jnp.int32, scores.shape, 0)
    kept = jnp.where(row < RET, have[0], have[1]) > 0
    return jnp.where(kept, scores, NEGATIVE), kept


def row_heads(row):
    return jnp.where(diagonal(), row, 0.0).astype(BF16)


def diagonal():
    head = lax.broadcasted_iota(jnp.int32, (16, D), 1) // HD
    return head == lax.broadcasted_iota(jnp.int32, (16, D), 0)


def own_heads(wide):
    return jnp.sum(jnp.where(diagonal(), wide, 0.0), axis=0, keepdims=True)


def softmax_columns(scores, kept):
    peak = jnp.max(scores, axis=0, keepdims=True)
    weights = jnp.where(kept, jnp.exp2(scores - peak), 0.0)
    total = jnp.sum(weights, axis=0, keepdims=True)
    some = total > 0.0
    safe = jnp.where(some, total, 1.0)
    return weights / safe, jnp.where(some, peak + jnp.log2(safe), 0.0)


def each_window(windows, visit):
    count = 4 if windows % 4 == 0 else 1

    def step(i, _):
        for k in range(count):
            visit(i * count + k, 0)
        return 0

    lax.fori_loop(0, windows // count, step, 0)


def cross_body(windows, present, present_next, cq, memory, memory_next, out, lse, shifted, win):
    s = pl.program_id(0)
    rows = cq.shape[1]
    zero = jnp.zeros((1, D), F32)
    wide = cq[0].astype(F32)
    shifted[...] = move_later(wide, zero).reshape(windows, GROUP, D)

    def window(w, _):
        have = [present[s, w, k] for k in range(NEIGH)]
        for p in range(HEADS // 2):
            at = pl.ds(p * PAIR, PAIR)
            keys = memory[0, w, :, p * PAIR : (p + 1) * PAIR]
            values = memory[0, w, :, D + p * PAIR : D + (p + 1) * PAIR]
            ca, logs = softmax_columns(*cross_scores(keys, head_rows(shifted[w, :, at]), have))
            win[w, :, at] = fold_rows(jnp.transpose(dot_tn(values, ca.astype(BF16))))
            lse[0, w, p : p + 1] = logs
        return 0

    each_window(windows, window)
    have = [present_next[s, k] for k in range(NEIGH)]
    ca, _ = softmax_columns(
        *cross_scores(memory_next[0, :, :D], row_heads(wide[rows - 1 :]), have)
    )
    last = own_heads(dot_tn(ca.astype(BF16), memory_next[0, :, D:]))
    out[0] = move_earlier(win[...].reshape(rows, D), last).astype(BF16)


def cross_call(present, present_next, cq, memory, memory_next):
    seqs, windows = present.shape[:2]
    rows = cq.shape[1]
    keys = NEIGH * RET
    block = pl.BlockSpec((1, rows, D), lambda s: (s, 0, 0))
    return pl.pallas_call(
        lambda *refs: cross_body(windows, *refs),
        grid=(seqs,),
        in_specs=[
            pl.BlockSpec(memory_space=pltpu.SMEM),
            pl.BlockSpec(memory_space=pltpu.SMEM),
            block,
            pl.BlockSpec((1, windows, keys, 2 * D), lambda s: (s, 0, 0, 0)),
            pl.BlockSpec((1, keys, 2 * D), lambda s: (s, 0, 0)),
        ],
        out_specs=[block, pl.BlockSpec((1, windows, 8, PAIR), lambda s: (s, 0, 0, 0))],
        out_shape=[
            jax.ShapeDtypeStruct((seqs, rows, D), BF16),
            jax.ShapeDtypeStruct((seqs, windows, 8, PAIR), F32),
        ],
        scratch_shapes=[pltpu.VMEM((windows, GROUP, D), F32)] * 2,
        compiler_params=params(),
        name="cross",
    )(present, present_next, cq, memory, memory_next)


def gelu_parts(u):
    phi = 0.5 + 0.5 * lax.erf(u * math.sqrt(0.5))
    slope = phi + u * (jnp.exp2(u * u * (-0.5 * LOG2E)) * (1.0 / math.sqrt(2.0 * math.pi)))
    return u * phi, slope


def feed_body(
    steps,
    r1,
    cross_rows,
    cot,
    w_cross,
    gain,
    shift,
    w_up,
    w_down,
    output,
    d2,
    e2,
    dr,
    vectors,
    grads,
    normed,
    inverse,
    row,
    row_t,
    total,
    grad,
    up_stage,
    down_stage,
    sems,
):
    f = pl.program_id(0)
    seqs, rows = r1.shape[:2]
    batch, sq, groups, _, own, cols = grads.shape
    near = down_stage.shape[2]

    def copies(at):
        slot = lax.rem(at, 2)
        first = at * near
        return (
            pltpu.make_async_copy(up_stage.at[slot], grads.at[at, :, :, 0], sems.at[slot, 0]),
            pltpu.make_async_copy(
                down_stage.at[slot],
                grads.at[:, pl.ds(lax.rem(first, sq), near), first // sq, 1],
                sems.at[slot, 1],
            ),
        )

    @pl.when(f == 0)
    def _():
        for s in range(seqs):
            at = pl.ds(s * rows, rows)
            r2 = r1[s] + dot(cross_rows[s], w_cross[...])
            total[at] = r2
            n, inv = norm_stats(r2)
            normed[at] = n
            inverse[at] = inv
            a3 = (n * gain[...][None] + shift[...][None]).astype(BF16)
            row[at] = a3
            row_t[:, at] = flip(a3).astype(BF16)
        grad[...] = jnp.zeros_like(grad)

    up, down = w_up[...], w_down[...]
    given = cot[...]
    act, slope = gelu_parts(dot(row[...], up))
    act_low = act.astype(BF16)
    total[...] += dot(act_low, down)
    gu = (dot_nt(given, down) * slope).astype(BF16)
    grad[...] += dot_nt(gu, up)
    part = dot(row_t[...], gu).astype(BF16)
    part_down = dot(flip(act).astype(BF16), given).astype(BF16)

    @pl.when(f >= 2)
    def _():
        for copy in copies(f - 2):
            copy.wait()

    slot = lax.rem(f, 2)
    for g in range(groups):
        for q in range(sq):
            start = (g * sq + q) * own
            up_stage[slot, q, g] = part[start : start + own]
    deep = own * cols // D
    for q in range(near):
        for b in range(batch):
            start = (q * batch + b) * deep
            for x in range(D // cols):
                down_stage[slot, b, q, x * deep : (x + 1) * deep] = part_down[
                    start : start + deep, x * cols : (x + 1) * cols
                ]
    for copy in copies(f):
        copy.start()

    @pl.when(f == steps - 1)
    def _():
        output[...] = total[...].astype(BF16)
        n, back = normed[...], grad[...]
        vectors[0:1] = jnp.sum(n * back, axis=0, keepdims=True)
        vectors[1:2] = jnp.sum(back, axis=0, keepdims=True)
        summed = given.astype(F32) + norm_back(n, inverse[...], gain[...][None], back)
        d2[...] = summed
        low = summed.astype(BF16)
        e2[...] = low
        dr[...] = dot_nt(low, w_cross[...]).astype(BF16)
        for at in (steps - 2, steps - 1):
            for copy in copies(at):
                copy.wait()


def feed_call(r1, cross_rows, cot, w_cross, gain, shift, w_up, w_down, batch, peers):
    seqs, rows, _ = r1.shape
    count = seqs * rows
    sq = peers // GROUPS
    steps = batch
    cols = FF // steps
    own = D // peers
    near = peers // batch
    flat = jax.ShapeDtypeStruct((count, D), BF16)
    wide = jax.ShapeDtypeStruct((count, D), F32)
    return pl.pallas_call(
        lambda *refs: feed_body(steps, *refs),
        grid=(steps,),
        in_specs=[
            const((seqs, rows, D)),
            const((seqs, rows, D)),
            const((count, D)),
            const((D, D)),
            VECTOR,
            VECTOR,
            pl.BlockSpec((D, cols), lambda f: (0, f)),
            pl.BlockSpec((cols, D), lambda f: (f, 0)),
        ],
        out_specs=[const((count, D))] * 4
        + [const((8, D)), pl.BlockSpec(memory_space=pl.ANY)],
        out_shape=[
            flat,
            wide,
            flat,
            flat,
            jax.ShapeDtypeStruct((8, D), F32),
            jax.ShapeDtypeStruct((batch, sq, GROUPS, 2, own, cols), BF16),
        ],
        scratch_shapes=[
            pltpu.VMEM((count, D), F32),
            pltpu.VMEM((count, 1), F32),
            pltpu.VMEM((count, D), BF16),
            pltpu.VMEM((D, count), BF16),
            pltpu.VMEM((count, D), F32),
            pltpu.VMEM((count, D), F32),
            pltpu.VMEM((2, sq, GROUPS, own, cols), BF16),
            pltpu.VMEM((2, batch, near, own, cols), BF16),
            pltpu.SemaphoreType.DMA((2, 2)),
        ],
        compiler_params=params(),
        name="feed",
    )(r1, cross_rows, cot, w_cross, gain, shift, w_up, w_down)


def cross_back_body(
    windows, present, present_next, cq, dr, memory, memory_next, lse, dmem, dcq, shifted, dwin, dshifted
):
    s = pl.program_id(0)
    rows = cq.shape[1]
    zero = jnp.zeros((1, D), F32)
    wide, wide_dr = cq[0].astype(F32), dr[0].astype(F32)
    shifted[...] = move_later(wide, zero).reshape(windows, GROUP, D)
    dwin[...] = move_later(wide_dr, zero).reshape(windows, GROUP, D)

    def window(w, _):
        have = [present[s, w, k] for k in range(NEIGH)]
        for p in range(HEADS // 2):
            at = pl.ds(p * PAIR, PAIR)
            keys = memory[0, w, :, p * PAIR : (p + 1) * PAIR]
            values = memory[0, w, :, D + p * PAIR : D + (p + 1) * PAIR]
            query_rows = head_rows(shifted[w, :, at])
            grad_rows = head_rows(dwin[w, :, at])
            scores, kept = cross_scores(keys, query_rows, have)
            ca = jnp.where(kept, jnp.exp2(scores - lse[0, w, p : p + 1]), 0.0)
            dca = dot_nt(values, grad_rows)
            inner = jnp.sum(ca * dca, axis=0, keepdims=True)
            dcs = (ca * (dca - inner)).astype(BF16)
            dmem[0, w, :, at] = (dot(dcs, query_rows) * SCALE).astype(BF16)
            dmem[0, w, :, pl.ds(D + p * PAIR, PAIR)] = dot(ca.astype(BF16), grad_rows).astype(BF16)
            dshifted[w, :, at] = fold_rows(jnp.transpose(dot_tn(keys, dcs))) * SCALE
        return 0

    each_window(windows, window)
    have = [present_next[s, k] for k in range(NEIGH)]
    _, dcs, _ = row_grads(memory_next[0], wide[rows - 1 :], wide_dr[rows - 1 :], have)
    last = own_heads(dot_tn(dcs, memory_next[0, :, :D])) * SCALE
    dcq[0] = move_earlier(dshifted[...].reshape(rows, D), last).astype(BF16)


def row_grads(memory, row, grad, have):
    query_rows, grad_rows = row_heads(row), row_heads(grad)
    ca, _ = softmax_columns(*cross_scores(memory[:, :D], query_rows, have))
    dca = dot_nt(memory[:, D:], grad_rows)
    inner = jnp.sum(ca * dca, axis=0, keepdims=True)
    return ca.astype(BF16), (ca * (dca - inner)).astype(BF16), (query_rows, grad_rows)


def cross_back_call(present, present_next, cq, dr, memory, memory_next, lse):
    seqs, windows = present.shape[:2]
    rows = cq.shape[1]
    keys = NEIGH * RET
    block = pl.BlockSpec((1, rows, D), lambda s: (s, 0, 0))
    wide = pl.BlockSpec((1, windows, keys, 2 * D), lambda s: (s, 0, 0, 0))
    return pl.pallas_call(
        lambda *refs: cross_back_body(windows, *refs),
        grid=(seqs,),
        in_specs=[
            pl.BlockSpec(memory_space=pltpu.SMEM),
            pl.BlockSpec(memory_space=pltpu.SMEM),
            block,
            block,
            wide,
            pl.BlockSpec((1, keys, 2 * D), lambda s: (s, 0, 0)),
            pl.BlockSpec((1, windows, 8, PAIR), lambda s: (s, 0, 0, 0)),
        ],
        out_specs=[wide, block],
        out_shape=[
            jax.ShapeDtypeStruct((seqs, windows, keys, 2 * D), BF16),
            jax.ShapeDtypeStruct((seqs, rows, D), BF16),
        ],
        scratch_shapes=[pltpu.VMEM((windows, GROUP, D), F32)] * 3,
        compiler_params=params(),
        name="cross_grads",
    )(present, present_next, cq, dr, memory, memory_next, lse)


def project_back_body(dcq, r1, d2, w_query, gain, w_attn, do, d1, e1, vectors):
    s = pl.program_id(0)
    rows = r1.shape[1]
    back = dot_nt(dcq[0], w_query[...])
    normed, inverse = norm_stats(r1[0])

    @pl.when(s == 0)
    def _():
        vectors[...] = jnp.zeros_like(vectors)

    vectors[0:1] += jnp.sum(normed * back, axis=0, keepdims=True)
    vectors[1:2] += jnp.sum(back, axis=0, keepdims=True)
    summed = d2[0] + norm_back(normed, inverse, gain[...][None], back)
    d1[0] = summed
    low = summed.astype(BF16)
    e1[0] = low
    heads = dot_nt(low, w_attn[...])
    for g in range(GROUPS):
        do[g, 0, 0:rows] = heads[:, g * PAIR : (g + 1) * PAIR].astype(BF16)
    tiles = [heads[:, (GROUPS + k) * PAIR : (GROUPS + k + 1) * PAIR] for k in range(2)]
    for g, part in enumerate(third_parts(tiles)):
        do[g, 0, rows:] = part.astype(BF16)


def project_back_call(dcq, r1, d2, w_query, gain, w_attn):
    seqs, rows, _ = r1.shape
    block = pl.BlockSpec((1, rows, D), lambda s: (s, 0, 0))
    shape = lambda kind: jax.ShapeDtypeStruct((seqs, rows, D), kind)
    return pl.pallas_call(
        project_back_body,
        grid=(seqs,),
        in_specs=[
            block,
            block,
            block,
            const((D, D)),
            VECTOR,
            const((D, D)),
        ],
        out_specs=[
            pl.BlockSpec((GROUPS, 1, rows + rows // 2, PAIR), lambda s: (0, s, 0, 0)),
            block,
            block,
            const((8, D)),
        ],
        out_shape=[
            jax.ShapeDtypeStruct((GROUPS, seqs, rows + rows // 2, PAIR), BF16),
            shape(F32),
            shape(BF16),
            jax.ShapeDtypeStruct((8, D), F32),
        ],
        compiler_params=params(),
        name="project_grads",
    )(dcq, r1, d2, w_query, gain, w_attn)


def put_rows(place, outs, block, value):
    batch, groups, part, _ = outs[0].shape[:1] + outs[0].shape[-3:]
    sq = 2 if len(outs) == 2 else outs[0].shape[1]
    own = D // (sq * groups)
    value = value.astype(BF16)

    def store(q, slot):
        for g in range(groups):
            start, done = block * own, 0
            at = (g * sq + q) * own
            while done < own:
                b, x = divmod(start + done, part)
                count = min(part - x, own - done)
                slot(b, g, x, count, value[at + done : at + done + count])
                done += count

    for q in range(sq):
        if len(outs) == 1:

            def put(b, g, x, count, rows, q=q):
                outs[0][b, q, g, x : x + count] = rows

            store(q, put)
            continue
        for k, out in enumerate(outs):

            @pl.when(place[1] == q ^ k)
            def _(q=q, out=out):
                def put(b, g, x, count, rows):
                    out[b, g, x : x + count] = rows

                store(q, put)


def others_body(
    split,
    per_sequence,
    place,
    present,
    near,
    dmem,
    memory,
    before,
    w_memory,
    o,
    e1,
    vectors,
    c_far,
    dq_far,
    cross_far,
    e2_far,
    dnear,
    *refs,
):
    outs, (acc, grads, c, dq, cross_rows, e2, sems) = refs[:-7], refs[-7:]
    i = pl.program_id(0)
    copies = [
        pltpu.make_async_copy(source, target, sems.at[k])
        for k, (source, target) in enumerate(
            ((c_far, c), (dq_far, dq), (cross_far, cross_rows), (e2_far, e2))
        )
    ]

    @pl.when(i == 0)
    def _():
        for copy in copies:
            copy.start()
        acc[...] = jnp.zeros_like(acc)

    grads[...] = dmem[...].reshape(grads.shape)

    @pl.when(lax.rem(i, per_sequence) == 0)
    def _():
        keys = memory.shape[2]
        edge = edge_grads(
            memory[0, 0],
            before[0, 0:1].astype(F32),
            before[0, 1:2].astype(F32),
            [present[i // per_sequence, 0, k] for k in range(NEIGH)],
        )
        grads[0:keys] = (dmem[0, 0].astype(F32) + edge).astype(BF16)

    dnear[...] = dot_nt(grads[...], w_memory[...]).astype(BF16)
    acc[...] += dot_tn(near[...], grads[...])

    @pl.when(i == 0)
    def _():
        put_rows(place, outs, 0, dot_tn(o[...], e1[...]))

    @pl.when(i == pl.num_programs(0) - 1)
    def _():
        for copy in copies:
            copy.wait()
        put_rows(place, outs, 1, dot_tn(c[...], dq[...]))
        put_rows(place, outs, 2, dot_tn(cross_rows[...], e2[...]))
        put_rows(place, outs, 3, acc[:, :D])
        put_rows(place, outs, 4, acc[:, D:])
        batch, groups, size = outs[0].shape[0], outs[0].shape[-3], outs[0].shape[-2]
        sq = vectors.shape[0] // groups
        used = 5 * D // (sq * groups) - (batch - 1) * size
        for g in range(groups):
            if split:
                for k, out in enumerate(outs):
                    out[batch - 1, g, used:] = vectors[g * sq + (place[1] ^ k)]
            else:
                for q in range(sq):
                    outs[0][batch - 1, q, g, used:] = vectors[g * sq + q]


def edge_grads(memory, row, grad, have):
    ca, dcs, (query_rows, grad_rows) = row_grads(memory, row, grad, have)
    return jnp.concatenate([dot(dcs, query_rows) * SCALE, dot(ca, grad_rows)], axis=1)


def others_call(
    split,
    place,
    present,
    near,
    dmem,
    memory,
    before,
    w_memory,
    o,
    e1,
    c,
    dq,
    cross_rows,
    e2,
    vectors,
    batch,
    peers,
):
    seqs, windows, keys, _ = dmem.shape
    count = o.shape[0]
    size = min(2, windows)
    steps = windows // size
    own = D // peers
    part = (5 * own + vectors.shape[1]) // batch
    shapes = [(batch, peers // GROUPS, GROUPS, part, D)]
    if split:
        shapes = [(batch, GROUPS, part, D)] * 2
    smem = pl.BlockSpec(memory_space=pltpu.SMEM)
    far = pl.BlockSpec(memory_space=pl.ANY)
    block = pl.BlockSpec((size * keys, D), lambda i: (i, 0))
    return pl.pallas_call(
        lambda *refs: others_body(split, steps, *refs),
        grid=(seqs * steps,),
        in_specs=[
            smem,
            smem,
            block,
            pl.BlockSpec((1, size, keys, 2 * D), lambda i: (i // steps, lax.rem(i, steps), 0, 0)),
            pl.BlockSpec((1, 1, keys, 2 * D), lambda i: (i // steps, 0, 0, 0)),
            pl.BlockSpec((1, 2, D), lambda i: (i // steps, 0, 0)),
            const((D, 2 * D)),
            const((count, D)),
            const((count, D)),
            const(vectors.shape),
            far,
            far,
            far,
            far,
        ],
        out_specs=[block] + [const(shape) for shape in shapes],
        out_shape=[jax.ShapeDtypeStruct(near.shape, BF16)]
        + [jax.ShapeDtypeStruct(shape, BF16) for shape in shapes],
        scratch_shapes=[
            pltpu.VMEM((D, 2 * D), F32),
            pltpu.VMEM((size * keys, 2 * D), BF16),
        ]
        + [pltpu.VMEM((count, D), BF16)] * 4
        + [pltpu.SemaphoreType.DMA((4,))],
        compiler_params=params(),
        name="other_grads",
    )(
        place,
        present,
        near,
        dmem,
        memory,
        before,
        w_memory,
        o,
        e1,
        vectors,
        c,
        dq,
        cross_rows,
        e2,
    )


def last_body(pair, single, tok, d1, gain, w_qkv, out):
    rows = tok.shape[1]
    half = rows // 2
    low = lanes(rows) < HD
    boths = [single[g, 0, 0:rows].astype(F32) for g in range(GROUPS)]
    queries = third_tiles([single[g, 0, rows : rows + half].astype(F32) for g in range(GROUPS)])
    keys = [jnp.where(low, boths[k], swap_heads(boths[k + 1])) for k in (0, 2)]
    values = [jnp.where(low, swap_heads(boths[k]), boths[k + 1]) for k in (0, 2)]
    parts = []
    for at, third in ((0, queries), (rows, keys), (2 * rows, values)):
        parts += [pair[g, 0, at : at + rows] for g in range(GROUPS)]
        parts += [tile.astype(BF16) for tile in third]
    back = dot_nt(jnp.concatenate(parts, axis=1), w_qkv[...])
    normed, inverse = norm_stats(tok[0].astype(F32))
    out[0] = (d1[0] + norm_back(normed, inverse, gain[...][None], back)).astype(BF16)


def last_call(pair, single, tokens, d1, gain, w_qkv):
    seqs, rows, _ = tokens.shape
    block = pl.BlockSpec((1, rows, D), lambda s: (s, 0, 0))
    return pl.pallas_call(
        last_body,
        grid=(seqs,),
        in_specs=[
            pl.BlockSpec((GROUPS, 1, 3 * rows, PAIR), lambda s: (0, s, 0, 0)),
            pl.BlockSpec((GROUPS, 1, 3 * rows // 2, PAIR), lambda s: (0, s, 0, 0)),
            block,
            block,
            VECTOR,
            const((D, 3 * D)),
        ],
        out_specs=block,
        out_shape=jax.ShapeDtypeStruct((seqs, rows, D), BF16),
        compiler_params=params(),
        name="token_grads",
    )(
        pair.reshape(GROUPS, seqs, 3 * rows, PAIR),
        single.reshape(GROUPS, seqs, 3 * rows // 2, PAIR),
        tokens,
        d1,
        gain,
        w_qkv,
    )


def heads_body(place, *refs):
    pieces, (pair, single, gain, shift) = refs[:GROUPS], refs[GROUPS : GROUPS + 4]
    weights, (out, acc, sums, held) = refs[GROUPS + 4 : GROUPS + 10], refs[GROUPS + 10 :]
    i = pl.program_id(0)
    per, rows = pair.shape[0], pair.shape[1] // 3
    for k, piece in enumerate(pieces):

        @pl.when(i == k)
        def _(piece=piece):
            held[...] = piece[...]

    third = unpack_half(single[:, rows : rows + rows // 2], rows)
    grads = jnp.concatenate(
        [pair[:, k * rows : (k + 1) * rows].reshape(per * rows, PAIR) for k in range(3)]
        + [single[:, 0:rows].reshape(per * rows, PAIR), third],
        axis=1,
    )
    part = dot_tn(held[...], grads)
    total = jnp.sum(grads.astype(F32), axis=0, keepdims=True)

    @pl.when(i == 0)
    def _():
        acc[...] = part
        sums[0:1] = total

    @pl.when(i > 0)
    def _():
        acc[...] += part
        sums[0:1] += total

    @pl.when(i == pl.num_programs(0) - 1)
    def _():
        low = lanes(D) < HD
        odd = lax.rem(place[0], 2) == 1
        wide = [weight[...].astype(F32) for weight in weights]
        q3, k3, v3 = [jnp.where(odd, swap_heads(t), t) for t in wide[3:]]
        columns = wide[:3] + [jnp.where(low, k3, swap_heads(v3)), jnp.where(low, q3, 0.0)]
        columns = jnp.concatenate(columns, axis=1)
        whole, over = acc[...], sums[0:1]
        d_gain = jnp.sum(whole * columns, axis=1, keepdims=True)
        d_shift = jnp.sum(over * columns, axis=1, keepdims=True)
        lane = lax.broadcasted_iota(jnp.int32, whole.shape, 1)
        flipped = jnp.transpose(
            jnp.concatenate([gain[...][None], shift[...][None], jnp.zeros((6, D), F32)], axis=0)
        )
        value = whole * flipped[:, 0:1] + flipped[:, 1:2] * over
        at = 4 * PAIR + HD
        value = jnp.where(lane == at, d_gain, jnp.where(lane == at + 1, d_shift, value))
        high, low, sq, groups, own, _ = out.shape
        for g in range(groups):
            for q in range(sq):
                for b in range(high * low):
                    start = ((g * sq + q) * high * low + b) * own
                    out[b // low, b % low, q, g] = value[start : start + own].astype(BF16)


def heads_call(place, pieces, pair, single, gain, shift, weight, batch):
    peers, rows = pair.shape[0], pair.shape[1] // 3
    per = peers // GROUPS
    shape = (batch // 2, 2, per, GROUPS, D // peers // batch, 5 * PAIR)

    def chunk(i, place):
        return (place[2 + i], 0, 0)

    return pl.pallas_call(
        heads_body,
        grid_spec=pltpu.PrefetchScalarGridSpec(
            num_scalar_prefetch=1,
            grid=(GROUPS,),
            in_specs=[const((per * rows, D))] * GROUPS
            + [
                pl.BlockSpec((per, 3 * rows, PAIR), chunk),
                pl.BlockSpec((per, 3 * rows // 2, PAIR), chunk),
                VECTOR,
                VECTOR,
            ]
            + head_columns(0),
            out_specs=const(shape),
            scratch_shapes=[
                pltpu.VMEM((D, 5 * PAIR), F32),
                pltpu.VMEM((8, 5 * PAIR), F32),
                pltpu.VMEM((per * rows, D), BF16),
            ],
        ),
        out_shape=jax.ShapeDtypeStruct(shape, BF16),
        compiler_params=params(),
        name="qkv_grads",
    )(place, *pieces, pair, single, gain, shift, *[weight] * 6)


SEQ = ("hg", "sq")
BATCH = ("by", "bx")


def from_behind(value, by):
    peers = lax.axis_size(SEQ)
    pairs = [(i, i + by) for i in range(peers) if 0 <= i + by < peers]
    return lax.ppermute(value, SEQ, pairs)


def swap_all(value):
    return lax.all_to_all(value, SEQ, 0, 0, tiled=True)


def add_rows(value):
    flat = value.reshape((value.shape[0] * value.shape[1],) + value.shape[2:])
    own = lax.psum_scatter(flat, BATCH + ("sq",), scatter_dimension=0, tiled=True)
    return own.reshape(value.shape[2:])


def rotated(value, by):
    return lax.ppermute(value, "hg", [(i, (i + by) % GROUPS) for i in range(GROUPS)])


def add_groups(own):
    here = lax.axis_index("hg")
    total = lax.dynamic_index_in_dim(own, here, 0, keepdims=False).astype(F32)
    for k in range(1, GROUPS):
        part = lax.dynamic_index_in_dim(own, lax.rem(here + k, GROUPS), 0, keepdims=False)
        total += rotated(part, k).astype(F32)
    return total.astype(BF16)


def gather_groups(own):
    here = lax.axis_index("hg")
    pieces = [lax.dynamic_index_in_dim(own, here, 0, keepdims=False)]
    for k in range(1, GROUPS):
        part = lax.dynamic_index_in_dim(own, lax.rem(here + k, GROUPS), 0, keepdims=False)
        pieces.append(rotated(part, k))
    return in_order([pieces[(-j) % GROUPS] for j in range(GROUPS)], here, "shift")


def passed(value, by):
    pairs = [(i, i + by) for i in range(GROUPS) if 0 <= i + by < GROUPS]
    return lax.ppermute(value, "hg", pairs)


def in_order(pieces, here, how):
    count = len(pieces)
    out = []
    for j in range(count):
        value = pieces[j]
        for me in range(1, count):
            at = (j - me) % count if how == "shift" else j ^ me
            value = jnp.where(here == me, pieces[at], value)
        out.append(value)
    return out


def gather_batch(value):
    size = lax.axis_size(BATCH)
    pieces = [value] + [
        lax.ppermute(value, BATCH, [(i, i ^ k) for i in range(size)]) for k in range(1, size)
    ]
    return in_order(pieces, lax.axis_index(BATCH), "xor")


def halve(value, name, axis):
    if lax.axis_size(name) == 2:
        here = lax.axis_index(name)
        kept = lax.dynamic_index_in_dim(value, here, axis, keepdims=False)
        given = lax.dynamic_index_in_dim(value, 1 - here, axis, keepdims=False)
        got = lax.ppermute(given, name, [(0, 1), (1, 0)])
        return (kept.astype(F32) + got.astype(F32)).astype(BF16)
    parts = lax.all_to_all(value, name, axis, 0, tiled=False)
    return jnp.sum(parts.astype(F32), axis=0).astype(BF16)


def own_sequence(value):
    if lax.axis_size("sq") == 2:
        here = lax.axis_index("sq")
        kept = lax.dynamic_index_in_dim(value, here, 0, keepdims=False)
        given = lax.dynamic_index_in_dim(value, 1 - here, 0, keepdims=False)
        return [kept, lax.ppermute(given, "sq", [(0, 1), (1, 0)])]
    return [lax.all_to_all(value, "sq", 0, 0, tiled=True)]


def together(*values):
    return lax.optimization_barrier(values)


def shards(
    tokens,
    neighbours,
    present,
    qkv_weight,
    attn_weight,
    query_weight,
    memory_weight,
    cross_weight,
    up_weight,
    down_weight,
    attn_gain,
    attn_shift,
    cross_gain,
    cross_shift,
    mlp_gain,
    mlp_shift,
    cotangent,
):
    seqs, rows = tokens.shape[:2]
    count = seqs * rows
    peers = lax.axis_size(SEQ)
    batch = lax.axis_size(BATCH)
    easy = [lax.axis_size(name) for name in ("by", "bx", "sq")] == [2, 2, 2]
    group, core = lax.axis_index("hg"), lax.axis_index("sq")
    place = jnp.stack([group, core] + [chunk_of(which, group) for which in range(GROUPS)])
    place = place.astype(jnp.int32)
    cos_np, sin_np = rope_tables(peers * rows)
    cosine, sine = jnp.asarray(cos_np), jnp.asarray(sin_np)
    cos_t = jnp.asarray(np.ascontiguousarray(cos_np[:, : HD // 2].T))
    sin_t = jnp.asarray(np.ascontiguousarray(sin_np[:, HD // 2 : HD].T))

    windows = present.shape[1]
    keys = NEIGH * RET
    near = neighbours.reshape(-1, D)

    def chunk(which, first, second):
        return chunk_call(
            which, place, first, second, attn_gain, attn_shift, qkv_weight, cosine, sine
        )

    own = own_sequence(tokens)
    behind, ahead = [passed(part, 1) for part in own], [passed(part, -1) for part in own]
    chunks = [chunk(0, own, own)]
    chunks[0], behind[0], ahead[0] = together(chunks[0], behind[0], ahead[0])
    behind_two = [passed(part, 1) for part in behind]
    ahead_two = [passed(part, -1) for part in ahead]
    memory = memory_call(near, memory_weight)
    memory, behind_two[0], ahead_two[0] = together(memory, behind_two[0], ahead_two[0])
    chunks.append(chunk(1, ahead, behind))
    chunks[1], behind_two[-1], ahead_two[-1] = together(chunks[1], behind_two[-1], ahead_two[-1])
    behind_three = [passed(part, 1) for part in behind_two]
    ahead_three = [passed(part, -1) for part in ahead_two]
    chunks.append(chunk(2, ahead_two, behind_two))
    chunks[2], behind_three, ahead_three = together(chunks[2], behind_three, ahead_three)
    last = [jnp.where(group == GROUPS - 1, x, y) for x, y in zip(behind_three, behind)]
    chunks.append(chunk(3, ahead_three, last))
    memory = memory.reshape(seqs, windows, keys, 2 * D)
    near_next, chunks[3] = together(neighbours[:, 0].reshape(seqs * keys, D), chunks[3])
    near_next = from_behind(near_next, -1)
    present_next = from_behind(present[:, 0], -1)
    pieces = [chunk[0] for chunk in chunks]
    o_pair, o_pair_t, lse_pair, pairs = pair_forward(place, [chunk[1] for chunk in chunks])
    singles, o_pair, near_next = together([chunk[2] for chunk in chunks], o_pair, near_next)
    memory_next = memory_call(near_next, memory_weight).reshape(seqs, keys, 2 * D)
    o_pair = swap_all(o_pair.reshape(peers, rows, PAIR))
    o_single, o_single_t, lse_single, singles = single_forward(place, singles, rows)
    o_single, o_pair = together(o_single, o_pair)
    o_single = swap_all(o_single)
    o_single, memory_next = together(o_single, memory_next)
    o, r1, c, cq = project_call(
        o_pair, o_single, tokens, attn_weight, cross_gain, cross_shift, query_weight
    )
    cross_rows, lse = cross_call(present, present_next, cq, memory, memory_next)
    output, d2, e2, dr, mlp_vectors, feed = feed_call(
        r1,
        cross_rows,
        cotangent.reshape(count, D),
        cross_weight,
        mlp_gain,
        mlp_shift,
        up_weight,
        down_weight,
        batch,
        peers,
    )
    dr = dr.reshape(seqs, rows, D)
    before = from_behind(jnp.concatenate([cq[:, -1:], dr[:, -1:]], axis=1), 1)
    feed, before = together(feed, before)
    feed = add_rows(feed)
    dmem, dq = cross_back_call(present, present_next, cq, dr, memory, memory_next, lse)
    do, d1, e1, cross_vectors = project_back_call(
        dq, r1, d2.reshape(seqs, rows, D), query_weight, cross_gain, attn_weight
    )
    do = swap_all(do.reshape(peers, 3 * rows // 2, PAIR))
    own = D // peers
    vectors = jnp.concatenate([mlp_vectors[:2], cross_vectors[:2]], axis=0).astype(BF16)
    vectors = vectors.reshape(4, peers, own).transpose(1, 0, 2).reshape(peers, 1, 4 * own)
    vectors = jnp.pad(vectors, ((0, 0), (0, own // 3 - 1), (0, D - 4 * own)))
    dnear, *others = others_call(
        easy,
        place,
        present,
        near,
        dmem,
        memory,
        before,
        memory_weight,
        o.reshape(count, D),
        e1.reshape(count, D),
        c.reshape(count, D),
        dq.reshape(count, D),
        cross_rows.reshape(count, D),
        e2,
        vectors,
        batch,
        peers,
    )
    do, others = together(do, others)
    if easy:
        kept, given = others
        got = lax.ppermute(given, "sq", [(0, 1), (1, 0)])
    else:
        others = add_rows(others[0])
    d_single = single_backward(singles, do, o_single_t, lse_single, cos_t, sin_t, cosine, sine)
    do, d_single = together(do, d_single)
    d_single_all = swap_all(d_single)
    do, feed = together(do, feed)
    feed = lax.psum_scatter(feed, "hg", scatter_dimension=0, tiled=False)
    d_pair = pair_backward(pairs, do, o_pair_t, lse_pair, cos_t, sin_t, cosine, sine)
    d_pair_all, d_single_all = together(d_pair, d_single_all)
    d_pair_all = swap_all(d_pair_all)
    if easy:
        d_pair, kept, got = together(d_pair, kept, got)
        others = (kept.astype(F32) + got.astype(F32)).astype(BF16)
        others = others.reshape((2, 2) + others.shape[1:])
        cut = GROUPS // 2
        others = [halve(others[:, :, :cut], "bx", 1), halve(others[:, :, cut:], "by", 0)]
    g_qkv = heads_call(place, pieces, d_pair, d_single, attn_gain, attn_shift, qkv_weight, batch)
    g_qkv, others, feed = together(g_qkv, others, feed)
    g_qkv = add_rows(g_qkv.reshape((batch,) + g_qkv.shape[2:]))
    feed = gather_batch(feed)
    if easy:
        others = [halve(others[0], "by", 0), halve(others[1], "bx", 0)]
        others = jnp.concatenate(others, axis=0)
    others = add_groups(others)
    grad_tokens = last_call(d_pair_all, d_single_all, tokens, d1, attn_gain, qkv_weight)
    g_qkv, others, grad_tokens, feed = together(g_qkv, others, grad_tokens, feed)
    g_qkv = jnp.stack(gather_groups(g_qkv))
    others = gather_batch(others)
    g_qkv = jnp.stack(gather_batch(g_qkv))

    others = jnp.concatenate(others, axis=0).astype(F32)
    kinds = [others[k * own : (k + 1) * own] for k in range(5)]
    others = others[5 * own, : 4 * own].reshape(4, own)
    g_up = jnp.concatenate([part[0] for part in feed], axis=1).astype(F32)
    deep = FF // peers // batch
    g_down = jnp.stack([part[1] for part in feed]).reshape(batch, D * batch // FF, deep, FF // batch)
    g_down = g_down.transpose(0, 2, 1, 3).reshape(FF // peers, D).astype(F32)
    g_qkv = g_qkv.transpose(0, 2, 1, 3).reshape(own, GROUPS, 5 * PAIR).astype(F32)

    def mine(start, width):
        return g_qkv[:, :, start : start + width].reshape(own, GROUPS * width)

    third = 3 * PAIR
    grad_qkv = jnp.concatenate(
        [
            mine(0, PAIR),
            mine(4 * PAIR, HD),
            mine(PAIR, PAIR),
            mine(third, HD),
            mine(2 * PAIR, PAIR),
            mine(third + HD, HD),
        ],
        axis=1,
    )
    vectors = jnp.sum(g_qkv[:, :, 4 * PAIR + HD : 4 * PAIR + HD + 2], axis=1)
    return (
        output.reshape(seqs, rows, D),
        grad_tokens,
        dnear.reshape(neighbours.shape),
        grad_qkv,
        kinds[0],
        kinds[1],
        jnp.concatenate(kinds[3:], axis=1),
        kinds[2],
        g_up,
        g_down,
        vectors[:, 0],
        vectors[:, 1],
        others[2],
        others[3],
        others[0],
        others[1],
    )


def solution(mesh):
    batch, seq = mesh.shape["batch"], mesh.shape["seq"]
    fine = Mesh(
        mesh.devices.reshape(batch // 2, 2, GROUPS, seq // GROUPS), ("by", "bx", "hg", "sq")
    )
    rows = P(BATCH, SEQ, None)
    windows = P(BATCH, SEQ, None, None, None)
    return jax.shard_map(
        shards,
        mesh=fine,
        in_specs=(rows, windows, rows) + (P(),) * 13 + (rows,),
        out_specs=(rows, rows, windows) + (P(SEQ, None),) * 7 + (P(SEQ),) * 6,
        check_vma=False,
    )
```

```python
import itertools
import math

import jax
import jax.numpy as jnp
import numpy as np
from jax import lax
from jax.experimental import pallas as pl
from jax.experimental.pallas import tpu as pltpu
from jax.sharding import Mesh
from jax.sharding import PartitionSpec as P

D = 768
HEADS = 12
HD = 64
FF = 3072
GROUP = 64
NEIGH = 2
RET = 128
PAIR = 128
BLK = 512
GROUPS = 4

EPSILON = 1e-05
NEGATIVE = -1e30
SCALE = 1.0 / math.sqrt(HD)
LOG2E = math.log2(math.e)
VMEM_LIMIT = 56 * 1024 * 1024

F32 = jnp.float32
BF16 = jnp.bfloat16


def params(limit=VMEM_LIMIT):
    return pltpu.CompilerParams(vmem_limit_bytes=limit)


def dot(left, right):
    return jnp.dot(left, right, preferred_element_type=F32)


def dot_nt(left, right):
    return lax.dot_general(left, right, (((1,), (1,)), ((), ())), preferred_element_type=F32)


def dot_tn(left, right):
    return lax.dot_general(left, right, (((0,), (0,)), ((), ())), preferred_element_type=F32)


def flip(value):
    return jnp.transpose(value.astype(F32))


def rope_tables(length):
    half = HD // 2
    frequency = np.float32(10000.0) ** (-np.arange(half, dtype=np.float32) * np.float32(2.0) / np.float32(HD))
    angles = np.arange(length, dtype=np.float32)[:, None] * frequency[None, :].astype(np.float32)
    cosine, sine = np.cos(angles).astype(np.float32), np.sin(angles).astype(np.float32)
    return (
        np.concatenate([cosine] * 4, axis=1),
        np.concatenate([-sine, sine] * 2, axis=1),
    )


def lanes(rows):
    return lax.broadcasted_iota(jnp.int32, (rows, PAIR), 1)


def turn(tile, cosine, sine):
    rows = tile.shape[0]
    first = (lanes(rows) % HD) < HD // 2
    swapped = jnp.where(first, pltpu.roll(tile, PAIR - HD // 2, 1), pltpu.roll(tile, HD // 2, 1))
    return tile * cosine + swapped * sine


def swap_heads(tile):
    return pltpu.roll(tile, HD, 1)


def norm_stats(values):
    mean = jnp.mean(values, axis=-1, keepdims=True)
    centred = values - mean
    inverse = lax.rsqrt(jnp.mean(centred * centred, axis=-1, keepdims=True) + EPSILON)
    return centred * inverse, inverse


def norm_back(normed, inverse, gain, grad):
    scaled = grad * gain
    return inverse * (
        scaled
        - jnp.mean(scaled, axis=-1, keepdims=True)
        - normed * jnp.mean(scaled * normed, axis=-1, keepdims=True)
    )


VECTOR = pl.BlockSpec((D,), lambda *ids: (0,))


def const(shape):
    rank = len(shape)
    return pl.BlockSpec(shape, lambda *ids: (0,) * rank)


def chunk_body(which, place, *refs):
    halves = (len(refs) - 15) // 2
    near, far, refs = refs[:halves], refs[halves : 2 * halves], refs[2 * halves :]
    gain, shift = refs[:2]
    weights, (cosine, sine, normed, pair, single, tokens, columns) = refs[2:8], refs[8:]
    rows = tokens.shape[0] // halves
    first = use_first(which, place[0])
    for parts, wanted in ((near, first), (far, jnp.logical_not(first))):

        @pl.when(wanted)
        def _(parts=parts):
            for k, part in enumerate(parts):
                at = place[1] * (1 - 2 * k) + k if halves > 1 else 0
                tokens[pl.ds(at * rows, rows)] = part[...].reshape(rows, D)

    odd = lax.rem(place[0], 2) == 1
    for k, weight in enumerate(weights):
        columns[:, k * PAIR : (k + 1) * PAIR] = weight[...]
    n, _ = norm_stats(tokens[...].astype(F32))
    normed[...] = n.astype(BF16)
    out = dot((n * gain[...][None] + shift[...][None]).astype(BF16), columns[...])
    cos, sin = cosine[...], sine[...]
    q01, k01, v01, q2, k2, v2 = [out[:, k * PAIR : (k + 1) * PAIR] for k in range(6)]
    low = lanes(tokens.shape[0]) < HD
    q2, k2, v2 = [jnp.where(odd, swap_heads(t), t) for t in (q2, k2, v2)]
    pair[:, :PAIR] = (turn(q01, cos, sin) * (SCALE * LOG2E)).astype(BF16)
    pair[:, PAIR : 2 * PAIR] = turn(k01, cos, sin).astype(BF16)
    pair[:, 2 * PAIR :] = v01.astype(BF16)
    single[:, :PAIR] = jnp.where(low, turn(k2, cos, sin), swap_heads(v2)).astype(BF16)
    single[:, PAIR:] = jnp.where(low, turn(q2, cos, sin) * (SCALE * LOG2E), 0.0).astype(BF16)


def use_first(which, group):
    if which == 0:
        return group >= 0
    if which == 1:
        return group < GROUPS - 1
    if which == 2:
        return group < 2
    return group == 0


def chunk_of(which, group):
    if which == 0:
        return group
    if which == 1:
        return jnp.where(group < GROUPS - 1, group + 1, group - 1)
    if which == 2:
        return lax.rem(group + 2, GROUPS)
    return jnp.where(group == 0, GROUPS - 1, jnp.where(group == GROUPS - 1, 0, group - 1))


def head_columns(index):
    def column(first, shared):
        def at(i, place):
            return (0, first + (place[0] // 2 if shared else place[0]))

        return pl.BlockSpec((D, PAIR), at)

    return [column(6 * k, False) for k in range(3)] + [column(6 * k + 4, True) for k in range(3)]


def chunk_call(which, place, near, far, gain, shift, weight, cosine, sine):
    count = sum(part.size for part in near) // D
    whole = lambda part: pl.BlockSpec(part.shape, lambda i, place: (0,) * part.ndim)
    table = pl.BlockSpec((count, PAIR), lambda i, place: (place[2 + which], 0))
    return pl.pallas_call(
        lambda *refs: chunk_body(which, *refs),
        grid_spec=pltpu.PrefetchScalarGridSpec(
            num_scalar_prefetch=1,
            grid=(1,),
            in_specs=[whole(part) for part in (*near, *far)]
            + [VECTOR, VECTOR]
            + head_columns(0)
            + [table, table],
            out_specs=[const((count, D)), const((count, 3 * PAIR)), const((count, 2 * PAIR))],
            scratch_shapes=[pltpu.VMEM((count, D), BF16), pltpu.VMEM((D, 6 * PAIR), BF16)],
        ),
        out_shape=[
            jax.ShapeDtypeStruct((count, D), BF16),
            jax.ShapeDtypeStruct((count, 3 * PAIR), BF16),
            jax.ShapeDtypeStruct((count, 2 * PAIR), BF16),
        ],
        compiler_params=params(),
        name="qkv_chunk",
    )(place, *near, *far, gain, shift, *[weight] * 6, cosine, sine)


def unpack_half(packed, rows):
    peers = packed.shape[0]
    wide = packed.astype(F32).reshape(peers * rows // 2, PAIR)
    low = lanes(peers * rows // 2) < HD
    top = jnp.where(low, wide, 0.0).reshape(peers, rows // 2, PAIR)
    bottom = jnp.where(low, swap_heads(wide), 0.0).reshape(peers, rows // 2, PAIR)
    return jnp.concatenate([top, bottom], axis=1).reshape(peers * rows, PAIR).astype(BF16)


def pack_half(tile, rows):
    blocks = tile.shape[0] // rows
    cut = tile.reshape(blocks, rows, PAIR)
    top = cut[:, : rows // 2].reshape(blocks * rows // 2, PAIR)
    bottom = cut[:, rows // 2 :].reshape(blocks * rows // 2, PAIR)
    return (top + swap_heads(bottom)).reshape(blocks, rows // 2, PAIR)


def causal():
    key = lax.broadcasted_iota(jnp.int32, (BLK, BLK), 0)
    query = lax.broadcasted_iota(jnp.int32, (BLK, BLK), 1)
    return key <= query


def head_masks(tile_t):
    upper = lax.broadcasted_iota(jnp.int32, tile_t.shape, 0) < HD
    return jnp.where(upper, tile_t, 0.0).astype(BF16), jnp.where(upper, 0.0, tile_t).astype(BF16)


def softmax_sweep(i, heads, key_at, value_t_at):
    def visit(j, carry, masked):
        keys = key_at(j)
        values_t = value_t_at(j)
        out = []
        for (query_t, at), (top, total, acc) in zip(heads, carry):
            s = dot(keys, query_t)
            if masked:
                s = jnp.where(causal(), s, NEGATIVE)
            peak = jnp.maximum(top, jnp.max(s, axis=0, keepdims=True))
            p = jnp.exp2(s - peak)
            fade = jnp.exp2(top - peak)
            out.append(
                (
                    peak,
                    total * fade + jnp.sum(p, axis=0, keepdims=True),
                    acc * fade + dot(values_t[at : at + HD], p.astype(BF16)),
                )
            )
        return tuple(out)

    start = tuple(
        (
            jnp.full((1, BLK), NEGATIVE, F32),
            jnp.zeros((1, BLK), F32),
            jnp.zeros((HD, BLK), F32),
        )
        for _ in heads
    )
    carry = lax.fori_loop(0, i, lambda j, carry: visit(j, carry, False), start)
    carry = visit(i, carry, True)
    return [(acc / total, top + jnp.log2(total)) for top, total, acc in carry]


def pair_forward_body(place, *refs):
    chunks, (out, out_t, lse, whole, values_t) = refs[:GROUPS], refs[GROUPS:]
    i = pl.program_id(0)

    @pl.when(i == 0)
    def _():
        for which, chunk in enumerate(chunks):
            at = place[2 + which]
            whole[at] = chunk[...]
            values_t[at] = flip(chunk[:, 2 * PAIR :]).astype(BF16)

    low, high = head_masks(flip(whole[i, :, :PAIR]))
    heads = softmax_sweep(
        i,
        [(low, 0), (high, HD)],
        lambda j: whole[j, :, PAIR : 2 * PAIR],
        lambda j: values_t[j],
    )
    o_t = jnp.concatenate([heads[0][0], heads[1][0]], axis=0)
    out_t[...] = o_t
    lse[0, 0:1] = heads[0][1]
    lse[0, 1:2] = heads[1][1]
    out[...] = jnp.transpose(o_t).astype(BF16)


def pair_forward(place, chunks):
    return pl.pallas_call(
        pair_forward_body,
        grid_spec=pltpu.PrefetchScalarGridSpec(
            num_scalar_prefetch=1,
            grid=(GROUPS,),
            in_specs=[const((BLK, 3 * PAIR))] * GROUPS,
            out_specs=[
                pl.BlockSpec((BLK, PAIR), lambda i, place: (i, 0)),
                pl.BlockSpec((PAIR, BLK), lambda i, place: (0, i)),
                pl.BlockSpec((1, 8, BLK), lambda i, place: (i, 0, 0)),
                const((GROUPS, BLK, 3 * PAIR)),
            ],
            scratch_shapes=[pltpu.VMEM((GROUPS, PAIR, BLK), BF16)],
        ),
        out_shape=[
            jax.ShapeDtypeStruct((GROUPS * BLK, PAIR), BF16),
            jax.ShapeDtypeStruct((PAIR, GROUPS * BLK), F32),
            jax.ShapeDtypeStruct((GROUPS, 8, BLK), F32),
            jax.ShapeDtypeStruct((GROUPS, BLK, 3 * PAIR), BF16),
        ],
        compiler_params=params(),
        name="attend_pair",
    )(place, *chunks)


def single_forward_body(rows, place, *refs):
    chunks, (out, out_t, lse, whole, values_t) = refs[:GROUPS], refs[GROUPS:]
    i = pl.program_id(0)

    @pl.when(i == 0)
    def _():
        for which, chunk in enumerate(chunks):
            at = place[2 + which]
            whole[at] = chunk[...]
            values_t[at] = flip(chunk[:, :PAIR]).astype(BF16)

    query_t = flip(whole[i, :, PAIR:]).astype(BF16)
    ((o_t, total),) = softmax_sweep(
        i, [(query_t, HD)], lambda j: whole[j, :, :PAIR], lambda j: values_t[j]
    )
    out_t[...] = o_t
    lse[0, 0:1] = total
    tile = jnp.transpose(jnp.concatenate([o_t, jnp.zeros_like(o_t)], axis=0))
    out[...] = pack_half(tile, rows).astype(BF16)


def single_forward(place, chunks, rows):
    per = BLK // rows
    return pl.pallas_call(
        lambda *refs: single_forward_body(rows, *refs),
        grid_spec=pltpu.PrefetchScalarGridSpec(
            num_scalar_prefetch=1,
            grid=(GROUPS,),
            in_specs=[const((BLK, 2 * PAIR))] * GROUPS,
            out_specs=[
                pl.BlockSpec((per, rows // 2, PAIR), lambda i, place: (i, 0, 0)),
                pl.BlockSpec((HD, BLK), lambda i, place: (0, i)),
                pl.BlockSpec((1, 8, BLK), lambda i, place: (i, 0, 0)),
                const((GROUPS, BLK, 2 * PAIR)),
            ],
            scratch_shapes=[pltpu.VMEM((GROUPS, PAIR, BLK), BF16)],
        ),
        out_shape=[
            jax.ShapeDtypeStruct((GROUPS * per, rows // 2, PAIR), BF16),
            jax.ShapeDtypeStruct((HD, GROUPS * BLK), F32),
            jax.ShapeDtypeStruct((GROUPS, 8, BLK), F32),
            jax.ShapeDtypeStruct((GROUPS, BLK, 2 * PAIR), BF16),
        ],
        compiler_params=params(),
        name="attend_single",
    )(place, *chunks)


def unturn_t(part_t, cosine_t, sine_t):
    first, second = part_t[: HD // 2], part_t[HD // 2 :]
    return jnp.concatenate(
        [first * cosine_t + second * sine_t, second * cosine_t - first * sine_t], axis=0
    )


def grads_sweep(i, heads, key_at, value_at, key_t_at, add):
    def visit(j, carry, masked):
        keys, values, keys_t = key_at(j), value_at(j), key_t_at(j)
        ps, dss, out = [], [], []
        for (query_t, grad_t, lse, delta, at), dq in zip(heads, carry):
            p = jnp.exp2(dot(keys, query_t) - lse)
            if masked:
                p = jnp.where(causal(), p, 0.0)
            ds = (p * (dot(values, grad_t) - delta)).astype(BF16)
            ps.append(p.astype(BF16))
            dss.append(ds)
            out.append(dq + dot(keys_t[at : at + HD], ds))
        add(j, ps, dss)
        return tuple(out)

    start = tuple(jnp.zeros((HD, BLK), F32) for _ in heads)
    carry = lax.fori_loop(0, i, lambda j, carry: visit(j, carry, False), start)
    return visit(i, carry, True)


def pair_backward_body(
    rows, whole, grad, out_t, lse, cos_t, sin_t, cosine, sine, out, keys_t, dk, dv
):
    i = pl.program_id(0)
    blocks = whole.shape[0]
    per = BLK // rows

    @pl.when(i == 0)
    def _():
        for b in range(blocks):
            keys_t[b] = flip(whole[b, :, PAIR : 2 * PAIR]).astype(BF16)
        dk[...] = jnp.zeros_like(dk)
        dv[...] = jnp.zeros_like(dv)

    query = whole[i, :, :PAIR]
    do = grad[pl.ds(i * per, per), 0:rows].reshape(BLK, PAIR)
    q_low, q_high = head_masks(flip(query))
    do_t = flip(do)
    do_low, do_high = head_masks(do_t)
    product = do_t * out_t[...]
    low = lanes(BLK) < HD
    wide_q, wide_do = query.astype(F32), do.astype(F32)
    q_rows = jnp.concatenate(
        [jnp.where(low, wide_q, 0.0), jnp.where(low, 0.0, wide_q)], axis=0
    ).astype(BF16)
    do_rows = jnp.concatenate(
        [jnp.where(low, wide_do, 0.0), jnp.where(low, 0.0, wide_do)], axis=0
    ).astype(BF16)

    def add(j, ps, dss):
        dv[j] += dot(jnp.concatenate(ps, axis=1), do_rows)
        dk[j] += dot(jnp.concatenate(dss, axis=1), q_rows)

    heads = [
        (q_low, do_low, lse[0, 0:1], jnp.sum(product[:HD], axis=0, keepdims=True), 0),
        (q_high, do_high, lse[0, 1:2], jnp.sum(product[HD:], axis=0, keepdims=True), HD),
    ]
    dqs = grads_sweep(
        i,
        heads,
        lambda j: whole[j, :, PAIR : 2 * PAIR],
        lambda j: whole[j, :, 2 * PAIR :],
        lambda j: keys_t[j],
        add,
    )
    cos, sin = cos_t[...], sin_t[...]
    dq = jnp.concatenate([unturn_t(part * SCALE, cos, sin) for part in dqs], axis=0)
    out[pl.ds(i * per, per), 0:rows] = jnp.transpose(dq).reshape(per, rows, PAIR).astype(BF16)

    @pl.when(i == blocks - 1)
    def _():
        for b in range(blocks):
            at = pl.ds(b * BLK, BLK)
            back = turn(dk[b] * (1.0 / LOG2E), cosine[at], -sine[at])
            out[b * per : (b + 1) * per, rows : 2 * rows] = back.reshape(per, rows, PAIR).astype(BF16)
            out[b * per : (b + 1) * per, 2 * rows : 3 * rows] = (
                dv[b].reshape(per, rows, PAIR).astype(BF16)
            )


def pair_backward(whole, grad, out_t, lse, cos_t, sin_t, cosine, sine):
    peers, rows = grad.shape[0], grad.shape[1] * 2 // 3
    blocks = whole.shape[0]
    shape = (peers, 3 * rows, PAIR)
    return pl.pallas_call(
        lambda *refs: pair_backward_body(rows, *refs),
        grid=(blocks,),
        in_specs=[
            const(whole.shape),
            const(grad.shape),
            pl.BlockSpec((PAIR, BLK), lambda i: (0, i)),
            pl.BlockSpec((1, 8, BLK), lambda i: (i, 0, 0)),
            pl.BlockSpec((HD // 2, BLK), lambda i: (0, i)),
            pl.BlockSpec((HD // 2, BLK), lambda i: (0, i)),
            const(cosine.shape),
            const(sine.shape),
        ],
        out_specs=const(shape),
        out_shape=jax.ShapeDtypeStruct(shape, BF16),
        scratch_shapes=[
            pltpu.VMEM((blocks, PAIR, BLK), BF16),
            pltpu.VMEM((blocks, BLK, PAIR), F32),
            pltpu.VMEM((blocks, BLK, PAIR), F32),
        ],
        compiler_params=params(),
        name="attend_pair_grads",
    )(whole, grad, out_t, lse, cos_t, sin_t, cosine, sine)


def single_backward_body(
    rows, whole, grad, out_t, lse, cos_t, sin_t, cosine, sine, out, both_t, grads, dboth
):
    i = pl.program_id(0)
    blocks = whole.shape[0]
    per = BLK // rows
    half = rows // 2

    @pl.when(i == 0)
    def _():
        for b in range(blocks):
            both_t[b] = flip(whole[b, :, :PAIR]).astype(BF16)
        grads[...] = unpack_half(grad[:, rows:], rows).reshape(blocks, BLK, PAIR)
        dboth[...] = jnp.zeros_like(dboth)

    wide_q, wide_do = whole[i, :, PAIR:].astype(F32), grads[i].astype(F32)
    q_t = jnp.transpose(wide_q).astype(BF16)
    shifted = swap_heads(wide_do)
    do_t = jnp.transpose(shifted)
    delta = jnp.sum(do_t[HD:] * out_t[...], axis=0, keepdims=True)
    sides = jnp.concatenate([wide_q, shifted], axis=0).astype(BF16)

    def add(j, ps, dss):
        dboth[j] += dot(jnp.concatenate([dss[0], ps[0]], axis=1), sides)

    (dq,) = grads_sweep(
        i,
        [(q_t, do_t.astype(BF16), lse[0, 0:1], delta, 0)],
        lambda j: whole[j, :, :PAIR],
        lambda j: whole[j, :, :PAIR],
        lambda j: both_t[j],
        add,
    )
    dq = unturn_t(dq * SCALE, cos_t[...], sin_t[...])
    tile = jnp.transpose(jnp.concatenate([dq, jnp.zeros_like(dq)], axis=0))
    out[pl.ds(i * per, per), rows : rows + half] = pack_half(tile, rows).astype(BF16)

    @pl.when(i == blocks - 1)
    def _():
        low = lanes(BLK) < HD
        for b in range(blocks):
            at = pl.ds(b * BLK, BLK)
            part = dboth[b]
            back = turn(part * (1.0 / LOG2E), cosine[at], -sine[at])
            out[b * per : (b + 1) * per, 0:rows] = (
                jnp.where(low, back, part).reshape(per, rows, PAIR).astype(BF16)
            )


def single_backward(whole, grad, out_t, lse, cos_t, sin_t, cosine, sine):
    peers, rows = grad.shape[0], grad.shape[1] * 2 // 3
    blocks = whole.shape[0]
    shape = (peers, 3 * rows // 2, PAIR)
    return pl.pallas_call(
        lambda *refs: single_backward_body(rows, *refs),
        grid=(blocks,),
        in_specs=[
            const(whole.shape),
            const(grad.shape),
            pl.BlockSpec((HD, BLK), lambda i: (0, i)),
            pl.BlockSpec((1, 8, BLK), lambda i: (i, 0, 0)),
            pl.BlockSpec((HD // 2, BLK), lambda i: (0, i)),
            pl.BlockSpec((HD // 2, BLK), lambda i: (0, i)),
            const(cosine.shape),
            const(sine.shape),
        ],
        out_specs=const(shape),
        out_shape=jax.ShapeDtypeStruct(shape, BF16),
        scratch_shapes=[
            pltpu.VMEM((blocks, PAIR, BLK), BF16),
            pltpu.VMEM((blocks, BLK, PAIR), BF16),
            pltpu.VMEM((blocks, BLK, PAIR), F32),
        ],
        compiler_params=params(),
        name="attend_single_grads",
    )(whole, grad, out_t, lse, cos_t, sin_t, cosine, sine)


def third_tiles(parts):
    low = lanes(parts[0].shape[0]) < HD
    tiles = []
    for k in (0, 2):
        a, b = parts[k], parts[k + 1]
        top = jnp.where(low, a, swap_heads(b))
        bottom = jnp.where(low, swap_heads(a), b)
        tiles.append(jnp.concatenate([top, bottom], axis=0))
    return tiles


def third_parts(tiles):
    parts = []
    for tile in tiles:
        half = tile.shape[0] // 2
        top, bottom = tile[:half], tile[half:]
        low = lanes(half) < HD
        parts.append(jnp.where(low, top, swap_heads(bottom)))
        parts.append(jnp.where(low, swap_heads(top), bottom))
    return parts


def project_body(pair, single, tok, w_attn, gain, shift, w_query, o, r1, c, cq):
    tiles = [pair[g, 0].astype(F32) for g in range(GROUPS)]
    tiles += third_tiles([single[g, 0].astype(F32) for g in range(GROUPS)])
    heads = jnp.concatenate(tiles, axis=1).astype(BF16)
    o[0] = heads
    after = tok[0].astype(F32) + dot(heads, w_attn[...])
    r1[0] = after
    row = (norm_stats(after)[0] * gain[...][None] + shift[...][None]).astype(BF16)
    c[0] = row
    cq[0] = dot(row, w_query[...]).astype(BF16)


def project_call(pair, single, tokens, w_attn, gain, shift, w_query):
    seqs, rows, _ = tokens.shape
    block = pl.BlockSpec((1, rows, D), lambda s: (s, 0, 0))
    shape = lambda kind: jax.ShapeDtypeStruct((seqs, rows, D), kind)
    return pl.pallas_call(
        project_body,
        grid=(seqs,),
        in_specs=[
            pl.BlockSpec((GROUPS, 1, rows, PAIR), lambda s: (0, s, 0, 0)),
            pl.BlockSpec((GROUPS, 1, rows // 2, PAIR), lambda s: (0, s, 0, 0)),
            block,
            const((D, D)),
            VECTOR,
            VECTOR,
            const((D, D)),
        ],
        out_specs=[block] * 4,
        out_shape=[shape(BF16), shape(F32), shape(BF16), shape(BF16)],
        compiler_params=params(),
        name="project",
    )(
        pair.reshape(GROUPS, seqs, rows, PAIR),
        single.reshape(GROUPS, seqs, rows // 2, PAIR),
        tokens,
        w_attn,
        gain,
        shift,
        w_query,
    )


def memory_body(near, weight, out):
    out[...] = dot(near[...], weight[...]).astype(BF16)


def memory_call(near, weight):
    rows = near.shape[0]
    step = min(rows, 512)
    return pl.pallas_call(
        memory_body,
        grid=(rows // step,),
        in_specs=[pl.BlockSpec((step, D), lambda i: (i, 0)), const((D, 2 * D))],
        out_specs=pl.BlockSpec((step, 2 * D), lambda i: (i, 0)),
        out_shape=jax.ShapeDtypeStruct((rows, 2 * D), BF16),
        compiler_params=params(),
        name="memory",
    )(near, weight)


def move_later(values, before):
    first = lax.broadcasted_iota(jnp.int32, values.shape, 0) == 0
    return jnp.where(first, before.astype(F32), pltpu.roll(values.astype(F32), 1, 0))


def move_earlier(values, after):
    rows = values.shape[0]
    last = lax.broadcasted_iota(jnp.int32, values.shape, 0) == rows - 1
    return jnp.where(last, after.astype(F32), pltpu.roll(values.astype(F32), rows - 1, 0))


def head_rows(tile):
    low = lanes(GROUP) < HD
    return jnp.concatenate(
        [jnp.where(low, tile, 0.0), jnp.where(low, 0.0, tile)], axis=0
    ).astype(BF16)


def fold_rows(both):
    return jnp.where(lanes(GROUP) < HD, both[:GROUP], both[GROUP:])


def cross_scores(keys, query_rows, have):
    scores = dot_nt(keys, query_rows) * (SCALE * LOG2E)
    row = lax.broadcasted_iota(jnp.int32, scores.shape, 0)
    kept = jnp.where(row < RET, have[0], have[1]) > 0
    return jnp.where(kept, scores, NEGATIVE), kept


def row_heads(row):
    return jnp.where(diagonal(), row, 0.0).astype(BF16)


def diagonal():
    head = lax.broadcasted_iota(jnp.int32, (16, D), 1) // HD
    return head == lax.broadcasted_iota(jnp.int32, (16, D), 0)


def own_heads(wide):
    return jnp.sum(jnp.where(diagonal(), wide, 0.0), axis=0, keepdims=True)


def softmax_columns(scores, kept):
    peak = jnp.max(scores, axis=0, keepdims=True)
    weights = jnp.where(kept, jnp.exp2(scores - peak), 0.0)
    total = jnp.sum(weights, axis=0, keepdims=True)
    some = total > 0.0
    safe = jnp.where(some, total, 1.0)
    return weights / safe, jnp.where(some, peak + jnp.log2(safe), 0.0)


def each_window(windows, visit):
    count = 4 if windows % 4 == 0 else 1

    def step(i, _):
        for k in range(count):
            visit(i * count + k, 0)
        return 0

    lax.fori_loop(0, windows // count, step, 0)


def cross_body(windows, present, present_next, cq, memory, memory_next, out, lse, shifted, win):
    s = pl.program_id(0)
    rows = cq.shape[1]
    zero = jnp.zeros((1, D), F32)
    wide = cq[0].astype(F32)
    shifted[...] = move_later(wide, zero).reshape(windows, GROUP, D)

    def window(w, _):
        have = [present[s, w, k] for k in range(NEIGH)]
        for p in range(HEADS // 2):
            at = pl.ds(p * PAIR, PAIR)
            keys = memory[0, w, :, p * PAIR : (p + 1) * PAIR]
            values = memory[0, w, :, D + p * PAIR : D + (p + 1) * PAIR]
            ca, logs = softmax_columns(*cross_scores(keys, head_rows(shifted[w, :, at]), have))
            win[w, :, at] = fold_rows(jnp.transpose(dot_tn(values, ca.astype(BF16))))
            lse[0, w, p : p + 1] = logs
        return 0

    each_window(windows, window)
    have = [present_next[s, k] for k in range(NEIGH)]
    ca, _ = softmax_columns(
        *cross_scores(memory_next[0, :, :D], row_heads(wide[rows - 1 :]), have)
    )
    last = own_heads(dot_tn(ca.astype(BF16), memory_next[0, :, D:]))
    out[0] = move_earlier(win[...].reshape(rows, D), last).astype(BF16)


def cross_call(present, present_next, cq, memory, memory_next):
    seqs, windows = present.shape[:2]
    rows = cq.shape[1]
    keys = NEIGH * RET
    block = pl.BlockSpec((1, rows, D), lambda s: (s, 0, 0))
    return pl.pallas_call(
        lambda *refs: cross_body(windows, *refs),
        grid=(seqs,),
        in_specs=[
            pl.BlockSpec(memory_space=pltpu.SMEM),
            pl.BlockSpec(memory_space=pltpu.SMEM),
            block,
            pl.BlockSpec((1, windows, keys, 2 * D), lambda s: (s, 0, 0, 0)),
            pl.BlockSpec((1, keys, 2 * D), lambda s: (s, 0, 0)),
        ],
        out_specs=[block, pl.BlockSpec((1, windows, 8, PAIR), lambda s: (s, 0, 0, 0))],
        out_shape=[
            jax.ShapeDtypeStruct((seqs, rows, D), BF16),
            jax.ShapeDtypeStruct((seqs, windows, 8, PAIR), F32),
        ],
        scratch_shapes=[pltpu.VMEM((windows, GROUP, D), F32)] * 2,
        compiler_params=params(),
        name="cross",
    )(present, present_next, cq, memory, memory_next)


def gelu_parts(u):
    phi = 0.5 + 0.5 * lax.erf(u * math.sqrt(0.5))
    slope = phi + u * (jnp.exp2(u * u * (-0.5 * LOG2E)) * (1.0 / math.sqrt(2.0 * math.pi)))
    return u * phi, slope


def feed_body(
    steps,
    r1,
    cross_rows,
    cot,
    w_cross,
    gain,
    shift,
    w_up,
    w_down,
    output,
    d2,
    e2,
    dr,
    vectors,
    grads,
    normed,
    inverse,
    row,
    row_t,
    total,
    grad,
    up_stage,
    down_stage,
    sems,
):
    f = pl.program_id(0)
    seqs, rows = r1.shape[:2]
    batch, sq, groups, _, own, cols = grads.shape
    near = down_stage.shape[2]

    def copies(at):
        slot = lax.rem(at, 2)
        first = at * near
        return (
            pltpu.make_async_copy(up_stage.at[slot], grads.at[at, :, :, 0], sems.at[slot, 0]),
            pltpu.make_async_copy(
                down_stage.at[slot],
                grads.at[:, pl.ds(lax.rem(first, sq), near), first // sq, 1],
                sems.at[slot, 1],
            ),
        )

    @pl.when(f == 0)
    def _():
        for s in range(seqs):
            at = pl.ds(s * rows, rows)
            r2 = r1[s] + dot(cross_rows[s], w_cross[...])
            total[at] = r2
            n, inv = norm_stats(r2)
            normed[at] = n
            inverse[at] = inv
            a3 = (n * gain[...][None] + shift[...][None]).astype(BF16)
            row[at] = a3
            row_t[:, at] = flip(a3).astype(BF16)
        grad[...] = jnp.zeros_like(grad)

    up, down = w_up[...], w_down[...]
    given = cot[...]
    act, slope = gelu_parts(dot(row[...], up))
    act_low = act.astype(BF16)
    total[...] += dot(act_low, down)
    gu = (dot_nt(given, down) * slope).astype(BF16)
    grad[...] += dot_nt(gu, up)
    part = dot(row_t[...], gu).astype(BF16)
    part_down = dot(flip(act).astype(BF16), given).astype(BF16)

    @pl.when(f >= 2)
    def _():
        for copy in copies(f - 2):
            copy.wait()

    slot = lax.rem(f, 2)
    for g in range(groups):
        for q in range(sq):
            start = (g * sq + q) * own
            up_stage[slot, q, g] = part[start : start + own]
    deep = own * cols // D
    for q in range(near):
        for b in range(batch):
            start = (q * batch + b) * deep
            for x in range(D // cols):
                down_stage[slot, b, q, x * deep : (x + 1) * deep] = part_down[
                    start : start + deep, x * cols : (x + 1) * cols
                ]
    for copy in copies(f):
        copy.start()

    @pl.when(f == steps - 1)
    def _():
        output[...] = total[...].astype(BF16)
        n, back = normed[...], grad[...]
        vectors[0:1] = jnp.sum(n * back, axis=0, keepdims=True)
        vectors[1:2] = jnp.sum(back, axis=0, keepdims=True)
        summed = given.astype(F32) + norm_back(n, inverse[...], gain[...][None], back)
        d2[...] = summed
        low = summed.astype(BF16)
        e2[...] = low
        dr[...] = dot_nt(low, w_cross[...]).astype(BF16)
        for at in (steps - 2, steps - 1):
            for copy in copies(at):
                copy.wait()


def feed_call(r1, cross_rows, cot, w_cross, gain, shift, w_up, w_down, batch, peers):
    seqs, rows, _ = r1.shape
    count = seqs * rows
    sq = peers // GROUPS
    steps = batch
    cols = FF // steps
    own = D // peers
    near = peers // batch
    flat = jax.ShapeDtypeStruct((count, D), BF16)
    wide = jax.ShapeDtypeStruct((count, D), F32)
    return pl.pallas_call(
        lambda *refs: feed_body(steps, *refs),
        grid=(steps,),
        in_specs=[
            const((seqs, rows, D)),
            const((seqs, rows, D)),
            const((count, D)),
            const((D, D)),
            VECTOR,
            VECTOR,
            pl.BlockSpec((D, cols), lambda f: (0, f)),
            pl.BlockSpec((cols, D), lambda f: (f, 0)),
        ],
        out_specs=[const((count, D))] * 4
        + [const((8, D)), pl.BlockSpec(memory_space=pl.ANY)],
        out_shape=[
            flat,
            wide,
            flat,
            flat,
            jax.ShapeDtypeStruct((8, D), F32),
            jax.ShapeDtypeStruct((batch, sq, GROUPS, 2, own, cols), BF16),
        ],
        scratch_shapes=[
            pltpu.VMEM((count, D), F32),
            pltpu.VMEM((count, 1), F32),
            pltpu.VMEM((count, D), BF16),
            pltpu.VMEM((D, count), BF16),
            pltpu.VMEM((count, D), F32),
            pltpu.VMEM((count, D), F32),
            pltpu.VMEM((2, sq, GROUPS, own, cols), BF16),
            pltpu.VMEM((2, batch, near, own, cols), BF16),
            pltpu.SemaphoreType.DMA((2, 2)),
        ],
        compiler_params=params(),
        name="feed",
    )(r1, cross_rows, cot, w_cross, gain, shift, w_up, w_down)


def cross_back_body(
    windows, present, present_next, cq, dr, memory, memory_next, lse, dmem, dcq, shifted, dwin, dshifted
):
    s = pl.program_id(0)
    rows = cq.shape[1]
    zero = jnp.zeros((1, D), F32)
    wide, wide_dr = cq[0].astype(F32), dr[0].astype(F32)
    shifted[...] = move_later(wide, zero).reshape(windows, GROUP, D)
    dwin[...] = move_later(wide_dr, zero).reshape(windows, GROUP, D)

    def window(w, _):
        have = [present[s, w, k] for k in range(NEIGH)]
        for p in range(HEADS // 2):
            at = pl.ds(p * PAIR, PAIR)
            keys = memory[0, w, :, p * PAIR : (p + 1) * PAIR]
            values = memory[0, w, :, D + p * PAIR : D + (p + 1) * PAIR]
            query_rows = head_rows(shifted[w, :, at])
            grad_rows = head_rows(dwin[w, :, at])
            scores, kept = cross_scores(keys, query_rows, have)
            ca = jnp.where(kept, jnp.exp2(scores - lse[0, w, p : p + 1]), 0.0)
            dca = dot_nt(values, grad_rows)
            inner = jnp.sum(ca * dca, axis=0, keepdims=True)
            dcs = (ca * (dca - inner)).astype(BF16)
            dmem[0, w, :, at] = (dot(dcs, query_rows) * SCALE).astype(BF16)
            dmem[0, w, :, pl.ds(D + p * PAIR, PAIR)] = dot(ca.astype(BF16), grad_rows).astype(BF16)
            dshifted[w, :, at] = fold_rows(jnp.transpose(dot_tn(keys, dcs))) * SCALE
        return 0

    each_window(windows, window)
    have = [present_next[s, k] for k in range(NEIGH)]
    _, dcs, _ = row_grads(memory_next[0], wide[rows - 1 :], wide_dr[rows - 1 :], have)
    last = own_heads(dot_tn(dcs, memory_next[0, :, :D])) * SCALE
    dcq[0] = move_earlier(dshifted[...].reshape(rows, D), last).astype(BF16)


def row_grads(memory, row, grad, have):
    query_rows, grad_rows = row_heads(row), row_heads(grad)
    ca, _ = softmax_columns(*cross_scores(memory[:, :D], query_rows, have))
    dca = dot_nt(memory[:, D:], grad_rows)
    inner = jnp.sum(ca * dca, axis=0, keepdims=True)
    return ca.astype(BF16), (ca * (dca - inner)).astype(BF16), (query_rows, grad_rows)


def cross_back_call(present, present_next, cq, dr, memory, memory_next, lse):
    seqs, windows = present.shape[:2]
    rows = cq.shape[1]
    keys = NEIGH * RET
    block = pl.BlockSpec((1, rows, D), lambda s: (s, 0, 0))
    wide = pl.BlockSpec((1, windows, keys, 2 * D), lambda s: (s, 0, 0, 0))
    return pl.pallas_call(
        lambda *refs: cross_back_body(windows, *refs),
        grid=(seqs,),
        in_specs=[
            pl.BlockSpec(memory_space=pltpu.SMEM),
            pl.BlockSpec(memory_space=pltpu.SMEM),
            block,
            block,
            wide,
            pl.BlockSpec((1, keys, 2 * D), lambda s: (s, 0, 0)),
            pl.BlockSpec((1, windows, 8, PAIR), lambda s: (s, 0, 0, 0)),
        ],
        out_specs=[wide, block],
        out_shape=[
            jax.ShapeDtypeStruct((seqs, windows, keys, 2 * D), BF16),
            jax.ShapeDtypeStruct((seqs, rows, D), BF16),
        ],
        scratch_shapes=[pltpu.VMEM((windows, GROUP, D), F32)] * 3,
        compiler_params=params(),
        name="cross_grads",
    )(present, present_next, cq, dr, memory, memory_next, lse)


def project_back_body(dcq, r1, d2, w_query, gain, w_attn, do, d1, e1, vectors):
    s = pl.program_id(0)
    rows = r1.shape[1]
    back = dot_nt(dcq[0], w_query[...])
    normed, inverse = norm_stats(r1[0])

    @pl.when(s == 0)
    def _():
        vectors[...] = jnp.zeros_like(vectors)

    vectors[0:1] += jnp.sum(normed * back, axis=0, keepdims=True)
    vectors[1:2] += jnp.sum(back, axis=0, keepdims=True)
    summed = d2[0] + norm_back(normed, inverse, gain[...][None], back)
    d1[0] = summed
    low = summed.astype(BF16)
    e1[0] = low
    heads = dot_nt(low, w_attn[...])
    for g in range(GROUPS):
        do[g, 0, 0:rows] = heads[:, g * PAIR : (g + 1) * PAIR].astype(BF16)
    tiles = [heads[:, (GROUPS + k) * PAIR : (GROUPS + k + 1) * PAIR] for k in range(2)]
    for g, part in enumerate(third_parts(tiles)):
        do[g, 0, rows:] = part.astype(BF16)


def project_back_call(dcq, r1, d2, w_query, gain, w_attn):
    seqs, rows, _ = r1.shape
    block = pl.BlockSpec((1, rows, D), lambda s: (s, 0, 0))
    shape = lambda kind: jax.ShapeDtypeStruct((seqs, rows, D), kind)
    return pl.pallas_call(
        project_back_body,
        grid=(seqs,),
        in_specs=[
            block,
            block,
            block,
            const((D, D)),
            VECTOR,
            const((D, D)),
        ],
        out_specs=[
            pl.BlockSpec((GROUPS, 1, rows + rows // 2, PAIR), lambda s: (0, s, 0, 0)),
            block,
            block,
            const((8, D)),
        ],
        out_shape=[
            jax.ShapeDtypeStruct((GROUPS, seqs, rows + rows // 2, PAIR), BF16),
            shape(F32),
            shape(BF16),
            jax.ShapeDtypeStruct((8, D), F32),
        ],
        compiler_params=params(),
        name="project_grads",
    )(dcq, r1, d2, w_query, gain, w_attn)


def put_rows(place, outs, block, value):
    batch, groups, part, _ = outs[0].shape[:1] + outs[0].shape[-3:]
    sq = 2 if len(outs) == 2 else outs[0].shape[1]
    own = D // (sq * groups)
    value = value.astype(BF16)

    def store(q, slot):
        for g in range(groups):
            start, done = block * own, 0
            at = (g * sq + q) * own
            while done < own:
                b, x = divmod(start + done, part)
                count = min(part - x, own - done)
                slot(b, g, x, count, value[at + done : at + done + count])
                done += count

    for q in range(sq):
        if len(outs) == 1:

            def put(b, g, x, count, rows, q=q):
                outs[0][b, q, g, x : x + count] = rows

            store(q, put)
            continue
        for k, out in enumerate(outs):

            @pl.when(place[1] == q ^ k)
            def _(q=q, out=out):
                def put(b, g, x, count, rows):
                    out[b, g, x : x + count] = rows

                store(q, put)


def others_body(
    own,
    per_sequence,
    place,
    present,
    near,
    dmem,
    memory,
    before,
    w_memory,
    o,
    e1,
    c_far,
    dq_far,
    cross_far,
    e2_far,
    dnear,
    *refs,
):
    outs, (acc, grads, c, dq, cross_rows, e2, sems) = refs[:-7], refs[-7:]
    i = pl.program_id(0)
    copies = [
        pltpu.make_async_copy(source, target, sems.at[k])
        for k, (source, target) in enumerate(
            ((c_far, c), (dq_far, dq), (cross_far, cross_rows), (e2_far, e2))
        )
    ]

    @pl.when(i == 0)
    def _():
        for copy in copies:
            copy.start()
        acc[...] = jnp.zeros_like(acc)

    grads[...] = dmem[...].reshape(grads.shape)

    @pl.when(lax.rem(i, per_sequence) == 0)
    def _():
        keys = memory.shape[2]
        edge = edge_grads(
            memory[0, 0],
            before[0, 0:1].astype(F32),
            before[0, 1:2].astype(F32),
            [present[i // per_sequence, 0, k] for k in range(NEIGH)],
        )
        grads[0:keys] = (dmem[0, 0].astype(F32) + edge).astype(BF16)

    dnear[...] = dot_nt(grads[...], w_memory[...]).astype(BF16)
    acc[...] += dot_tn(near[...], grads[...])

    @pl.when(i == 0)
    def _():
        put_rows(place, outs, 0, dot_tn(o[...], e1[...]))

    @pl.when(i == pl.num_programs(0) - 1)
    def _():
        for copy in copies:
            copy.wait()
        put_rows(place, outs, 1, dot_tn(c[...], dq[...]))
        put_rows(place, outs, 2, dot_tn(cross_rows[...], e2[...]))
        put_rows(place, outs, 3, acc[:, :D])
        put_rows(place, outs, 4, acc[:, D:])
        batch, groups, size = outs[0].shape[0], outs[0].shape[-3], outs[0].shape[-2]
        used = 5 * own - (batch - 1) * size
        for out in outs:
            for at in itertools.product(*map(range, out.shape[1:-2])):
                out[(batch - 1, *at, slice(used, size))] = jnp.zeros((size - used, D), BF16)


def edge_grads(memory, row, grad, have):
    ca, dcs, (query_rows, grad_rows) = row_grads(memory, row, grad, have)
    return jnp.concatenate([dot(dcs, query_rows) * SCALE, dot(ca, grad_rows)], axis=1)


def others_call(
    split,
    place,
    present,
    near,
    dmem,
    memory,
    before,
    w_memory,
    o,
    e1,
    c,
    dq,
    cross_rows,
    e2,
    batch,
    peers,
):
    seqs, windows, keys, _ = dmem.shape
    count = o.shape[0]
    size = min(2, windows)
    steps = windows // size
    own = D // peers
    part = (5 * own + own // 3) // batch
    shapes = [(batch, peers // GROUPS, GROUPS, part, D)]
    if split:
        shapes = [(batch, GROUPS, part, D)] * 2
    smem = pl.BlockSpec(memory_space=pltpu.SMEM)
    far = pl.BlockSpec(memory_space=pl.ANY)
    block = pl.BlockSpec((size * keys, D), lambda i: (i, 0))
    return pl.pallas_call(
        lambda *refs: others_body(own, steps, *refs),
        grid=(seqs * steps,),
        in_specs=[
            smem,
            smem,
            block,
            pl.BlockSpec((1, size, keys, 2 * D), lambda i: (i // steps, lax.rem(i, steps), 0, 0)),
            pl.BlockSpec((1, 1, keys, 2 * D), lambda i: (i // steps, 0, 0, 0)),
            pl.BlockSpec((1, 2, D), lambda i: (i // steps, 0, 0)),
            const((D, 2 * D)),
            const((count, D)),
            const((count, D)),
            far,
            far,
            far,
            far,
        ],
        out_specs=[block] + [const(shape) for shape in shapes],
        out_shape=[jax.ShapeDtypeStruct(near.shape, BF16)]
        + [jax.ShapeDtypeStruct(shape, BF16) for shape in shapes],
        scratch_shapes=[
            pltpu.VMEM((D, 2 * D), F32),
            pltpu.VMEM((size * keys, 2 * D), BF16),
        ]
        + [pltpu.VMEM((count, D), BF16)] * 4
        + [pltpu.SemaphoreType.DMA((4,))],
        compiler_params=params(),
        name="other_grads",
    )(
        place,
        present,
        near,
        dmem,
        memory,
        before,
        w_memory,
        o,
        e1,
        c,
        dq,
        cross_rows,
        e2,
    )


def last_body(pair, single, tok, d1, gain, w_qkv, out):
    rows = tok.shape[1]
    half = rows // 2
    low = lanes(rows) < HD
    boths = [single[g, 0, 0:rows].astype(F32) for g in range(GROUPS)]
    queries = third_tiles([single[g, 0, rows : rows + half].astype(F32) for g in range(GROUPS)])
    keys = [jnp.where(low, boths[k], swap_heads(boths[k + 1])) for k in (0, 2)]
    values = [jnp.where(low, swap_heads(boths[k]), boths[k + 1]) for k in (0, 2)]
    parts = []
    for at, third in ((0, queries), (rows, keys), (2 * rows, values)):
        parts += [pair[g, 0, at : at + rows] for g in range(GROUPS)]
        parts += [tile.astype(BF16) for tile in third]
    back = dot_nt(jnp.concatenate(parts, axis=1), w_qkv[...])
    normed, inverse = norm_stats(tok[0].astype(F32))
    out[0] = (d1[0] + norm_back(normed, inverse, gain[...][None], back)).astype(BF16)


def last_call(pair, single, tokens, d1, gain, w_qkv):
    seqs, rows, _ = tokens.shape
    block = pl.BlockSpec((1, rows, D), lambda s: (s, 0, 0))
    return pl.pallas_call(
        last_body,
        grid=(seqs,),
        in_specs=[
            pl.BlockSpec((GROUPS, 1, 3 * rows, PAIR), lambda s: (0, s, 0, 0)),
            pl.BlockSpec((GROUPS, 1, 3 * rows // 2, PAIR), lambda s: (0, s, 0, 0)),
            block,
            block,
            VECTOR,
            const((D, 3 * D)),
        ],
        out_specs=block,
        out_shape=jax.ShapeDtypeStruct((seqs, rows, D), BF16),
        compiler_params=params(),
        name="token_grads",
    )(
        pair.reshape(GROUPS, seqs, 3 * rows, PAIR),
        single.reshape(GROUPS, seqs, 3 * rows // 2, PAIR),
        tokens,
        d1,
        gain,
        w_qkv,
    )


def heads_body(place, *refs):
    pieces, refs = refs[:GROUPS], refs[GROUPS:]
    (pair, single, gain, shift, one, two), refs = refs[:6], refs[6:]
    weights, (out, acc, sums, held) = refs[:6], refs[6:]
    i = pl.program_id(0)
    per, rows = pair.shape[0], pair.shape[1] // 3
    for k, piece in enumerate(pieces):

        @pl.when(i == k)
        def _(piece=piece):
            held[...] = piece[...]

    third = unpack_half(single[:, rows : rows + rows // 2], rows)
    grads = jnp.concatenate(
        [pair[:, k * rows : (k + 1) * rows].reshape(per * rows, PAIR) for k in range(3)]
        + [single[:, 0:rows].reshape(per * rows, PAIR), third],
        axis=1,
    )
    part = dot_tn(held[...], grads)
    total = jnp.sum(grads.astype(F32), axis=0, keepdims=True)

    @pl.when(i == 0)
    def _():
        acc[...] = part
        sums[0:1] = total

    @pl.when(i > 0)
    def _():
        acc[...] += part
        sums[0:1] += total

    @pl.when(i == pl.num_programs(0) - 1)
    def _():
        low = lanes(D) < HD
        odd = lax.rem(place[0], 2) == 1
        wide = [weight[...].astype(F32) for weight in weights]
        q3, k3, v3 = [jnp.where(odd, swap_heads(t), t) for t in wide[3:]]
        columns = wide[:3] + [jnp.where(low, k3, swap_heads(v3)), jnp.where(low, q3, 0.0)]
        columns = jnp.concatenate(columns, axis=1)
        whole, over = acc[...], sums[0:1]
        d_gain = jnp.sum(whole * columns, axis=1, keepdims=True)
        d_shift = jnp.sum(over * columns, axis=1, keepdims=True)
        lane = lax.broadcasted_iota(jnp.int32, whole.shape, 1)
        flipped = jnp.transpose(
            jnp.concatenate(
                [gain[...][None], shift[...][None], one[0:2], two[0:2], jnp.zeros((2, D), F32)], axis=0
            )
        )
        value = whole * flipped[:, 0:1] + flipped[:, 1:2] * over
        at = 4 * PAIR + HD
        value = jnp.where(lane == at, d_gain, jnp.where(lane == at + 1, d_shift, value))
        for n in range(2, 6):
            value = jnp.where(lane == at + n, flipped[:, n : n + 1], value)
        high, low, sq, groups, own, _ = out.shape
        for g in range(groups):
            for q in range(sq):
                for b in range(high * low):
                    start = ((g * sq + q) * high * low + b) * own
                    out[b // low, b % low, q, g] = value[start : start + own].astype(BF16)


def heads_call(place, pieces, pair, single, gain, shift, one, two, weight, batch):
    peers, rows = pair.shape[0], pair.shape[1] // 3
    per = peers // GROUPS
    shape = (batch // 2, 2, per, GROUPS, D // peers // batch, 5 * PAIR)

    def chunk(i, place):
        return (place[2 + i], 0, 0)

    return pl.pallas_call(
        heads_body,
        grid_spec=pltpu.PrefetchScalarGridSpec(
            num_scalar_prefetch=1,
            grid=(GROUPS,),
            in_specs=[const((per * rows, D))] * GROUPS
            + [
                pl.BlockSpec((per, 3 * rows, PAIR), chunk),
                pl.BlockSpec((per, 3 * rows // 2, PAIR), chunk),
                VECTOR,
                VECTOR,
                const((8, D)),
                const((8, D)),
            ]
            + head_columns(0),
            out_specs=const(shape),
            scratch_shapes=[
                pltpu.VMEM((D, 5 * PAIR), F32),
                pltpu.VMEM((8, 5 * PAIR), F32),
                pltpu.VMEM((per * rows, D), BF16),
            ],
        ),
        out_shape=jax.ShapeDtypeStruct(shape, BF16),
        compiler_params=params(),
        name="qkv_grads",
    )(place, *pieces, pair, single, gain, shift, one, two, *[weight] * 6)


SEQ = ("hg", "sq")
BATCH = ("by", "bx")


def from_behind(value, by):
    peers = lax.axis_size(SEQ)
    pairs = [(i, i + by) for i in range(peers) if 0 <= i + by < peers]
    return lax.ppermute(value, SEQ, pairs)


def swap_all(value):
    return lax.all_to_all(value, SEQ, 0, 0, tiled=True)


def add_rows(value):
    flat = value.reshape((value.shape[0] * value.shape[1],) + value.shape[2:])
    own = lax.psum_scatter(flat, BATCH + ("sq",), scatter_dimension=0, tiled=True)
    return own.reshape(value.shape[2:])


def rotated(value, by):
    return lax.ppermute(value, "hg", [(i, (i + by) % GROUPS) for i in range(GROUPS)])


def add_groups(own):
    here = lax.axis_index("hg")
    total = lax.dynamic_index_in_dim(own, here, 0, keepdims=False).astype(F32)
    for k in range(1, GROUPS):
        part = lax.dynamic_index_in_dim(own, lax.rem(here + k, GROUPS), 0, keepdims=False)
        total += rotated(part, k).astype(F32)
    return total.astype(BF16)


def gather_groups(own):
    here = lax.axis_index("hg")
    pieces = [lax.dynamic_index_in_dim(own, here, 0, keepdims=False)]
    for k in range(1, GROUPS):
        part = lax.dynamic_index_in_dim(own, lax.rem(here + k, GROUPS), 0, keepdims=False)
        pieces.append(rotated(part, k))
    return in_order([pieces[(-j) % GROUPS] for j in range(GROUPS)], here, "shift")


def passed(value, by):
    pairs = [(i, i + by) for i in range(GROUPS) if 0 <= i + by < GROUPS]
    return lax.ppermute(value, "hg", pairs)


def in_order(pieces, here, how):
    count = len(pieces)
    out = []
    for j in range(count):
        value = pieces[j]
        for me in range(1, count):
            at = (j - me) % count if how == "shift" else j ^ me
            value = jnp.where(here == me, pieces[at], value)
        out.append(value)
    return out


def gather_batch(value):
    size = lax.axis_size(BATCH)
    pieces = [value] + [
        lax.ppermute(value, BATCH, [(i, i ^ k) for i in range(size)]) for k in range(1, size)
    ]
    return in_order(pieces, lax.axis_index(BATCH), "xor")


def halve(value, name, axis):
    if lax.axis_size(name) == 2:
        here = lax.axis_index(name)
        kept = lax.dynamic_index_in_dim(value, here, axis, keepdims=False)
        given = lax.dynamic_index_in_dim(value, 1 - here, axis, keepdims=False)
        got = lax.ppermute(given, name, [(0, 1), (1, 0)])
        return (kept.astype(F32) + got.astype(F32)).astype(BF16)
    parts = lax.all_to_all(value, name, axis, 0, tiled=False)
    return jnp.sum(parts.astype(F32), axis=0).astype(BF16)


def own_sequence(value):
    if lax.axis_size("sq") == 2:
        here = lax.axis_index("sq")
        kept = lax.dynamic_index_in_dim(value, here, 0, keepdims=False)
        given = lax.dynamic_index_in_dim(value, 1 - here, 0, keepdims=False)
        return [kept, lax.ppermute(given, "sq", [(0, 1), (1, 0)])]
    return [lax.all_to_all(value, "sq", 0, 0, tiled=True)]


def together(*values):
    return lax.optimization_barrier(values)


def shards(
    tokens,
    neighbours,
    present,
    qkv_weight,
    attn_weight,
    query_weight,
    memory_weight,
    cross_weight,
    up_weight,
    down_weight,
    attn_gain,
    attn_shift,
    cross_gain,
    cross_shift,
    mlp_gain,
    mlp_shift,
    cotangent,
):
    seqs, rows = tokens.shape[:2]
    count = seqs * rows
    peers = lax.axis_size(SEQ)
    batch = lax.axis_size(BATCH)
    easy = [lax.axis_size(name) for name in ("by", "bx", "sq")] == [2, 2, 2]
    group, core = lax.axis_index("hg"), lax.axis_index("sq")
    place = jnp.stack([group, core] + [chunk_of(which, group) for which in range(GROUPS)])
    place = place.astype(jnp.int32)
    cos_np, sin_np = rope_tables(peers * rows)
    cosine, sine = jnp.asarray(cos_np), jnp.asarray(sin_np)
    cos_t = jnp.asarray(np.ascontiguousarray(cos_np[:, : HD // 2].T))
    sin_t = jnp.asarray(np.ascontiguousarray(sin_np[:, HD // 2 : HD].T))

    windows = present.shape[1]
    keys = NEIGH * RET
    near = neighbours.reshape(-1, D)

    def chunk(which, first, second):
        return chunk_call(
            which, place, first, second, attn_gain, attn_shift, qkv_weight, cosine, sine
        )

    own = own_sequence(tokens)
    behind, ahead = [passed(part, 1) for part in own], [passed(part, -1) for part in own]
    chunks = [chunk(0, own, own)]
    chunks[0], behind[0], ahead[0] = together(chunks[0], behind[0], ahead[0])
    behind_two = [passed(part, 1) for part in behind]
    ahead_two = [passed(part, -1) for part in ahead]
    memory = memory_call(near, memory_weight)
    memory, behind_two[0], ahead_two[0] = together(memory, behind_two[0], ahead_two[0])
    chunks.append(chunk(1, ahead, behind))
    chunks[1], behind_two[-1], ahead_two[-1] = together(chunks[1], behind_two[-1], ahead_two[-1])
    behind_three = [passed(part, 1) for part in behind_two]
    ahead_three = [passed(part, -1) for part in ahead_two]
    chunks.append(chunk(2, ahead_two, behind_two))
    chunks[2], behind_three, ahead_three = together(chunks[2], behind_three, ahead_three)
    last = [jnp.where(group == GROUPS - 1, x, y) for x, y in zip(behind_three, behind)]
    chunks.append(chunk(3, ahead_three, last))
    memory = memory.reshape(seqs, windows, keys, 2 * D)
    near_next, chunks[3] = together(neighbours[:, 0].reshape(seqs * keys, D), chunks[3])
    near_next = from_behind(near_next, -1)
    present_next = from_behind(present[:, 0], -1)
    pieces = [chunk[0] for chunk in chunks]
    o_pair, o_pair_t, lse_pair, pairs = pair_forward(place, [chunk[1] for chunk in chunks])
    singles, o_pair, near_next = together([chunk[2] for chunk in chunks], o_pair, near_next)
    memory_next = memory_call(near_next, memory_weight).reshape(seqs, keys, 2 * D)
    o_pair = swap_all(o_pair.reshape(peers, rows, PAIR))
    o_single, o_single_t, lse_single, singles = single_forward(place, singles, rows)
    o_single, o_pair = together(o_single, o_pair)
    o_single = swap_all(o_single)
    o_single, memory_next = together(o_single, memory_next)
    o, r1, c, cq = project_call(
        o_pair, o_single, tokens, attn_weight, cross_gain, cross_shift, query_weight
    )
    cross_rows, lse = cross_call(present, present_next, cq, memory, memory_next)
    output, d2, e2, dr, mlp_vectors, feed = feed_call(
        r1,
        cross_rows,
        cotangent.reshape(count, D),
        cross_weight,
        mlp_gain,
        mlp_shift,
        up_weight,
        down_weight,
        batch,
        peers,
    )
    dr = dr.reshape(seqs, rows, D)
    before = from_behind(jnp.concatenate([cq[:, -1:], dr[:, -1:]], axis=1), 1)
    feed, before = together(feed, before)
    feed = add_rows(feed)
    dmem, dq = cross_back_call(present, present_next, cq, dr, memory, memory_next, lse)
    do, d1, e1, cross_vectors = project_back_call(
        dq, r1, d2.reshape(seqs, rows, D), query_weight, cross_gain, attn_weight
    )
    do = swap_all(do.reshape(peers, 3 * rows // 2, PAIR))
    own = D // peers
    dnear, *others = others_call(
        easy,
        place,
        present,
        near,
        dmem,
        memory,
        before,
        memory_weight,
        o.reshape(count, D),
        e1.reshape(count, D),
        c.reshape(count, D),
        dq.reshape(count, D),
        cross_rows.reshape(count, D),
        e2,
        batch,
        peers,
    )
    do, others = together(do, others)
    if easy:
        kept, given = others
        got = lax.ppermute(given, "sq", [(0, 1), (1, 0)])
    else:
        others = add_rows(others[0])
    d_single = single_backward(singles, do, o_single_t, lse_single, cos_t, sin_t, cosine, sine)
    do, d_single = together(do, d_single)
    d_single_all = swap_all(d_single)
    do, feed = together(do, feed)
    feed = lax.psum_scatter(feed, "hg", scatter_dimension=0, tiled=False)
    d_pair = pair_backward(pairs, do, o_pair_t, lse_pair, cos_t, sin_t, cosine, sine)
    d_pair_all, d_single_all = together(d_pair, d_single_all)
    d_pair_all = swap_all(d_pair_all)
    if easy:
        d_pair, kept, got = together(d_pair, kept, got)
        others = (kept.astype(F32) + got.astype(F32)).astype(BF16)
        others = others.reshape((2, 2) + others.shape[1:])
        cut = GROUPS // 2
        others = [halve(others[:, :, :cut], "bx", 1), halve(others[:, :, cut:], "by", 0)]
    g_qkv = heads_call(
        place,
        pieces,
        d_pair,
        d_single,
        attn_gain,
        attn_shift,
        mlp_vectors,
        cross_vectors,
        qkv_weight,
        batch,
    )
    g_qkv, others, feed = together(g_qkv, others, feed)
    g_qkv = add_rows(g_qkv.reshape((batch,) + g_qkv.shape[2:]))
    feed = gather_batch(feed)
    if easy:
        others = [halve(others[0], "by", 0), halve(others[1], "bx", 0)]
        others = jnp.concatenate(others, axis=0)
    others = add_groups(others)
    grad_tokens = last_call(d_pair_all, d_single_all, tokens, d1, attn_gain, qkv_weight)
    g_qkv, others, grad_tokens, feed = together(g_qkv, others, grad_tokens, feed)
    g_qkv = jnp.stack(gather_groups(g_qkv))
    others = gather_batch(others)
    g_qkv = jnp.stack(gather_batch(g_qkv))

    others = jnp.concatenate(others, axis=0).astype(F32)
    kinds = [others[k * own : (k + 1) * own] for k in range(5)]
    g_up = jnp.concatenate([part[0] for part in feed], axis=1).astype(F32)
    deep = FF // peers // batch
    g_down = jnp.stack([part[1] for part in feed]).reshape(batch, D * batch // FF, deep, FF // batch)
    g_down = g_down.transpose(0, 2, 1, 3).reshape(FF // peers, D).astype(F32)
    g_qkv = g_qkv.transpose(0, 2, 1, 3).reshape(own, GROUPS, 5 * PAIR).astype(F32)

    def mine(start, width):
        return g_qkv[:, :, start : start + width].reshape(own, GROUPS * width)

    third = 3 * PAIR
    grad_qkv = jnp.concatenate(
        [
            mine(0, PAIR),
            mine(4 * PAIR, HD),
            mine(PAIR, PAIR),
            mine(third, HD),
            mine(2 * PAIR, PAIR),
            mine(third + HD, HD),
        ],
        axis=1,
    )
    vectors = jnp.sum(g_qkv[:, :, 4 * PAIR + HD : 4 * PAIR + HD + 6], axis=1)
    return (
        output.reshape(seqs, rows, D),
        grad_tokens,
        dnear.reshape(neighbours.shape),
        grad_qkv,
        kinds[0],
        kinds[1],
        jnp.concatenate(kinds[3:], axis=1),
        kinds[2],
        g_up,
        g_down,
        vectors[:, 0],
        vectors[:, 1],
        vectors[:, 4],
        vectors[:, 5],
        vectors[:, 2],
        vectors[:, 3],
    )


def solution(mesh):
    batch, seq = mesh.shape["batch"], mesh.shape["seq"]
    fine = Mesh(
        mesh.devices.reshape(batch // 2, 2, GROUPS, seq // GROUPS), ("by", "bx", "hg", "sq")
    )
    rows = P(BATCH, SEQ, None)
    windows = P(BATCH, SEQ, None, None, None)
    return jax.shard_map(
        shards,
        mesh=fine,
        in_specs=(rows, windows, rows) + (P(),) * 13 + (rows,),
        out_specs=(rows, rows, windows) + (P(SEQ, None),) * 7 + (P(SEQ),) * 6,
        check_vma=False,
    )
```
